32 devices in a mesh: wide: 8 (over z, x), narrow: 4 (over y, core).
Axes of the slice: x: 2, y: 2, z: 4, core: 2. Of those that a mesh axis runs over, the one named last changes fastest.
Arguments:
- tokens: bfloat16 [8192, 768], P(('wide', 'narrow')), may hold values from -6 to 6
- memory: bfloat16 [32768, 768], P(('wide', 'narrow')), may hold values from -6 to 6
- cotangent: bfloat16 [8192, 768], P(('wide', 'narrow')), may hold values from -6 to 6
- target_lengths: int32 [32], P(('wide', 'narrow')), may hold values from 1 to 256, as said below
- memory_lengths: int32 [32], P(('wide', 'narrow')), may hold values from 1 to 1024, as said below
- self_gain: bfloat16 [768], P(('wide', 'narrow')), may hold values from 0.25 to 1.75
- self_query: bfloat16 [768, 768], P(('wide', 'narrow')), may hold values from -0.21875 to 0.21875
- self_key: bfloat16 [768, 768], P(('wide', 'narrow')), may hold values from -0.21875 to 0.21875
- self_value: bfloat16 [768, 768], P(('wide', 'narrow')), may hold values from -0.21875 to 0.21875
- self_out: bfloat16 [768, 768], P(('wide', 'narrow')), may hold values from -0.625 to 0.625
- position_table: bfloat16 [32, 12], replicated, may hold values from -4 to 4
- cross_gain: bfloat16 [768], P(('wide', 'narrow')), may hold values from 0.25 to 1.75
- cross_query: bfloat16 [768, 768], P(('wide', 'narrow')), may hold values from -0.21875 to 0.21875
- cross_key: bfloat16 [768, 768], P(('wide', 'narrow')), may hold values from -0.21875 to 0.21875
- cross_value: bfloat16 [768, 768], P(('wide', 'narrow')), may hold values from -0.21875 to 0.21875
- cross_out: bfloat16 [768, 768], P(('wide', 'narrow')), may hold values from -0.875 to 0.875
- ffn_gain: bfloat16 [768], P(('wide', 'narrow')), may hold values from 0.25 to 1.75
- ffn_in: bfloat16 [768, 3072], P(('wide', 'narrow')), may hold values from -0.21875 to 0.21875
- ffn_out: bfloat16 [3072, 768], P(('wide', 'narrow')), may hold values from -0.15625 to 0.15625
Outputs:
- output: bfloat16 [8192, 768], P(('wide', 'narrow'))
- input_grad: float32 [8192, 768], P(('wide', 'narrow'))
- memory_grad: float32 [32768, 768], P(('wide', 'narrow'))
- self_gain_grad: float32 [768], P(('wide', 'narrow'))
- self_query_grad: float32 [768, 768], P(('wide', 'narrow'))
- self_key_grad: float32 [768, 768], P(('wide', 'narrow'))
- self_value_grad: float32 [768, 768], P(('wide', 'narrow'))
- self_out_grad: float32 [768, 768], P(('wide', 'narrow'))
- position_table_grad: float32 [32, 12], replicated
- cross_gain_grad: float32 [768], P(('wide', 'narrow'))
- cross_query_grad: float32 [768, 768], P(('wide', 'narrow'))
- cross_key_grad: float32 [768, 768], P(('wide', 'narrow'))
- cross_value_grad: float32 [768, 768], P(('wide', 'narrow'))
- cross_out_grad: float32 [768, 768], P(('wide', 'narrow'))
- ffn_gain_grad: float32 [768], P(('wide', 'narrow'))
- ffn_in_grad: float32 [768, 3072], P(('wide', 'narrow'))
- ffn_out_grad: float32 [3072, 768], P(('wide', 'narrow'))
The draws below stay inside these ranges and needn't reach their ends.
Inputs may be any that keep to these rules, and one draw needn't show every extreme that they name: `target_lengths`: some sequence has exactly 256 in every draw. `memory_lengths`: some sequence has exactly 1024 in every draw.
All inputs are finite; a program needn't handle non-finite values.
Results may differ from the reference program's by a relative error of at most 0.02.
Values may be sent and summed in bfloat16 or wider, within the bound.
A program may use at most 192 MiB of HBM per device.

```python
import math
from functools import partial
import jax
import jax.numpy as jnp
from jax import lax

D = 768
H = 12
DH = 64
FF = 3072
NB = 32
MAXDIST = 128
LT = 256
LM = 1024
SEQ_DEV = 1
SEQS = 32
TOKENS = 8192
MEMORY_ROWS = 32768


def draw_target_lengths(key, part):
    drawn = jax.random.randint(jax.random.fold_in(key, 11), (SEQS,), 1, LT + 1, dtype=jnp.int32)
    chosen = jax.random.randint(jax.random.fold_in(key, 12), (), 0, SEQS, dtype=jnp.int32)
    return jnp.where(jnp.arange(SEQS, dtype=jnp.int32) == chosen, LT, drawn)


def draw_memory_lengths(key, part):
    drawn = jax.random.randint(jax.random.fold_in(key, 21), (SEQS,), 1, LM + 1, dtype=jnp.int32)
    chosen = jax.random.randint(jax.random.fold_in(key, 22), (), 0, SEQS, dtype=jnp.int32)
    return jnp.where(jnp.arange(SEQS, dtype=jnp.int32) == chosen, LM, drawn)


def block_levels(own_key, dims, pieces, smallest, top_value):
    level = 1.0
    for dim, blocks in pieces:
        draws = jax.random.uniform(jax.random.fold_in(jax.random.fold_in(own_key, 6), dim), (blocks,), jnp.float32, smallest / len(pieces), top_value / len(pieces))
        level = level * jnp.repeat(jnp.exp(draws), dims[dim] // blocks).reshape((-1,) + (1,) * (len(dims) - 1 - dim))
    return level


def gaussian(rng, dims, spread, most, cuts=(), held_as=jnp.bfloat16):
    level = block_levels(rng, dims, cuts, -0.22, 0.18) if cuts else 1.0
    entries = jax.random.normal(rng, dims, jnp.float32) * spread * level
    return jnp.minimum(jnp.maximum(entries, -most), most).astype(held_as)


def setup_inputs(seed: int = 0) -> dict:
    key_list = jax.random.split(jax.random.key(seed), 20)
    return {
        "tokens": gaussian(key_list[0], (TOKENS, D), 1.0, 6.0, ((0, 32),)),
        "memory": gaussian(key_list[1], (MEMORY_ROWS, D), 1.0, 6.0, ((0, 32),)),
        "cotangent": gaussian(key_list[2], (TOKENS, D), 1.0, 6.0, ((0, 32),)),
        "target_lengths": draw_target_lengths(jax.random.fold_in(key_list[19], 71), 0),
        "memory_lengths": draw_memory_lengths(jax.random.fold_in(key_list[19], 71), 0),
        "self_gain": jnp.clip(1.0 + 0.15 * jax.random.normal(key_list[5], (D,), jnp.float32), 0.25, 1.75).astype(jnp.bfloat16),
        "self_query": gaussian(key_list[6], (D, D), D ** -0.5, 0.21875, ((0, 32),)),
        "self_key": gaussian(key_list[7], (D, D), D ** -0.5, 0.21875, ((0, 32),)),
        "self_value": gaussian(key_list[8], (D, D), D ** -0.5, 0.21875, ((0, 32),)),
        "self_out": gaussian(key_list[9], (D, D), (D // 8) ** -0.5, 0.625, ((0, 32),)),
        "position_table": gaussian(key_list[10], (NB, H), 1.0, 4.0),
        "cross_gain": jnp.clip(1.0 + 0.15 * jax.random.normal(key_list[11], (D,), jnp.float32), 0.25, 1.75).astype(jnp.bfloat16),
        "cross_query": gaussian(key_list[12], (D, D), D ** -0.5, 0.21875, ((0, 32),)),
        "cross_key": gaussian(key_list[13], (D, D), D ** -0.5, 0.21875, ((0, 32),)),
        "cross_value": gaussian(key_list[14], (D, D), D ** -0.5, 0.21875, ((0, 32),)),
        "cross_out": gaussian(key_list[15], (D, D), (D // 16) ** -0.5, 0.875, ((0, 32),)),
        "ffn_gain": jnp.clip(1.0 + 0.15 * jax.random.normal(key_list[16], (D,), jnp.float32), 0.25, 1.75).astype(jnp.bfloat16),
        "ffn_in": gaussian(key_list[17], (D, FF), D ** -0.5, 0.21875, ((0, 32),)),
        "ffn_out": gaussian(key_list[18], (FF, D), (FF // 2) ** -0.5, 0.15625, ((0, 32),)),
    }


EPSILON = 1e-06
NEGATIVE = -1e+30

@jax.custom_vjp
def low(v):
    return lax.optimization_barrier(v.astype(jnp.bfloat16)).astype(jnp.float32)

@jax.custom_vjp
def low_back(v):
    return v

def low_keep(v):
    return (low(v), None)

def low_pass(kept, grad):
    return (grad,)

def back_keep(v):
    return (v, None)

def back_low(kept, grad):
    return (low(grad),)
low.defvjp(low_keep, low_pass)
low_back.defvjp(back_keep, back_low)

def rounded_both(value):
    return low_back(low(value))

def bucket_index(length):
    offsets = jnp.arange(length, dtype=jnp.int32)
    distance = jnp.maximum(offsets[:, None] - offsets[None, :], 0)
    exact_part = NB // 2
    bucket = jnp.minimum(distance, exact_part)
    for step in range(1, NB - exact_part):
        bound = math.ceil(exact_part * (MAXDIST / exact_part) ** (step / (NB - exact_part)))
        bucket = bucket + (distance >= bound).astype(jnp.int32)
    return bucket

def rms_apply(field, gain):
    inverse = lax.rsqrt(lax.optimization_barrier(jnp.mean(field * field, axis=-1, keepdims=True)) + EPSILON)
    return field * inverse * gain

def product(left, right):
    return jnp.dot(left, right, precision=lax.Precision.HIGHEST)

def attention(query, keys, values, extra, visible):
    seq_count = visible.shape[0]
    shaped_query = query.reshape(seq_count, -1, H, DH)
    shaped_keys = keys.reshape(seq_count, -1, H, DH)
    shaped_values = values.reshape(seq_count, -1, H, DH)
    raw = low_back(jnp.einsum('sqhd,skhd->shqk', shaped_query, shaped_keys, precision=lax.Precision.HIGHEST) * DH ** (-0.5))
    scores = jnp.where(visible[:, None], raw + extra, NEGATIVE)
    peak = lax.optimization_barrier(jnp.max(scores, axis=-1, keepdims=True))
    raised = jnp.exp(scores - peak)
    attend = raised / lax.optimization_barrier(jnp.sum(raised, axis=-1, keepdims=True))
    mixed = jnp.einsum('shqk,skhd->sqhd', low(attend), shaped_values, precision=lax.Precision.HIGHEST)
    return rounded_both(mixed.reshape(query.shape[0], H * DH))

def layer_group(weight_list, one_hot, group):
    source, mem, self_visible, memory_visible = group
    self_gain, self_query, self_key, self_value, self_out, position_table, cross_gain, cross_query, cross_key, cross_value, cross_out, ffn_gain, ffn_in, ffn_out = weight_list
    relative = jnp.einsum('ijb,bh->hij', one_hot, position_table, precision=lax.Precision.HIGHEST)
    normed_one = low(rms_apply(source, self_gain))
    query_one = rounded_both(product(normed_one, self_query))
    keys_one = rounded_both(product(normed_one, self_key))
    values_one = rounded_both(product(normed_one, self_value))
    context_one = attention(query_one, keys_one, values_one, relative, self_visible)
    after_self = source + low_back(product(context_one, self_out))
    normed_two = low(rms_apply(after_self, cross_gain))
    query_two = rounded_both(product(normed_two, cross_query))
    keys_two = rounded_both(product(mem, cross_key))
    values_two = rounded_both(product(mem, cross_value))
    context_two = attention(query_two, keys_two, values_two, 0.0, memory_visible)
    after_cross = after_self + low_back(product(context_two, cross_out))
    normed_three = low(rms_apply(after_cross, ffn_gain))
    before = low_back(product(normed_three, ffn_in))
    hidden = low(jax.nn.gelu(before, approximate=True))
    return after_cross + low_back(product(hidden, ffn_out))

def reference(tokens, memory, cotangent, target_lengths, memory_lengths, self_gain, self_query, self_key, self_value, self_out, position_table, cross_gain, cross_query, cross_key, cross_value, cross_out, ffn_gain, ffn_in, ffn_out):
    groups = target_lengths.shape[0] // SEQ_DEV
    bucket = bucket_index(LT)
    one_hot = (bucket[:, :, None] == jnp.arange(NB, dtype=jnp.int32)[None, None, :]).astype(jnp.float32)
    positions = jnp.arange(LT, dtype=jnp.int32)
    live = positions[None, :] < target_lengths[:, None]
    causal = positions[None, :] <= positions[:, None]
    self_visible = causal[None] & live[:, None, :]
    memory_visible = (jnp.arange(LM, dtype=jnp.int32)[None, :] < memory_lengths[:, None])[:, None, :]
    grad_y = jnp.where(live.reshape(-1, 1), cotangent.astype(jnp.float32), 0.0)
    weight_list = tuple((array.astype(jnp.float32) for array in (self_gain, self_query, self_key, self_value, self_out, position_table, cross_gain, cross_query, cross_key, cross_value, cross_out, ffn_gain, ffn_in, ffn_out)))

    def forward(source, mem, weights):
        grouped = (source.reshape(groups, SEQ_DEV * LT, D), mem.reshape(groups, SEQ_DEV * LM, D), self_visible.reshape(groups, SEQ_DEV, LT, LT), memory_visible.reshape(groups, SEQ_DEV, 1, LM))
        result = lax.map(jax.checkpoint(partial(layer_group, weights, one_hot)), grouped)
        return result.reshape(-1, D)
    output, backward = jax.vjp(forward, tokens.astype(jnp.float32), memory.astype(jnp.float32), weight_list)
    input_grad, memory_grad, weight_grads = backward(grad_y)
    g_self_gain, g_self_query, g_self_key, g_self_value, g_self_out, g_table, g_cross_gain, g_cross_query, g_cross_key, g_cross_value, g_cross_out, g_ffn_gain, g_ffn_in, g_ffn_out = weight_grads
    return (output.astype(jnp.bfloat16), input_grad, memory_grad, g_self_gain, g_self_query, g_self_key, g_self_value, g_self_out, g_table, g_cross_gain, g_cross_query, g_cross_key, g_cross_value, g_cross_out, g_ffn_gain, g_ffn_in, g_ffn_out)
```

```python
import math

import jax
import jax.numpy as jnp
from jax import lax
from jax.experimental import pallas as pl
from jax.experimental.pallas import tpu as pltpu
from jax.sharding import PartitionSpec as P

DH = 64
NB = 32
MAXDIST = 128


EPSILON = 1e-06
NEGATIVE = -1e30


def bucket_index(length):
    offsets = jnp.arange(length, dtype=jnp.int32)
    distance = jnp.maximum(offsets[:, None] - offsets[None, :], 0)
    exact_part = NB // 2
    bucket = jnp.minimum(distance, exact_part)
    for step in range(1, NB - exact_part):
        bound = math.ceil(exact_part * (MAXDIST / exact_part) ** (step / (NB - exact_part)))
        bucket = bucket + (distance >= bound).astype(jnp.int32)
    return bucket


def rms_apply(field, gain):
    inverse = lax.rsqrt(jnp.mean(field * field, axis=-1, keepdims=True) + EPSILON)
    return field * inverse * gain


def gelu_smooth(field):
    return jax.nn.gelu(field, approximate=True)


def product(left, right):
    return jnp.dot(left, right, preferred_element_type=jnp.float32)


def outer_sum(left, right):
    return jnp.einsum("rd,re->de", left, right, preferred_element_type=jnp.float32)


def back_project(left, right):
    return jnp.einsum("re,de->rd", left, right, preferred_element_type=jnp.float32)


def pack_rows(arrays, devices):
    return jnp.concatenate([array.reshape(devices, -1) for array in arrays], axis=1)


def unpack_rows(packed_row, arrays, devices):
    results = []
    offset = 0
    for array in arrays:
        shard_shape = (array.shape[0] // devices,) + array.shape[1:]
        count = array.size // devices
        results.append(packed_row[offset : offset + count].reshape(shard_shape))
        offset = offset + count
    return tuple(results)


def head_blocks(array, index, seq_count):
    block = lax.dynamic_slice_in_dim(array, index * 2 * DH, 2 * DH, 1)
    return block.reshape(seq_count, -1, 2, DH)


def flat_block(block):
    return block.reshape(-1, 2 * DH)


def scored(query_block, keys_block, extra, visible, index):
    scores = jnp.einsum(
        "sqhd,skhd->shqk", query_block, keys_block, preferred_element_type=jnp.float32
    ) * DH ** (-0.5)
    if extra is not None:
        scores = scores + lax.dynamic_slice_in_dim(extra, index * 2, 2, 0)[None]
    return jnp.where(visible[:, None], scores, NEGATIVE)


def attend_forward(query, keys, values, extra, visible, seq_count):
    pairs = query.shape[1] // (2 * DH)
    start_context = jnp.zeros(query.shape, jnp.bfloat16)
    start_totals = jnp.zeros((seq_count, 2 * pairs, query.shape[0] // seq_count), jnp.float32)

    def one_pair(index, carry):
        context, log_total = carry
        query_block = head_blocks(query, index, seq_count)
        scores = scored(query_block, head_blocks(keys, index, seq_count), extra, visible, index)
        peak = jnp.max(scores, axis=-1, keepdims=True)
        raised = jnp.exp(scores - peak)
        total = jnp.sum(raised, axis=-1, keepdims=True)
        attend = (raised / total).astype(jnp.bfloat16)
        mixed = jnp.einsum(
            "shqk,skhd->sqhd",
            attend,
            head_blocks(values, index, seq_count),
            preferred_element_type=jnp.float32,
        )
        context = lax.dynamic_update_slice_in_dim(
            context, flat_block(mixed.astype(jnp.bfloat16)), index * 2 * DH, 1
        )
        log_total = lax.dynamic_update_slice_in_dim(
            log_total, (peak + jnp.log(total))[..., 0], index * 2, 1
        )
        return (context, log_total)

    return lax.fori_loop(0, pairs, one_pair, (start_context, start_totals))


def attend_backward(query, keys, values, extra, visible, seq_count, log_total, grad_context):
    pairs = query.shape[1] // (2 * DH)
    scale = DH ** (-0.5)
    extra_shape = extra.shape if extra is not None else (1,)
    start_grads = (
        jnp.zeros(query.shape, jnp.bfloat16),
        jnp.zeros(keys.shape, jnp.bfloat16),
        jnp.zeros(values.shape, jnp.bfloat16),
        jnp.zeros(extra_shape, jnp.float32),
    )

    def one_pair(index, carry):
        grad_query, grad_keys, grad_values, grad_extra = carry
        query_block = head_blocks(query, index, seq_count)
        keys_block = head_blocks(keys, index, seq_count)
        value_block = head_blocks(values, index, seq_count)
        upstream = head_blocks(grad_context, index, seq_count)
        scores = scored(query_block, keys_block, extra, visible, index)
        attend = jnp.exp(scores - lax.dynamic_slice_in_dim(log_total, index * 2, 2, 1)[..., None])
        grad_attend = jnp.einsum(
            "sqhd,skhd->shqk", upstream, value_block, preferred_element_type=jnp.float32
        )
        value_grad = jnp.einsum(
            "shqk,sqhd->skhd",
            attend.astype(jnp.bfloat16),
            upstream,
            preferred_element_type=jnp.float32,
        ).astype(jnp.bfloat16)
        inner = jnp.sum(attend * grad_attend, axis=-1, keepdims=True)
        grad_score = attend * (grad_attend - inner)
        rounded = grad_score.astype(jnp.bfloat16)
        query_grad = (
            jnp.einsum("shqk,skhd->sqhd", rounded, keys_block, preferred_element_type=jnp.float32)
            * scale
        ).astype(jnp.bfloat16)
        keys_grad = (
            jnp.einsum("shqk,sqhd->skhd", rounded, query_block, preferred_element_type=jnp.float32)
            * scale
        ).astype(jnp.bfloat16)
        offset = index * 2 * DH
        grad_query = lax.dynamic_update_slice_in_dim(grad_query, flat_block(query_grad), offset, 1)
        grad_keys = lax.dynamic_update_slice_in_dim(grad_keys, flat_block(keys_grad), offset, 1)
        grad_values = lax.dynamic_update_slice_in_dim(
            grad_values, flat_block(value_grad), offset, 1
        )
        if extra is not None:
            grad_extra = lax.dynamic_update_slice_in_dim(
                grad_extra, jnp.sum(grad_score, axis=0), index * 2, 0
            )
        return (grad_query, grad_keys, grad_values, grad_extra)

    return lax.fori_loop(0, pairs, one_pair, start_grads)


MESH = pl.DeviceIdType.MESH
HALF = 384


def place():
    wide = lax.axis_index("wide")
    narrow = lax.axis_index("narrow")
    return wide // 2, lax.rem(wide, 2), narrow // 2, lax.rem(narrow, 2)


def device(z, x, y, c):
    return (z * 2 + x, y * 2 + c)


def partners(z, x, y, c):
    return (
        device(z ^ 1, x, y, c),
        device(z ^ 2, x, y, c),
        device(z ^ 3, x, y, c),
        device(z, 1 - x, y, c),
        device(z, x, 1 - y, c),
        device(z, x, y, 1 - c),
    )


def enter(everyone):
    barrier = pltpu.get_barrier_semaphore()
    for other in everyone:
        pl.semaphore_signal(barrier, inc=1, device_id=other, device_id_type=MESH)
    pl.semaphore_wait(barrier, len(everyone))


class Post:
    def __init__(self, send, recv):
        self.send, self.recv, self.used, self.started = send, recv, 0, []

    def copy(self, source, target, where):
        made = pltpu.make_async_remote_copy(
            src_ref=source,
            dst_ref=target,
            send_sem=self.send.at[self.used],
            recv_sem=self.recv.at[self.used],
            device_id=where,
            device_id_type=MESH,
        )
        self.used += 1
        made.start()
        self.started.append(made)
        return made

    def finish(self):
        for made in self.started:
            made.wait_send()


def gather_kernel(*refs):
    shards, (mats, down, gains), (send, recv) = refs[:11], refs[11:14], refs[14:]
    z, x, y, c = place()
    everyone = partners(z, x, y, c)
    for index in range(8):
        mats[index, z, x, y, c] = shards[index][...]
    for index in range(4):
        mats[8 + index, z, x, y, c] = shards[8][:, index * 768 : (index + 1) * 768]
    down[z, x, y, c] = shards[9][...]
    gains[z, x, y, c] = shards[10][...]
    enter(everyone)
    post = Post(send, recv)
    across, along, sibling = everyone[3], everyone[4], everyone[5]

    def part(first, last):
        return lambda *where: mats.at[(slice(first, last),) + where]

    def down_part(rows):
        return lambda *where: down.at[where + (pl.ds(rows, 48),)]

    every = slice(None)
    parts = (
        (lambda *where: gains.at[where], False),
        (part(0, 2), False),
        (part(2, 4), True),
        (part(4, 6), False),
        (part(6, 8), True),
        (part(8, 10), False),
        (part(10, 12), True),
        (down_part(0), False),
        (down_part(48), True),
    )
    state = [[] for _ in parts]
    last = []

    def stage(number, index):
        at, flipped = parts[index]
        for made in state[index]:
            made.wait_recv()
        if number == 0:
            state[index] = [post.copy(at(z, x, y, c), at(z, x, y, c), everyone[k]) for k in range(3)]
        if number == 1:
            if flipped:
                state[index] = [post.copy(at(every, x, y, c), at(every, x, y, c), along)]
            else:
                state[index] = [post.copy(at(every, x, y, c), at(every, x, y, c), across)]
            last.append(post.copy(at(every, x, y, c), at(every, x, y, c), sibling))
        if number == 2:
            if flipped:
                state[index] = [post.copy(at(every, x, every, c), at(every, x, every, c), across)]
                last.append(post.copy(at(every, x, 1 - y, c), at(every, x, 1 - y, c), sibling))
            else:
                state[index] = [post.copy(at(every, every, y, c), at(every, every, y, c), along)]
                last.append(post.copy(at(every, 1 - x, y, c), at(every, 1 - x, y, c), sibling))
        if number == 3:
            state[index] = []
            if flipped:
                last.append(post.copy(at(every, 1 - x, every, c), at(every, 1 - x, every, c), sibling))
            else:
                last.append(post.copy(at(every, every, 1 - y, c), at(every, every, 1 - y, c), sibling))

    count = len(parts)
    for step in range(count + 3):
        for number in (3, 2, 1, 0):
            index = step - number
            if 0 <= index < count:
                stage(number, index)
    for made in last:
        made.wait_recv()
    post.finish()


def gather(shards):
    kinds = (
        jax.ShapeDtypeStruct((12, 4, 2, 2, 2, 24, 768), jnp.bfloat16),
        jax.ShapeDtypeStruct((4, 2, 2, 2, 96, 768), jnp.bfloat16),
        jax.ShapeDtypeStruct((4, 2, 2, 2, 8, 768), jnp.bfloat16),
    )
    return pl.pallas_call(
        gather_kernel,
        out_shape=kinds,
        in_specs=[pl.BlockSpec(memory_space=pltpu.VMEM)] * 11,
        out_specs=[pl.BlockSpec(memory_space=pltpu.VMEM)] * 3,
        scratch_shapes=[pltpu.SemaphoreType.DMA((80,)), pltpu.SemaphoreType.DMA((80,))],
        compiler_params=pltpu.CompilerParams(
            collective_id=0, has_side_effects=True, vmem_limit_bytes=60 * 2**20
        ),
    )(*shards)


def scatter_kernel(*refs):
    (grads_in, down_in, extra_in), (grads_out, down_out, extra_out), scratch = refs[:3], refs[3:6], refs[6:]
    pair, first_in, second_in, third_in, done, done_in = scratch[:6]
    dpair, dfirst_in, dsecond_in, dthird_in, ddone, ddone_in = scratch[6:12]
    extra, extra_box, send, recv = scratch[12:]
    z, x, y, c = place()
    everyone = partners(z, x, y, c)
    across, along, sibling = everyone[3], everyone[4], everyone[5]
    enter(everyone)
    post = Post(send, recv)
    every = slice(None)
    mine = pl.ds(pl.multiple_of(c * HALF, 128), HALF)
    other = pl.ds(pl.multiple_of((1 - c) * HALF, 128), HALF)

    class Piece:
        pass

    pieces = []
    for index in range(8):
        piece = Piece()
        if index < 6:
            span = slice(index * 2, index * 2 + 2)
            piece.span = span
            piece.take = lambda ref, *where, span=span: ref.at[(span,) + where]
            piece.source, piece.total, piece.inbox = grads_in, pair, (first_in, second_in, third_in)
            piece.done, piece.done_in, piece.out = done, done_in, grads_out
        else:
            rows = pl.ds((index - 6) * 48, 48)
            piece.span = rows
            piece.take = lambda ref, *where, rows=rows: ref.at[where + (rows,)]
            piece.source, piece.total, piece.inbox = down_in, dpair, (dfirst_in, dsecond_in, dthird_in)
            piece.done, piece.done_in, piece.out = ddone, ddone_in, down_out
        piece.flipped = index % 2 == 1
        piece.is_down = index >= 6
        pieces.append(piece)

    def add(target, terms):
        total = target[...].astype(jnp.float32)
        for term in terms:
            total = total + term[...].astype(jnp.float32)
        target[...] = total.astype(target.dtype)

    def stage(number, piece):
        take, total = piece.take, piece.total
        one, two, three = piece.inbox
        if number == 0:
            source = piece.source
            if piece.is_down:
                out = source.at[(every,) * 4 + (piece.span, other)]
                own = source.at[(every,) * 4 + (piece.span, mine)]
            else:
                out = source.at[(piece.span,) + (every,) * 5 + (other,)]
                own = source.at[(piece.span,) + (every,) * 5 + (mine,)]
            piece.own = own
            where = (every,) * 4
            piece.wait = [post.copy(out, take(total, *where), sibling)]
        if number == 1:
            for made in piece.wait:
                made.wait_recv()
            add(take(total, *(every,) * 4), [piece.own])
            if piece.flipped:
                piece.wait = [post.copy(take(total, every, 1 - x, every, every), take(one, every, every, every), across)]
            else:
                piece.wait = [post.copy(take(total, every, every, 1 - y, every), take(one, every, every, every), along)]
        if number == 2:
            for made in piece.wait:
                made.wait_recv()
            if piece.flipped:
                add(take(total, every, x, every, every), [take(one, every, every, every)])
                piece.wait = [post.copy(take(total, every, x, 1 - y, every), take(two, every, every), along)]
            else:
                add(take(total, every, every, y, every), [take(one, every, every, every)])
                piece.wait = [post.copy(take(total, every, 1 - x, y, every), take(two, every, every), across)]
        if number == 3:
            for made in piece.wait:
                made.wait_recv()
            add(take(total, every, x, y, every), [take(two, every, every)])
            piece.wait = [
                post.copy(take(total, z ^ (k + 1), x, y, every), take(three, k, every), everyone[k])
                for k in range(3)
            ]
        if number == 4:
            for made in piece.wait:
                made.wait_recv()
            result = take(total, z, x, y, every)[...].astype(jnp.float32)
            for k in range(3):
                result = result + take(three, k, every)[...].astype(jnp.float32)
            take(piece.done, every)[...] = result
            piece.wait = [post.copy(take(piece.done, 1 - c), take(piece.done_in), sibling)]
        if number == 5:
            for made in piece.wait:
                made.wait_recv()
            if piece.is_down:
                rows = piece.span
                piece.out[rows, mine] = piece.done[c, rows]
                piece.out[rows, other] = piece.done_in[rows]
            else:
                span = piece.span
                piece.out[span, :, mine] = piece.done[span, c]
                piece.out[span, :, other] = piece.done_in[span]

    extra[...] = extra_in[...]
    hops = ((sibling,), (across,), (along,), everyone[:3])
    waiting = [post.copy(extra, extra_box.at[0], sibling)]
    sent = list(waiting)
    boxes = 1
    count = len(pieces)
    for step in range(count + 5):
        for number in (5, 4, 3, 2, 1, 0):
            index = step - number
            if 0 <= index < count:
                stage(number, pieces[index])
        if step < 4:
            total = extra[...]
            for k, made in enumerate(waiting):
                made.wait_recv()
                total = total + extra_box[boxes - len(waiting) + k]
            for made in waiting:
                made.wait_send()
                post.started = [other_made for other_made in post.started if other_made is not made]
            extra[...] = total
            if step < 3:
                waiting = [
                    post.copy(extra, extra_box.at[boxes + k], where) for k, where in enumerate(hops[step + 1])
                ]
                boxes += len(waiting)
    extra_out[...] = extra[...]
    post.finish()


def scatter(grads, down, extra):
    lead = (12,)
    low, full = jnp.bfloat16, jnp.float32
    return pl.pallas_call(
        scatter_kernel,
        out_shape=(
            jax.ShapeDtypeStruct((12, 24, 768), full),
            jax.ShapeDtypeStruct((96, 768), full),
            jax.ShapeDtypeStruct(extra.shape, full),
        ),
        in_specs=[pl.BlockSpec(memory_space=pltpu.VMEM)] * 3,
        out_specs=[pl.BlockSpec(memory_space=pltpu.VMEM)] * 3,
        scratch_shapes=[
            pltpu.VMEM((12, 4, 2, 2, 2, 24, HALF), low),
            pltpu.VMEM((12, 4, 2, 2, 24, HALF), low),
            pltpu.VMEM((12, 4, 2, 24, HALF), low),
            pltpu.VMEM((12, 3, 2, 24, HALF), low),
            pltpu.VMEM((12, 2, 24, HALF), full),
            pltpu.VMEM((12, 24, HALF), full),
            pltpu.VMEM((4, 2, 2, 2, 96, HALF), low),
            pltpu.VMEM((4, 2, 2, 96, HALF), low),
            pltpu.VMEM((4, 2, 96, HALF), low),
            pltpu.VMEM((3, 2, 96, HALF), low),
            pltpu.VMEM((2, 96, HALF), full),
            pltpu.VMEM((96, HALF), full),
            pltpu.VMEM(extra.shape, full),
            pltpu.VMEM((6,) + extra.shape, full),
            pltpu.SemaphoreType.DMA((80,)),
            pltpu.SemaphoreType.DMA((80,)),
        ],
        compiler_params=pltpu.CompilerParams(
            collective_id=1, has_side_effects=True, vmem_limit_bytes=60 * 2**20
        ),
    )(grads, down, extra)

def plain_body(
    tokens,
    memory,
    cotangent,
    target_lengths,
    memory_lengths,
    self_gain,
    self_query,
    self_key,
    self_value,
    self_out,
    position_table,
    cross_gain,
    cross_query,
    cross_key,
    cross_value,
    cross_out,
    ffn_gain,
    ffn_in,
    ffn_out,
):
    wide_count = lax.axis_size("wide")
    narrow_count = lax.axis_size("narrow")
    devices = wide_count * narrow_count
    seq_count = target_lengths.shape[0]
    target_rows = tokens.shape[0] // seq_count
    memory_rows = memory.shape[0] // seq_count
    positions = jnp.arange(target_rows, dtype=jnp.int32)
    live_rows = positions[None, :] < target_lengths[:, None]
    causal = positions[None, :] <= positions[:, None]
    self_visible = causal[None] & live_rows[:, None, :]
    memory_visible = (jnp.arange(memory_rows, dtype=jnp.int32)[None, :] < memory_lengths[:, None])[
        :, None, :
    ]
    grad_out = jnp.where(live_rows.reshape(-1, 1), cotangent.astype(jnp.float32), 0.0)
    bucket = bucket_index(target_rows)
    one_hot = (bucket[:, :, None] == jnp.arange(NB, dtype=jnp.int32)[None, None, :]).astype(
        jnp.float32
    )
    relative = jnp.einsum(
        "ijb,bh->hij", one_hot, position_table.astype(jnp.float32), precision=lax.Precision.HIGHEST
    )
    gain_one, weight_query, weight_key, weight_value, weight_out = (
        lax.all_gather(self_gain, ("wide", "narrow"), axis=0, tiled=True),
        lax.all_gather(self_query, ("wide", "narrow"), axis=0, tiled=True),
        lax.all_gather(self_key, ("wide", "narrow"), axis=0, tiled=True),
        lax.all_gather(self_value, ("wide", "narrow"), axis=0, tiled=True),
        lax.all_gather(self_out, ("wide", "narrow"), axis=0, tiled=True),
    )
    source = tokens.astype(jnp.float32)
    normed_value, norm_back_one = jax.vjp(rms_apply, source, gain_one.astype(jnp.float32))
    normed_one = normed_value.astype(jnp.bfloat16)
    query_one = product(normed_one, weight_query).astype(jnp.bfloat16)
    keys_one = product(normed_one, weight_key).astype(jnp.bfloat16)
    values_one = product(normed_one, weight_value).astype(jnp.bfloat16)
    context_one, totals_one = attend_forward(
        query_one, keys_one, values_one, relative, self_visible, seq_count
    )
    after_self = source + product(context_one, weight_out)
    gain_two, cross_weight_query, cross_weight_key, cross_weight_value, cross_weight_out = (
        lax.all_gather(cross_gain, ("wide", "narrow"), axis=0, tiled=True),
        lax.all_gather(cross_query, ("wide", "narrow"), axis=0, tiled=True),
        lax.all_gather(cross_key, ("wide", "narrow"), axis=0, tiled=True),
        lax.all_gather(cross_value, ("wide", "narrow"), axis=0, tiled=True),
        lax.all_gather(cross_out, ("wide", "narrow"), axis=0, tiled=True),
    )
    normed_value, norm_back_two = jax.vjp(rms_apply, after_self, gain_two.astype(jnp.float32))
    normed_two = normed_value.astype(jnp.bfloat16)
    query_two = product(normed_two, cross_weight_query).astype(jnp.bfloat16)
    keys_two = product(memory, cross_weight_key).astype(jnp.bfloat16)
    values_two = product(memory, cross_weight_value).astype(jnp.bfloat16)
    context_two, totals_two = attend_forward(
        query_two, keys_two, values_two, None, memory_visible, seq_count
    )
    after_cross = after_self + product(context_two, cross_weight_out)
    gain_three, weight_in, weight_down = (
        lax.all_gather(ffn_gain, ("wide", "narrow"), axis=0, tiled=True),
        lax.all_gather(ffn_in, ("wide", "narrow"), axis=0, tiled=True),
        lax.all_gather(ffn_out, ("wide", "narrow"), axis=0, tiled=True),
    )
    normed_value, norm_back_three = jax.vjp(rms_apply, after_cross, gain_three.astype(jnp.float32))
    normed_three = normed_value.astype(jnp.bfloat16)
    before = product(normed_three, weight_in)
    gelu_value, gelu_back = jax.vjp(gelu_smooth, before)
    hidden = gelu_value.astype(jnp.bfloat16)
    output = (after_cross + product(hidden, weight_down)).astype(jnp.bfloat16)
    back_in, back_down = (
        lax.all_gather(ffn_in, ("wide", "narrow"), axis=0, tiled=True),
        lax.all_gather(ffn_out, ("wide", "narrow"), axis=0, tiled=True),
    )
    grad_low = grad_out.astype(jnp.bfloat16)
    grad_down_weight = outer_sum(hidden, grad_low)
    grad_hidden = back_project(grad_low, back_down)
    grad_before = gelu_back(grad_hidden)[0].astype(jnp.bfloat16)
    grad_in_weight = outer_sum(normed_three, grad_before)
    grad_normed_three = back_project(grad_before, back_in)
    grad_cross_part, grad_gain_three = norm_back_three(grad_normed_three)
    grad_cross = grad_out + grad_cross_part
    ffn_terms = (grad_gain_three, grad_in_weight, grad_down_weight)
    summed_ffn = lax.psum_scatter(
        pack_rows(ffn_terms, devices), ("wide", "narrow"), scatter_dimension=0, tiled=True
    )
    ffn_gain_grad, ffn_in_grad, ffn_out_grad = unpack_rows(summed_ffn[0], ffn_terms, devices)
    back_cross_query, back_cross_key, back_cross_value, back_cross_out = (
        lax.all_gather(cross_query, ("wide", "narrow"), axis=0, tiled=True),
        lax.all_gather(cross_key, ("wide", "narrow"), axis=0, tiled=True),
        lax.all_gather(cross_value, ("wide", "narrow"), axis=0, tiled=True),
        lax.all_gather(cross_out, ("wide", "narrow"), axis=0, tiled=True),
    )
    grad_cross_low = grad_cross.astype(jnp.bfloat16)
    grad_cross_out_weight = outer_sum(context_two, grad_cross_low)
    grad_context_two = back_project(grad_cross_low, back_cross_out).astype(jnp.bfloat16)
    grad_query_two, grad_keys_two, grad_values_two, unused_extra = attend_backward(
        query_two,
        keys_two,
        values_two,
        None,
        memory_visible,
        seq_count,
        totals_two,
        grad_context_two,
    )
    grad_cross_query_weight = outer_sum(normed_two, grad_query_two)
    grad_cross_key_weight = outer_sum(memory, grad_keys_two)
    grad_cross_value_weight = outer_sum(memory, grad_values_two)
    memory_grad = back_project(grad_keys_two, back_cross_key) + back_project(
        grad_values_two, back_cross_value
    )
    grad_self_part, grad_gain_two = norm_back_two(back_project(grad_query_two, back_cross_query))
    grad_self = grad_cross + grad_self_part
    cross_terms = (
        grad_gain_two,
        grad_cross_query_weight,
        grad_cross_key_weight,
        grad_cross_value_weight,
        grad_cross_out_weight,
    )
    summed_cross = lax.psum_scatter(
        pack_rows(cross_terms, devices), ("wide", "narrow"), scatter_dimension=0, tiled=True
    )
    cross_gain_grad, cross_query_grad, cross_key_grad, cross_value_grad, cross_out_grad = (
        unpack_rows(summed_cross[0], cross_terms, devices)
    )
    back_query, back_key, back_value, back_out = (
        lax.all_gather(self_query, ("wide", "narrow"), axis=0, tiled=True),
        lax.all_gather(self_key, ("wide", "narrow"), axis=0, tiled=True),
        lax.all_gather(self_value, ("wide", "narrow"), axis=0, tiled=True),
        lax.all_gather(self_out, ("wide", "narrow"), axis=0, tiled=True),
    )
    grad_self_low = grad_self.astype(jnp.bfloat16)
    grad_out_weight = outer_sum(context_one, grad_self_low)
    grad_context_one = back_project(grad_self_low, back_out).astype(jnp.bfloat16)
    grad_query_one, grad_keys_one, grad_values_one, grad_relative = attend_backward(
        query_one,
        keys_one,
        values_one,
        relative,
        self_visible,
        seq_count,
        totals_one,
        grad_context_one,
    )
    table_term = jnp.einsum("hij,ijb->bh", grad_relative, one_hot, precision=lax.Precision.HIGHEST)
    position_table_grad = lax.psum(table_term, ("wide", "narrow"))
    grad_query_weight = outer_sum(normed_one, grad_query_one)
    grad_key_weight = outer_sum(normed_one, grad_keys_one)
    grad_value_weight = outer_sum(normed_one, grad_values_one)
    grad_normed_one = (
        back_project(grad_query_one, back_query)
        + back_project(grad_keys_one, back_key)
        + back_project(grad_values_one, back_value)
    )
    grad_source_part, grad_gain_one = norm_back_one(grad_normed_one)
    input_grad = grad_self + grad_source_part
    self_terms = (
        grad_gain_one,
        grad_query_weight,
        grad_key_weight,
        grad_value_weight,
        grad_out_weight,
    )
    summed_self = lax.psum_scatter(
        pack_rows(self_terms, devices), ("wide", "narrow"), scatter_dimension=0, tiled=True
    )
    self_gain_grad, self_query_grad, self_key_grad, self_value_grad, self_out_grad = unpack_rows(
        summed_self[0], self_terms, devices
    )
    return (
        output,
        input_grad,
        memory_grad,
        self_gain_grad,
        self_query_grad,
        self_key_grad,
        self_value_grad,
        self_out_grad,
        position_table_grad,
        cross_gain_grad,
        cross_query_grad,
        cross_key_grad,
        cross_value_grad,
        cross_out_grad,
        ffn_gain_grad,
        ffn_in_grad,
        ffn_out_grad,
    )


def body(
    tokens,
    memory,
    cotangent,
    target_lengths,
    memory_lengths,
    self_gain,
    self_query,
    self_key,
    self_value,
    self_out,
    position_table,
    cross_gain,
    cross_query,
    cross_key,
    cross_value,
    cross_out,
    ffn_gain,
    ffn_in,
    ffn_out,
):
    wide_count = lax.axis_size("wide")
    narrow_count = lax.axis_size("narrow")
    seq_count = target_lengths.shape[0]
    target_rows = tokens.shape[0] // seq_count
    memory_rows = memory.shape[0] // seq_count
    positions = jnp.arange(target_rows, dtype=jnp.int32)
    live_rows = positions[None, :] < target_lengths[:, None]
    causal = positions[None, :] <= positions[:, None]
    self_visible = causal[None] & live_rows[:, None, :]
    memory_visible = (jnp.arange(memory_rows, dtype=jnp.int32)[None, :] < memory_lengths[:, None])[
        :, None, :
    ]
    grad_out = jnp.where(live_rows.reshape(-1, 1), cotangent.astype(jnp.float32), 0.0)
    bucket = bucket_index(target_rows)
    one_hot = (bucket[:, :, None] == jnp.arange(NB, dtype=jnp.int32)[None, None, :]).astype(
        jnp.float32
    )
    relative = jnp.einsum(
        "ijb,bh->hij", one_hot, position_table.astype(jnp.float32), precision=lax.Precision.HIGHEST
    )
    rank = lax.axis_index("wide") * narrow_count + lax.axis_index("narrow")
    own_gains = jnp.stack([self_gain, cross_gain, ffn_gain])
    spread = lax.dynamic_update_slice(jnp.zeros((8, 768), jnp.bfloat16), own_gains, (0, rank * 24))
    mats, down, gains = gather(
        (self_query, self_key, self_value, self_out, cross_query, cross_key, cross_value, cross_out, ffn_in, ffn_out, spread)
    )
    gains = jnp.sum(gains.reshape(32, 8, 768).astype(jnp.float32), axis=0)
    gain_one, gain_two, gain_three = gains[0], gains[1], gains[2]
    (weight_query, weight_key, weight_value, weight_out, cross_weight_query, cross_weight_key, cross_weight_value, cross_weight_out) = (
        mats[k].reshape(768, 768) for k in range(8)
    )
    weight_in = [mats[8 + k].reshape(768, 768) for k in range(4)]
    weight_down = down.reshape(3072, 768)
    source = tokens.astype(jnp.float32)
    normed_value, norm_back_one = jax.vjp(rms_apply, source, gain_one.astype(jnp.float32))
    normed_one = normed_value.astype(jnp.bfloat16)
    query_one = product(normed_one, weight_query).astype(jnp.bfloat16)
    keys_one = product(normed_one, weight_key).astype(jnp.bfloat16)
    values_one = product(normed_one, weight_value).astype(jnp.bfloat16)
    context_one, totals_one = attend_forward(
        query_one, keys_one, values_one, relative, self_visible, seq_count
    )
    after_self = source + product(context_one, weight_out)
    normed_value, norm_back_two = jax.vjp(rms_apply, after_self, gain_two.astype(jnp.float32))
    normed_two = normed_value.astype(jnp.bfloat16)
    query_two = product(normed_two, cross_weight_query).astype(jnp.bfloat16)
    keys_two = product(memory, cross_weight_key).astype(jnp.bfloat16)
    values_two = product(memory, cross_weight_value).astype(jnp.bfloat16)
    context_two, totals_two = attend_forward(
        query_two, keys_two, values_two, None, memory_visible, seq_count
    )
    after_cross = after_self + product(context_two, cross_weight_out)
    normed_value, norm_back_three = jax.vjp(rms_apply, after_cross, gain_three.astype(jnp.float32))
    normed_three = normed_value.astype(jnp.bfloat16)
    before = jnp.concatenate([product(normed_three, block) for block in weight_in], axis=1)
    gelu_value, gelu_back = jax.vjp(gelu_smooth, before)
    hidden = gelu_value.astype(jnp.bfloat16)
    output = (after_cross + product(hidden, weight_down)).astype(jnp.bfloat16)
    grad_low = grad_out.astype(jnp.bfloat16)
    grad_down_weight = outer_sum(hidden, grad_low)
    grad_hidden = back_project(grad_low, weight_down)
    grad_before = gelu_back(grad_hidden)[0].astype(jnp.bfloat16)
    grad_in_weight = outer_sum(normed_three, grad_before)
    grad_normed_three = sum(back_project(grad_before[:, 768 * k : 768 * k + 768], weight_in[k]) for k in range(4))
    grad_cross_part, grad_gain_three = norm_back_three(grad_normed_three)
    grad_cross = grad_out + grad_cross_part
    grad_cross_low = grad_cross.astype(jnp.bfloat16)
    grad_cross_out_weight = outer_sum(context_two, grad_cross_low)
    grad_context_two = back_project(grad_cross_low, cross_weight_out).astype(jnp.bfloat16)
    grad_query_two, grad_keys_two, grad_values_two, unused_extra = attend_backward(
        query_two,
        keys_two,
        values_two,
        None,
        memory_visible,
        seq_count,
        totals_two,
        grad_context_two,
    )
    grad_cross_query_weight = outer_sum(normed_two, grad_query_two)
    grad_cross_key_weight = outer_sum(memory, grad_keys_two)
    grad_cross_value_weight = outer_sum(memory, grad_values_two)
    memory_grad = back_project(grad_keys_two, cross_weight_key) + back_project(
        grad_values_two, cross_weight_value
    )
    grad_self_part, grad_gain_two = norm_back_two(back_project(grad_query_two, cross_weight_query))
    grad_self = grad_cross + grad_self_part
    grad_self_low = grad_self.astype(jnp.bfloat16)
    grad_out_weight = outer_sum(context_one, grad_self_low)
    grad_context_one = back_project(grad_self_low, weight_out).astype(jnp.bfloat16)
    grad_query_one, grad_keys_one, grad_values_one, grad_relative = attend_backward(
        query_one,
        keys_one,
        values_one,
        relative,
        self_visible,
        seq_count,
        totals_one,
        grad_context_one,
    )
    table_term = jnp.einsum("hij,ijb->bh", grad_relative, one_hot, precision=lax.Precision.HIGHEST)
    grad_query_weight = outer_sum(normed_one, grad_query_one)
    grad_key_weight = outer_sum(normed_one, grad_keys_one)
    grad_value_weight = outer_sum(normed_one, grad_values_one)
    grad_normed_one = (
        back_project(grad_query_one, weight_query)
        + back_project(grad_keys_one, weight_key)
        + back_project(grad_values_one, weight_value)
    )
    grad_source_part, grad_gain_one = norm_back_one(grad_normed_one)
    input_grad = grad_self + grad_source_part
    mat_grads = jnp.stack(
        [
            term.astype(jnp.bfloat16)
            for term in (
                grad_query_weight,
                grad_key_weight,
                grad_value_weight,
                grad_out_weight,
                grad_cross_query_weight,
                grad_cross_key_weight,
                grad_cross_value_weight,
                grad_cross_out_weight,
                grad_in_weight[:, :768],
                grad_in_weight[:, 768:1536],
                grad_in_weight[:, 1536:2304],
                grad_in_weight[:, 2304:],
            )
        ]
    ).reshape(12, 4, 2, 2, 2, 24, 768)
    down_grads = grad_down_weight.astype(jnp.bfloat16).reshape(4, 2, 2, 2, 96, 768)
    table_rows = jnp.pad(table_term.T, ((0, 4), (0, 768 - NB)))
    extra = jnp.concatenate([jnp.stack([grad_gain_one, grad_gain_two, grad_gain_three]), jnp.zeros((5, 768), jnp.float32), table_rows])
    mat_sums, ffn_out_grad, extra = scatter(mat_grads, down_grads, extra)
    position_table_grad = extra[8:20, :NB].T
    own = lax.dynamic_slice(extra, (0, rank * 24), (8, 24))
    self_gain_grad, cross_gain_grad, ffn_gain_grad = own[0], own[1], own[2]
    (self_query_grad, self_key_grad, self_value_grad, self_out_grad, cross_query_grad, cross_key_grad, cross_value_grad, cross_out_grad) = (
        mat_sums[k] for k in range(8)
    )
    ffn_in_grad = jnp.concatenate([mat_sums[8 + k] for k in range(4)], axis=1)
    return (
        output,
        input_grad,
        memory_grad,
        self_gain_grad,
        self_query_grad,
        self_key_grad,
        self_value_grad,
        self_out_grad,
        position_table_grad,
        cross_gain_grad,
        cross_query_grad,
        cross_key_grad,
        cross_value_grad,
        cross_out_grad,
        ffn_gain_grad,
        ffn_in_grad,
        ffn_out_grad,
    )


def solution(mesh):
    whole = (mesh.shape["wide"], mesh.shape["narrow"]) == (8, 4)
    placed = (
        P(("wide", "narrow"), None),
        P(("wide", "narrow"), None),
        P(("wide", "narrow"), None),
        P(("wide", "narrow")),
        P(("wide", "narrow")),
        P(("wide", "narrow")),
        P(("wide", "narrow"), None),
        P(("wide", "narrow"), None),
        P(("wide", "narrow"), None),
        P(("wide", "narrow"), None),
        P(),
        P(("wide", "narrow")),
        P(("wide", "narrow"), None),
        P(("wide", "narrow"), None),
        P(("wide", "narrow"), None),
        P(("wide", "narrow"), None),
        P(("wide", "narrow")),
        P(("wide", "narrow"), None),
        P(("wide", "narrow"), None),
    )
    return jax.shard_map(
        body if whole else plain_body,
        mesh=mesh,
        in_specs=placed,
        out_specs=(
            P(("wide", "narrow"), None),
            P(("wide", "narrow"), None),
            P(("wide", "narrow"), None),
            P(("wide", "narrow")),
            P(("wide", "narrow"), None),
            P(("wide", "narrow"), None),
            P(("wide", "narrow"), None),
            P(("wide", "narrow"), None),
            P(),
            P(("wide", "narrow")),
            P(("wide", "narrow"), None),
            P(("wide", "narrow"), None),
            P(("wide", "narrow"), None),
            P(("wide", "narrow"), None),
            P(("wide", "narrow")),
            P(("wide", "narrow"), None),
            P(("wide", "narrow"), None),
        ),
        check_vma=False,
    )
```

```python
import math

import jax
import jax.numpy as jnp
from jax import lax
from jax.experimental import pallas as pl
from jax.experimental.pallas import tpu as pltpu
from jax.sharding import PartitionSpec as P

DH = 64
NB = 32
MAXDIST = 128


EPSILON = 1e-06
NEGATIVE = -1e30


def bucket_index(length):
    offsets = jnp.arange(length, dtype=jnp.int32)
    distance = jnp.maximum(offsets[:, None] - offsets[None, :], 0)
    exact_part = NB // 2
    bucket = jnp.minimum(distance, exact_part)
    for step in range(1, NB - exact_part):
        bound = math.ceil(exact_part * (MAXDIST / exact_part) ** (step / (NB - exact_part)))
        bucket = bucket + (distance >= bound).astype(jnp.int32)
    return bucket


def rms_apply(field, gain):
    inverse = lax.rsqrt(jnp.mean(field * field, axis=-1, keepdims=True) + EPSILON)
    return field * inverse * gain


def gelu_smooth(field):
    return jax.nn.gelu(field, approximate=True)


def product(left, right):
    return jnp.dot(left, right, preferred_element_type=jnp.float32)


def outer_sum(left, right):
    return jnp.einsum("rd,re->de", left, right, preferred_element_type=jnp.float32)


def back_project(left, right):
    return jnp.einsum("re,de->rd", left, right, preferred_element_type=jnp.float32)


def pack_rows(arrays, devices):
    return jnp.concatenate([array.reshape(devices, -1) for array in arrays], axis=1)


def unpack_rows(packed_row, arrays, devices):
    results = []
    offset = 0
    for array in arrays:
        shard_shape = (array.shape[0] // devices,) + array.shape[1:]
        count = array.size // devices
        results.append(packed_row[offset : offset + count].reshape(shard_shape))
        offset = offset + count
    return tuple(results)


def head_blocks(array, index, seq_count):
    block = lax.dynamic_slice_in_dim(array, index * 2 * DH, 2 * DH, 1)
    return block.reshape(seq_count, -1, 2, DH)


def flat_block(block):
    return block.reshape(-1, 2 * DH)


def scored(query_block, keys_block, extra, visible, index):
    scores = jnp.einsum(
        "sqhd,skhd->shqk", query_block, keys_block, preferred_element_type=jnp.float32
    ) * DH ** (-0.5)
    if extra is not None:
        scores = scores + lax.dynamic_slice_in_dim(extra, index * 2, 2, 0)[None]
    return jnp.where(visible[:, None], scores, NEGATIVE)


def attend_forward(query, keys, values, extra, visible, seq_count):
    pairs = query.shape[1] // (2 * DH)
    start_context = jnp.zeros(query.shape, jnp.bfloat16)
    start_totals = jnp.zeros((seq_count, 2 * pairs, query.shape[0] // seq_count), jnp.float32)

    def one_pair(index, carry):
        context, log_total = carry
        query_block = head_blocks(query, index, seq_count)
        scores = scored(query_block, head_blocks(keys, index, seq_count), extra, visible, index)
        peak = jnp.max(scores, axis=-1, keepdims=True)
        raised = jnp.exp(scores - peak)
        total = jnp.sum(raised, axis=-1, keepdims=True)
        attend = (raised / total).astype(jnp.bfloat16)
        mixed = jnp.einsum(
            "shqk,skhd->sqhd",
            attend,
            head_blocks(values, index, seq_count),
            preferred_element_type=jnp.float32,
        )
        context = lax.dynamic_update_slice_in_dim(
            context, flat_block(mixed.astype(jnp.bfloat16)), index * 2 * DH, 1
        )
        log_total = lax.dynamic_update_slice_in_dim(
            log_total, (peak + jnp.log(total))[..., 0], index * 2, 1
        )
        return (context, log_total)

    return lax.fori_loop(0, pairs, one_pair, (start_context, start_totals))


def attend_backward(query, keys, values, extra, visible, seq_count, log_total, grad_context):
    pairs = query.shape[1] // (2 * DH)
    scale = DH ** (-0.5)
    extra_shape = extra.shape if extra is not None else (1,)
    start_grads = (
        jnp.zeros(query.shape, jnp.bfloat16),
        jnp.zeros(keys.shape, jnp.bfloat16),
        jnp.zeros(values.shape, jnp.bfloat16),
        jnp.zeros(extra_shape, jnp.float32),
    )

    def one_pair(index, carry):
        grad_query, grad_keys, grad_values, grad_extra = carry
        query_block = head_blocks(query, index, seq_count)
        keys_block = head_blocks(keys, index, seq_count)
        value_block = head_blocks(values, index, seq_count)
        upstream = head_blocks(grad_context, index, seq_count)
        scores = scored(query_block, keys_block, extra, visible, index)
        attend = jnp.exp(scores - lax.dynamic_slice_in_dim(log_total, index * 2, 2, 1)[..., None])
        grad_attend = jnp.einsum(
            "sqhd,skhd->shqk", upstream, value_block, preferred_element_type=jnp.float32
        )
        value_grad = jnp.einsum(
            "shqk,sqhd->skhd",
            attend.astype(jnp.bfloat16),
            upstream,
            preferred_element_type=jnp.float32,
        ).astype(jnp.bfloat16)
        inner = jnp.sum(attend * grad_attend, axis=-1, keepdims=True)
        grad_score = attend * (grad_attend - inner)
        rounded = grad_score.astype(jnp.bfloat16)
        query_grad = (
            jnp.einsum("shqk,skhd->sqhd", rounded, keys_block, preferred_element_type=jnp.float32)
            * scale
        ).astype(jnp.bfloat16)
        keys_grad = (
            jnp.einsum("shqk,sqhd->skhd", rounded, query_block, preferred_element_type=jnp.float32)
            * scale
        ).astype(jnp.bfloat16)
        offset = index * 2 * DH
        grad_query = lax.dynamic_update_slice_in_dim(grad_query, flat_block(query_grad), offset, 1)
        grad_keys = lax.dynamic_update_slice_in_dim(grad_keys, flat_block(keys_grad), offset, 1)
        grad_values = lax.dynamic_update_slice_in_dim(
            grad_values, flat_block(value_grad), offset, 1
        )
        if extra is not None:
            grad_extra = lax.dynamic_update_slice_in_dim(
                grad_extra, jnp.sum(grad_score, axis=0), index * 2, 0
            )
        return (grad_query, grad_keys, grad_values, grad_extra)

    return lax.fori_loop(0, pairs, one_pair, start_grads)


MESH = pl.DeviceIdType.MESH
HALF = 384
ROWS = 256
LOW, FULL = jnp.bfloat16, jnp.float32
EVERY = slice(None)


def place():
    wide = lax.axis_index("wide")
    narrow = lax.axis_index("narrow")
    return wide // 2, lax.rem(wide, 2), narrow // 2, lax.rem(narrow, 2)


def device(z, x, y, c):
    return (z * 2 + x, y * 2 + c)


def partners(z, x, y, c):
    return (
        device(z ^ 1, x, y, c),
        device(z ^ 2, x, y, c),
        device(z ^ 3, x, y, c),
        device(z, 1 - x, y, c),
        device(z, x, 1 - y, c),
        device(z, x, y, 1 - c),
    )


def enter(everyone):
    barrier = pltpu.get_barrier_semaphore()
    for other in everyone:
        pl.semaphore_signal(barrier, inc=1, device_id=other, device_id_type=MESH)
    pl.semaphore_wait(barrier, len(everyone))


class Post:
    def __init__(self, send, recv, near):
        self.send, self.recv, self.near = send, recv, near
        self.used, self.used_near, self.started, self.open = 0, 0, [], []

    def copy(self, source, target, where):
        made = pltpu.make_async_remote_copy(
            src_ref=source,
            dst_ref=target,
            send_sem=self.send.at[self.used],
            recv_sem=self.recv.at[self.used],
            device_id=where,
            device_id_type=MESH,
        )
        self.used += 1
        made.start()
        self.started.append(made)
        return made

    def local(self, source, target, keep=False):
        made = pltpu.make_async_copy(source, target, self.near.at[self.used_near])
        self.used_near += 1
        made.start()
        if not keep:
            self.open.append(made)
        return made

    def finish(self):
        for made in self.started:
            made.wait_send()
        for made in self.open:
            made.wait()


def arrived(copies):
    for made in copies:
        made.wait_recv()


def dot(left, right):
    return jnp.dot(left, right, preferred_element_type=FULL)


def dot_last(left, right):
    return lax.dot_general(left, right, (((1,), (1,)), ((), ())), preferred_element_type=FULL)


def dot_first(left, right):
    return lax.dot_general(left, right, (((0,), (0,)), ((), ())), preferred_element_type=FULL)


def square(ref, index):
    return ref[index].reshape(768, 768)


def bucket_rows():
    distance = lax.broadcasted_iota(jnp.int32, (NB, ROWS), 1)
    row = lax.broadcasted_iota(jnp.int32, (NB, ROWS), 0)
    exact_part = NB // 2
    bucket = jnp.minimum(distance, exact_part)
    for step in range(1, NB - exact_part):
        bound = math.ceil(exact_part * (MAXDIST / exact_part) ** (step / (NB - exact_part)))
        bucket = bucket + (distance >= bound).astype(jnp.int32)
    return (bucket == row).astype(LOW)


def self_mask(length):
    key = lax.broadcasted_iota(jnp.int32, (ROWS, ROWS), 0)
    query = lax.broadcasted_iota(jnp.int32, (ROWS, ROWS), 1)
    return jnp.where((key <= query) & (key < length), 0.0, NEGATIVE)


def memory_mask(length, rows):
    key = lax.broadcasted_iota(jnp.int32, (rows, 1), 0)
    return jnp.where(key < length, 0.0, NEGATIVE)


def slanted(row):
    return pltpu.roll(jnp.broadcast_to(row, (ROWS, ROWS)), 0, 1, stride=1, stride_axis=0)


def one_head(block, head):
    lane = lax.broadcasted_iota(jnp.int32, block.shape, 1)
    return jnp.where((lane < DH) if head == 0 else (lane >= DH), block, jnp.zeros_like(block))


def inverse_rms(field):
    return lax.rsqrt(jnp.mean(field * field, axis=-1, keepdims=True) + EPSILON)


def forward_schedule():
    pairs = [("gains", 0, 1), (2, 3), (4, 7), (8, 9), (10, 11), ("down0", "down1")]
    early, ahead = (5, 6), 3
    events = [(unit, 0) for unit in pairs[0]] + [(unit, 0) for unit in early]
    for pair in pairs[1:ahead]:
        events += [(unit, 0) for unit in pair]
    count = len(pairs)
    for step in range(count + 4):
        for stage in (1, 0, None, 2, 3, 4):
            if stage is None:
                if step == 0:
                    events += [(unit, 1) for unit in early]
                if step == 2:
                    events += [(unit, 2) for unit in early]
                if step == 4:
                    events += [(unit, 3) for unit in early]
                if step == 5:
                    events += [(unit, 4) for unit in early]
                continue
            index = step + ahead if stage == 0 else step - stage + 1
            if 0 <= index < count:
                events += [(unit, stage) for unit in pairs[index]]
    return events


ORDERS = {5: "xyz", 6: "yxz", "gains": "zxy", "down0": "zxy", "down1": "zyx", 7: "zyx"}
for _unit in (0, 2, 4, 8, 10):
    ORDERS[_unit] = "zxy"
for _unit in (1, 3, 9, 11):
    ORDERS[_unit] = "zyx"


class Gather:
    def __init__(self, post, shards, mats, down, gains, loaded, spot, everyone):
        self.post, self.shards, self.loaded = post, shards, loaded
        self.mats, self.down, self.gains = mats, down, gains
        self.spot, self.everyone = spot, everyone
        self.events = forward_schedule()
        self.waits, self.near, self.copies, self.ready = {}, {}, {}, set()
        self.own = []

    def at(self, unit, *where):
        if unit == "gains":
            return self.gains.at[where]
        if unit == "down0":
            return self.down.at[where + (pl.ds(0, 48),)]
        if unit == "down1":
            return self.down.at[where + (pl.ds(48, 48),)]
        return self.mats.at[(unit,) + where]

    def shard(self, unit):
        if unit == "gains":
            return self.shards[10]
        if unit == "down0":
            return self.shards[9].at[pl.ds(0, 48)]
        if unit == "down1":
            return self.shards[9].at[pl.ds(48, 48)]
        if unit >= 8:
            return self.shards[8].at[:, pl.ds((unit - 8) * 768, 768)]
        return self.shards[unit]

    def keep_own(self):
        for unit in ORDERS:
            self.own.append(self.post.local(self.shard(unit), self.at(unit, *self.spot), keep=True))

    def forward(self, unit, where, targets):
        return [self.post.copy(self.at(unit, *where), self.at(unit, *where), target) for target in targets]

    def run(self, unit, stage):
        z, x, y, c = self.spot
        across, along, sibling = self.everyone[3:]
        order = ORDERS[unit]
        if stage == 0:
            targets = {"z": self.everyone[:3], "x": (across,), "y": (along,)}[order[0]]
            self.near[unit] = []
            self.waits[unit] = [
                self.post.copy(self.shard(unit), self.at(unit, *self.spot), target) for target in targets
            ]
            return
        if self.own:
            for made in self.own:
                made.wait()
            self.own = []
        if stage == 4:
            arrived(self.near[unit])
            if unit == "gains" or isinstance(unit, int):
                if unit != "gains":
                    self.copies[unit] = self.post.local(self.mats.at[unit], self.loaded.at[unit], keep=True)
            self.ready.add(unit)
            return
        arrived(self.waits[unit])
        steps = {
            "zxy": (
                ((EVERY, x, y, c), (across,), (EVERY, x, y, c)),
                ((EVERY, EVERY, y, c), (along,), (EVERY, 1 - x, y, c)),
                (None, (), (EVERY, EVERY, 1 - y, c)),
            ),
            "zyx": (
                ((EVERY, x, y, c), (along,), (EVERY, x, y, c)),
                ((EVERY, x, EVERY, c), (across,), (EVERY, x, 1 - y, c)),
                (None, (), (EVERY, 1 - x, EVERY, c)),
            ),
            "xyz": (
                ((z, EVERY, y, c), (along,), None),
                ((z, EVERY, EVERY, c), self.everyone[:3], (z, EVERY, EVERY, c)),
                (None, (), "others"),
            ),
            "yxz": (
                ((z, x, EVERY, c), (across,), None),
                ((z, EVERY, EVERY, c), self.everyone[:3], (z, EVERY, EVERY, c)),
                (None, (), "others"),
            ),
        }
        where, targets, near = steps[order][stage - 1]
        self.waits[unit] = self.forward(unit, where, targets) if targets else []
        if near == "others":
            for k in range(3):
                self.near[unit] += self.forward(unit, (z ^ (k + 1), EVERY, EVERY, c), (sibling,))
        elif near is not None:
            self.near[unit] += self.forward(unit, near, (sibling,))

    def pump(self, count):
        for _ in range(count):
            if self.events:
                self.run(*self.events.pop(0))

    def require(self, *units):
        for unit in units:
            while unit not in self.ready:
                self.pump(1)
            if unit in self.copies:
                self.copies.pop(unit).wait()


def forward_kernel(*refs):
    shards, (tokens, memory, table, lengths, memory_lengths) = refs[:11], refs[11:16]
    mats, down, gain_rows = refs[16:19]
    (turned, memory_turned, hidden_turned, small, keys_out, values_out, self_out, cross_out, hidden_out, slope_out) = refs[19:29]
    self_log, cross_log = refs[29:31]
    gains, loaded, keep, keys, values, stage, memory_stage, hidden, slope, hidden_stage, after_self, after_cross, near, send, recv = refs[31:]
    spot = place()
    everyone = partners(*spot)
    sibling = everyone[5]
    post = Post(send, recv, near)
    comm = Gather(post, shards, mats, down, gains, loaded, spot, everyone)
    comm.keep_own()
    enter(everyone)
    comm.pump(9)
    from_sibling = []

    def turn(block, staged, target, lanes=ROWS):
        staged[...] = block.T
        post.local(staged, target.at[:, pl.ds(0, lanes)])
        from_sibling.append(post.copy(staged, target.at[:, pl.ds(lanes, lanes)], sibling))

    for block in range(4):
        turn(memory[block * ROWS : (block + 1) * ROWS], memory_stage.at[block], memory_turned.at[block])
        comm.pump(1)
    source = tokens[...].astype(FULL)
    inverse = inverse_rms(source)
    one_hot = bucket_rows()
    bias = dot(table[...], one_hot)
    visible = self_mask(lengths[0])
    comm.require("gains")
    gain_rows[...] = jnp.sum(gains[...].astype(FULL).reshape(32, 8, 768), axis=0)
    normed = (source * inverse * gain_rows[0:1]).astype(LOW)
    turn(normed, stage.at[0], turned.at[0])

    def project(unit, slot, block):
        comm.require(unit)
        keep[slot] = dot(block, square(loaded, unit)).astype(LOW)
        post.local(keep.at[slot], small.at[slot])

    project(0, 0, normed)
    project(1, 1, normed)
    project(2, 2, normed)

    def attend(pair, head, query, key_block, value_block, extra, log_ref):
        scores = dot_last(key_block, one_head(query, head)) + extra
        peak = jnp.max(scores, axis=0, keepdims=True)
        raised = jnp.exp(scores - peak)
        total = jnp.sum(raised, axis=0, keepdims=True)
        mixed = dot_first(value_block, raised.astype(LOW)) / total
        log_ref[pair * 2 + head : pair * 2 + head + 1] = peak + jnp.log(total)
        return mixed[head * DH : head * DH + DH]

    for pair in range(6):
        span = slice(pair * 128, pair * 128 + 128)
        query = keep[0, :, span] * 0.125
        mixed = [
            attend(
                pair,
                head,
                query,
                keep[1, :, span],
                keep[2, :, span],
                slanted(bias[pair * 2 + head : pair * 2 + head + 1]) + visible,
                self_log,
            )
            for head in range(2)
        ]
        keep[3, :, span] = jnp.concatenate(mixed, axis=0).T.astype(LOW)
        comm.pump(1)
    post.local(keep.at[3], small.at[3])
    context = keep[3]
    turn(context, stage.at[1], turned.at[1])
    comm.require(3)
    after_self[...] = source + dot(context, square(loaded, 3))
    post.local(after_self, self_out)
    normed = (after_self[...] * inverse_rms(after_self[...]) * gain_rows[1:2]).astype(LOW)
    turn(normed, stage.at[2], turned.at[2])
    project(4, 4, normed)
    for unit, held, out in ((5, keys, keys_out), (6, values, values_out)):
        comm.require(unit)
        for block in range(4):
            rows = slice(block * ROWS, block * ROWS + ROWS)
            held[rows] = dot(memory[rows], square(loaded, unit)).astype(LOW)
            comm.pump(1)
        post.local(held, out)
    shown = memory_mask(memory_lengths[0], 1024)
    for pair in range(6):
        span = slice(pair * 128, pair * 128 + 128)
        query = keep[4, :, span] * 0.125
        mixed = [
            attend(pair, head, query, keys[:, span], values[:, span], shown, cross_log) for head in range(2)
        ]
        keep[5, :, span] = jnp.concatenate(mixed, axis=0).T.astype(LOW)
        comm.pump(1)
    post.local(keep.at[5], small.at[5])
    context = keep[5]
    turn(context, stage.at[3], turned.at[3])
    comm.require(7)
    after_cross[...] = after_self[...] + dot(context, square(loaded, 7))
    post.local(after_cross, cross_out)
    normed = (after_cross[...] * inverse_rms(after_cross[...]) * gain_rows[2:3]).astype(LOW)
    turn(normed, stage.at[4], turned.at[4])
    root = math.sqrt(2.0 / math.pi)
    for block in range(4):
        comm.require(8 + block)
        before = dot(normed, square(loaded, 8 + block))
        squared = before * before
        bent = jnp.tanh(root * before * (1.0 + 0.044715 * squared))
        lifted = 0.5 * (1.0 + bent)
        value = (before * lifted).astype(LOW)
        hidden[block] = value
        slope[block] = (
            lifted + 0.5 * root * before * (1.0 - bent * bent) * (1.0 + 3 * 0.044715 * squared)
        ).astype(LOW)
        post.local(hidden.at[block], hidden_out.at[block])
        post.local(slope.at[block], slope_out.at[block])
        turn(value, hidden_stage.at[block], hidden_turned.at[block])
    while comm.events:
        comm.pump(1)
    for unit in list(comm.copies):
        comm.copies.pop(unit).wait()
    arrived(from_sibling)
    post.finish()


def forward_call(shards, tokens, memory, table, lengths, memory_lengths):
    kind = jax.ShapeDtypeStruct
    anywhere, vmem = pl.BlockSpec(memory_space=pl.ANY), pl.BlockSpec(memory_space=pltpu.VMEM)
    smem = pl.BlockSpec(memory_space=pltpu.SMEM)
    outs = (
        (kind((12, 4, 2, 2, 2, 24, 768), LOW), anywhere),
        (kind((4, 2, 2, 2, 96, 768), LOW), anywhere),
        (kind((8, 768), FULL), vmem),
        (kind((5, 768, 512), LOW), anywhere),
        (kind((4, 768, 512), LOW), anywhere),
        (kind((4, 768, 512), LOW), anywhere),
        (kind((6, 256, 768), LOW), anywhere),
        (kind((1024, 768), LOW), anywhere),
        (kind((1024, 768), LOW), anywhere),
        (kind((256, 768), FULL), anywhere),
        (kind((256, 768), FULL), anywhere),
        (kind((4, 256, 768), LOW), anywhere),
        (kind((4, 256, 768), LOW), anywhere),
        (kind((16, 256), FULL), vmem),
        (kind((16, 256), FULL), vmem),
    )
    return pl.pallas_call(
        forward_kernel,
        out_shape=tuple(out[0] for out in outs),
        in_specs=[anywhere] * 11 + [vmem] * 3 + [smem] * 2,
        out_specs=tuple(out[1] for out in outs),
        scratch_shapes=[
            pltpu.VMEM((4, 2, 2, 2, 8, 768), LOW),
            pltpu.VMEM((12, 4, 2, 2, 2, 24, 768), LOW),
            pltpu.VMEM((6, 256, 768), LOW),
            pltpu.VMEM((1024, 768), LOW),
            pltpu.VMEM((1024, 768), LOW),
            pltpu.VMEM((5, 768, 256), LOW),
            pltpu.VMEM((4, 768, 256), LOW),
            pltpu.VMEM((4, 256, 768), LOW),
            pltpu.VMEM((4, 256, 768), LOW),
            pltpu.VMEM((4, 768, 256), LOW),
            pltpu.VMEM((256, 768), FULL),
            pltpu.VMEM((256, 768), FULL),
            pltpu.SemaphoreType.DMA((80,)),
            pltpu.SemaphoreType.DMA((150,)),
            pltpu.SemaphoreType.DMA((150,)),
        ],
        compiler_params=pltpu.CompilerParams(
            collective_id=0, has_side_effects=True, vmem_limit_bytes=60 * 2**20
        ),
    )(*shards, tokens, memory, table, lengths, memory_lengths)


def scatter_kernel(*refs):
    (grads_in, down_in, extra_in), (grads_out, down_out, extra_out), scratch = refs[:3], refs[3:6], refs[6:]
    pair, first_in, second_in, third_in, done, done_in = scratch[:6]
    dpair, dfirst_in, dsecond_in, dthird_in, ddone, ddone_in = scratch[6:12]
    extra, extra_box, send, recv = scratch[12:]
    z, x, y, c = place()
    everyone = partners(z, x, y, c)
    across, along, sibling = everyone[3], everyone[4], everyone[5]
    enter(everyone)
    post = Post(send, recv, None)
    every = slice(None)
    mine = pl.ds(pl.multiple_of(c * HALF, 128), HALF)
    other = pl.ds(pl.multiple_of((1 - c) * HALF, 128), HALF)

    class Piece:
        pass

    pieces = []
    for index in range(8):
        piece = Piece()
        if index < 6:
            span = slice(index * 2, index * 2 + 2)
            piece.span = span
            piece.take = lambda ref, *where, span=span: ref.at[(span,) + where]
            piece.source, piece.total, piece.inbox = grads_in, pair, (first_in, second_in, third_in)
            piece.done, piece.done_in, piece.out = done, done_in, grads_out
        else:
            rows = pl.ds((index - 6) * 48, 48)
            piece.span = rows
            piece.take = lambda ref, *where, rows=rows: ref.at[where + (rows,)]
            piece.source, piece.total, piece.inbox = down_in, dpair, (dfirst_in, dsecond_in, dthird_in)
            piece.done, piece.done_in, piece.out = ddone, ddone_in, down_out
        piece.flipped = index % 2 == 1
        piece.is_down = index >= 6
        pieces.append(piece)

    def add(target, terms):
        total = target[...].astype(jnp.float32)
        for term in terms:
            total = total + term[...].astype(jnp.float32)
        target[...] = total.astype(target.dtype)

    def stage(number, piece):
        take, total = piece.take, piece.total
        one, two, three = piece.inbox
        if number == 0:
            source = piece.source
            if piece.is_down:
                out = source.at[(every,) * 4 + (piece.span, other)]
                own = source.at[(every,) * 4 + (piece.span, mine)]
            else:
                out = source.at[(piece.span,) + (every,) * 5 + (other,)]
                own = source.at[(piece.span,) + (every,) * 5 + (mine,)]
            piece.own = own
            where = (every,) * 4
            piece.wait = [post.copy(out, take(total, *where), sibling)]
        if number == 1:
            for made in piece.wait:
                made.wait_recv()
            add(take(total, *(every,) * 4), [piece.own])
            if piece.flipped:
                piece.wait = [post.copy(take(total, every, 1 - x, every, every), take(one, every, every, every), across)]
            else:
                piece.wait = [post.copy(take(total, every, every, 1 - y, every), take(one, every, every, every), along)]
        if number == 2:
            for made in piece.wait:
                made.wait_recv()
            if piece.flipped:
                add(take(total, every, x, every, every), [take(one, every, every, every)])
                piece.wait = [post.copy(take(total, every, x, 1 - y, every), take(two, every, every), along)]
            else:
                add(take(total, every, every, y, every), [take(one, every, every, every)])
                piece.wait = [post.copy(take(total, every, 1 - x, y, every), take(two, every, every), across)]
        if number == 3:
            for made in piece.wait:
                made.wait_recv()
            add(take(total, every, x, y, every), [take(two, every, every)])
            piece.wait = [
                post.copy(take(total, z ^ (k + 1), x, y, every), take(three, k, every), everyone[k])
                for k in range(3)
            ]
        if number == 4:
            for made in piece.wait:
                made.wait_recv()
            result = take(total, z, x, y, every)[...].astype(jnp.float32)
            for k in range(3):
                result = result + take(three, k, every)[...].astype(jnp.float32)
            take(piece.done, every)[...] = result
            piece.wait = [post.copy(take(piece.done, 1 - c), take(piece.done_in), sibling)]
        if number == 5:
            for made in piece.wait:
                made.wait_recv()
            if piece.is_down:
                rows = piece.span
                piece.out[rows, mine] = piece.done[c, rows]
                piece.out[rows, other] = piece.done_in[rows]
            else:
                span = piece.span
                piece.out[span, :, mine] = piece.done[span, c]
                piece.out[span, :, other] = piece.done_in[span]

    extra[...] = extra_in[...]
    hops = ((sibling,), (across,), (along,), everyone[:3])
    waiting = [post.copy(extra, extra_box.at[0], sibling)]
    sent = list(waiting)
    boxes = 1
    count = len(pieces)
    for step in range(count + 5):
        for number in (5, 4, 3, 2, 1, 0):
            index = step - number
            if 0 <= index < count:
                stage(number, pieces[index])
        if step < 4:
            total = extra[...]
            for k, made in enumerate(waiting):
                made.wait_recv()
                total = total + extra_box[boxes - len(waiting) + k]
            for made in waiting:
                made.wait_send()
                post.started = [other_made for other_made in post.started if other_made is not made]
            extra[...] = total
            if step < 3:
                waiting = [
                    post.copy(extra, extra_box.at[boxes + k], where) for k, where in enumerate(hops[step + 1])
                ]
                boxes += len(waiting)
    extra_out[...] = extra[...]
    post.finish()


def scatter(grads, down, extra):
    lead = (12,)
    low, full = jnp.bfloat16, jnp.float32
    return pl.pallas_call(
        scatter_kernel,
        out_shape=(
            jax.ShapeDtypeStruct((12, 24, 768), full),
            jax.ShapeDtypeStruct((96, 768), full),
            jax.ShapeDtypeStruct(extra.shape, full),
        ),
        in_specs=[pl.BlockSpec(memory_space=pltpu.VMEM)] * 3,
        out_specs=[pl.BlockSpec(memory_space=pltpu.VMEM)] * 3,
        scratch_shapes=[
            pltpu.VMEM((12, 4, 2, 2, 2, 24, HALF), low),
            pltpu.VMEM((12, 4, 2, 2, 24, HALF), low),
            pltpu.VMEM((12, 4, 2, 24, HALF), low),
            pltpu.VMEM((12, 3, 2, 24, HALF), low),
            pltpu.VMEM((12, 2, 24, HALF), full),
            pltpu.VMEM((12, 24, HALF), full),
            pltpu.VMEM((4, 2, 2, 2, 96, HALF), low),
            pltpu.VMEM((4, 2, 2, 96, HALF), low),
            pltpu.VMEM((4, 2, 96, HALF), low),
            pltpu.VMEM((3, 2, 96, HALF), low),
            pltpu.VMEM((2, 96, HALF), full),
            pltpu.VMEM((96, HALF), full),
            pltpu.VMEM(extra.shape, full),
            pltpu.VMEM((6,) + extra.shape, full),
            pltpu.SemaphoreType.DMA((80,)),
            pltpu.SemaphoreType.DMA((80,)),
        ],
        compiler_params=pltpu.CompilerParams(
            collective_id=1, has_side_effects=True, vmem_limit_bytes=60 * 2**20
        ),
    )(grads, down, extra)

def plain_body(
    tokens,
    memory,
    cotangent,
    target_lengths,
    memory_lengths,
    self_gain,
    self_query,
    self_key,
    self_value,
    self_out,
    position_table,
    cross_gain,
    cross_query,
    cross_key,
    cross_value,
    cross_out,
    ffn_gain,
    ffn_in,
    ffn_out,
):
    wide_count = lax.axis_size("wide")
    narrow_count = lax.axis_size("narrow")
    devices = wide_count * narrow_count
    seq_count = target_lengths.shape[0]
    target_rows = tokens.shape[0] // seq_count
    memory_rows = memory.shape[0] // seq_count
    positions = jnp.arange(target_rows, dtype=jnp.int32)
    live_rows = positions[None, :] < target_lengths[:, None]
    causal = positions[None, :] <= positions[:, None]
    self_visible = causal[None] & live_rows[:, None, :]
    memory_visible = (jnp.arange(memory_rows, dtype=jnp.int32)[None, :] < memory_lengths[:, None])[
        :, None, :
    ]
    grad_out = jnp.where(live_rows.reshape(-1, 1), cotangent.astype(jnp.float32), 0.0)
    bucket = bucket_index(target_rows)
    one_hot = (bucket[:, :, None] == jnp.arange(NB, dtype=jnp.int32)[None, None, :]).astype(
        jnp.float32
    )
    relative = jnp.einsum(
        "ijb,bh->hij", one_hot, position_table.astype(jnp.float32), precision=lax.Precision.HIGHEST
    )
    gain_one, weight_query, weight_key, weight_value, weight_out = (
        lax.all_gather(self_gain, ("wide", "narrow"), axis=0, tiled=True),
        lax.all_gather(self_query, ("wide", "narrow"), axis=0, tiled=True),
        lax.all_gather(self_key, ("wide", "narrow"), axis=0, tiled=True),
        lax.all_gather(self_value, ("wide", "narrow"), axis=0, tiled=True),
        lax.all_gather(self_out, ("wide", "narrow"), axis=0, tiled=True),
    )
    source = tokens.astype(jnp.float32)
    normed_value, norm_back_one = jax.vjp(rms_apply, source, gain_one.astype(jnp.float32))
    normed_one = normed_value.astype(jnp.bfloat16)
    query_one = product(normed_one, weight_query).astype(jnp.bfloat16)
    keys_one = product(normed_one, weight_key).astype(jnp.bfloat16)
    values_one = product(normed_one, weight_value).astype(jnp.bfloat16)
    context_one, totals_one = attend_forward(
        query_one, keys_one, values_one, relative, self_visible, seq_count
    )
    after_self = source + product(context_one, weight_out)
    gain_two, cross_weight_query, cross_weight_key, cross_weight_value, cross_weight_out = (
        lax.all_gather(cross_gain, ("wide", "narrow"), axis=0, tiled=True),
        lax.all_gather(cross_query, ("wide", "narrow"), axis=0, tiled=True),
        lax.all_gather(cross_key, ("wide", "narrow"), axis=0, tiled=True),
        lax.all_gather(cross_value, ("wide", "narrow"), axis=0, tiled=True),
        lax.all_gather(cross_out, ("wide", "narrow"), axis=0, tiled=True),
    )
    normed_value, norm_back_two = jax.vjp(rms_apply, after_self, gain_two.astype(jnp.float32))
    normed_two = normed_value.astype(jnp.bfloat16)
    query_two = product(normed_two, cross_weight_query).astype(jnp.bfloat16)
    keys_two = product(memory, cross_weight_key).astype(jnp.bfloat16)
    values_two = product(memory, cross_weight_value).astype(jnp.bfloat16)
    context_two, totals_two = attend_forward(
        query_two, keys_two, values_two, None, memory_visible, seq_count
    )
    after_cross = after_self + product(context_two, cross_weight_out)
    gain_three, weight_in, weight_down = (
        lax.all_gather(ffn_gain, ("wide", "narrow"), axis=0, tiled=True),
        lax.all_gather(ffn_in, ("wide", "narrow"), axis=0, tiled=True),
        lax.all_gather(ffn_out, ("wide", "narrow"), axis=0, tiled=True),
    )
    normed_value, norm_back_three = jax.vjp(rms_apply, after_cross, gain_three.astype(jnp.float32))
    normed_three = normed_value.astype(jnp.bfloat16)
    before = product(normed_three, weight_in)
    gelu_value, gelu_back = jax.vjp(gelu_smooth, before)
    hidden = gelu_value.astype(jnp.bfloat16)
    output = (after_cross + product(hidden, weight_down)).astype(jnp.bfloat16)
    back_in, back_down = (
        lax.all_gather(ffn_in, ("wide", "narrow"), axis=0, tiled=True),
        lax.all_gather(ffn_out, ("wide", "narrow"), axis=0, tiled=True),
    )
    grad_low = grad_out.astype(jnp.bfloat16)
    grad_down_weight = outer_sum(hidden, grad_low)
    grad_hidden = back_project(grad_low, back_down)
    grad_before = gelu_back(grad_hidden)[0].astype(jnp.bfloat16)
    grad_in_weight = outer_sum(normed_three, grad_before)
    grad_normed_three = back_project(grad_before, back_in)
    grad_cross_part, grad_gain_three = norm_back_three(grad_normed_three)
    grad_cross = grad_out + grad_cross_part
    ffn_terms = (grad_gain_three, grad_in_weight, grad_down_weight)
    summed_ffn = lax.psum_scatter(
        pack_rows(ffn_terms, devices), ("wide", "narrow"), scatter_dimension=0, tiled=True
    )
    ffn_gain_grad, ffn_in_grad, ffn_out_grad = unpack_rows(summed_ffn[0], ffn_terms, devices)
    back_cross_query, back_cross_key, back_cross_value, back_cross_out = (
        lax.all_gather(cross_query, ("wide", "narrow"), axis=0, tiled=True),
        lax.all_gather(cross_key, ("wide", "narrow"), axis=0, tiled=True),
        lax.all_gather(cross_value, ("wide", "narrow"), axis=0, tiled=True),
        lax.all_gather(cross_out, ("wide", "narrow"), axis=0, tiled=True),
    )
    grad_cross_low = grad_cross.astype(jnp.bfloat16)
    grad_cross_out_weight = outer_sum(context_two, grad_cross_low)
    grad_context_two = back_project(grad_cross_low, back_cross_out).astype(jnp.bfloat16)
    grad_query_two, grad_keys_two, grad_values_two, unused_extra = attend_backward(
        query_two,
        keys_two,
        values_two,
        None,
        memory_visible,
        seq_count,
        totals_two,
        grad_context_two,
    )
    grad_cross_query_weight = outer_sum(normed_two, grad_query_two)
    grad_cross_key_weight = outer_sum(memory, grad_keys_two)
    grad_cross_value_weight = outer_sum(memory, grad_values_two)
    memory_grad = back_project(grad_keys_two, back_cross_key) + back_project(
        grad_values_two, back_cross_value
    )
    grad_self_part, grad_gain_two = norm_back_two(back_project(grad_query_two, back_cross_query))
    grad_self = grad_cross + grad_self_part
    cross_terms = (
        grad_gain_two,
        grad_cross_query_weight,
        grad_cross_key_weight,
        grad_cross_value_weight,
        grad_cross_out_weight,
    )
    summed_cross = lax.psum_scatter(
        pack_rows(cross_terms, devices), ("wide", "narrow"), scatter_dimension=0, tiled=True
    )
    cross_gain_grad, cross_query_grad, cross_key_grad, cross_value_grad, cross_out_grad = (
        unpack_rows(summed_cross[0], cross_terms, devices)
    )
    back_query, back_key, back_value, back_out = (
        lax.all_gather(self_query, ("wide", "narrow"), axis=0, tiled=True),
        lax.all_gather(self_key, ("wide", "narrow"), axis=0, tiled=True),
        lax.all_gather(self_value, ("wide", "narrow"), axis=0, tiled=True),
        lax.all_gather(self_out, ("wide", "narrow"), axis=0, tiled=True),
    )
    grad_self_low = grad_self.astype(jnp.bfloat16)
    grad_out_weight = outer_sum(context_one, grad_self_low)
    grad_context_one = back_project(grad_self_low, back_out).astype(jnp.bfloat16)
    grad_query_one, grad_keys_one, grad_values_one, grad_relative = attend_backward(
        query_one,
        keys_one,
        values_one,
        relative,
        self_visible,
        seq_count,
        totals_one,
        grad_context_one,
    )
    table_term = jnp.einsum("hij,ijb->bh", grad_relative, one_hot, precision=lax.Precision.HIGHEST)
    position_table_grad = lax.psum(table_term, ("wide", "narrow"))
    grad_query_weight = outer_sum(normed_one, grad_query_one)
    grad_key_weight = outer_sum(normed_one, grad_keys_one)
    grad_value_weight = outer_sum(normed_one, grad_values_one)
    grad_normed_one = (
        back_project(grad_query_one, back_query)
        + back_project(grad_keys_one, back_key)
        + back_project(grad_values_one, back_value)
    )
    grad_source_part, grad_gain_one = norm_back_one(grad_normed_one)
    input_grad = grad_self + grad_source_part
    self_terms = (
        grad_gain_one,
        grad_query_weight,
        grad_key_weight,
        grad_value_weight,
        grad_out_weight,
    )
    summed_self = lax.psum_scatter(
        pack_rows(self_terms, devices), ("wide", "narrow"), scatter_dimension=0, tiled=True
    )
    self_gain_grad, self_query_grad, self_key_grad, self_value_grad, self_out_grad = unpack_rows(
        summed_self[0], self_terms, devices
    )
    return (
        output,
        input_grad,
        memory_grad,
        self_gain_grad,
        self_query_grad,
        self_key_grad,
        self_value_grad,
        self_out_grad,
        position_table_grad,
        cross_gain_grad,
        cross_query_grad,
        cross_key_grad,
        cross_value_grad,
        cross_out_grad,
        ffn_gain_grad,
        ffn_in_grad,
        ffn_out_grad,
    )


def body(
    tokens,
    memory,
    cotangent,
    target_lengths,
    memory_lengths,
    self_gain,
    self_query,
    self_key,
    self_value,
    self_out,
    position_table,
    cross_gain,
    cross_query,
    cross_key,
    cross_value,
    cross_out,
    ffn_gain,
    ffn_in,
    ffn_out,
):
    wide_count = lax.axis_size("wide")
    narrow_count = lax.axis_size("narrow")
    seq_count = target_lengths.shape[0]
    target_rows = tokens.shape[0] // seq_count
    memory_rows = memory.shape[0] // seq_count
    positions = jnp.arange(target_rows, dtype=jnp.int32)
    live_rows = positions[None, :] < target_lengths[:, None]
    causal = positions[None, :] <= positions[:, None]
    self_visible = causal[None] & live_rows[:, None, :]
    memory_visible = (jnp.arange(memory_rows, dtype=jnp.int32)[None, :] < memory_lengths[:, None])[
        :, None, :
    ]
    grad_out = jnp.where(live_rows.reshape(-1, 1), cotangent.astype(jnp.float32), 0.0)
    bucket = bucket_index(target_rows)
    one_hot = (bucket[:, :, None] == jnp.arange(NB, dtype=jnp.int32)[None, None, :]).astype(
        jnp.float32
    )
    relative = jnp.einsum(
        "ijb,bh->hij", one_hot, position_table.astype(jnp.float32), precision=lax.Precision.HIGHEST
    )
    rank = lax.axis_index("wide") * narrow_count + lax.axis_index("narrow")
    own_gains = jnp.stack([self_gain, cross_gain, ffn_gain])
    spread = lax.dynamic_update_slice(jnp.zeros((8, 768), jnp.bfloat16), own_gains, (0, rank * 24))
    (mats, down, gains, turned, memory_turned, hidden_turned, small, keys_two, values_two, after_self, after_cross, hidden, slope, self_log, cross_log) = forward_call(
        (self_query, self_key, self_value, self_out, cross_query, cross_key, cross_value, cross_out, ffn_in, ffn_out, spread),
        tokens, memory, jnp.pad(position_table.T, ((0, 4), (0, 0))), target_lengths, memory_lengths)
    gain_one, gain_two, gain_three = gains[0], gains[1], gains[2]
    (weight_query, weight_key, weight_value, weight_out, cross_weight_query, cross_weight_key, cross_weight_value, cross_weight_out) = (
        mats[k].reshape(768, 768) for k in range(8)
    )
    weight_in = [mats[8 + k].reshape(768, 768) for k in range(4)]
    weight_down = down.reshape(3072, 768)
    query_one, keys_one, values_one, context_one, query_two, context_two = (small[k] for k in range(6))
    totals_one, totals_two = self_log[None, :12], cross_log[None, :12]
    source = tokens.astype(jnp.float32)
    _, norm_back_one = jax.vjp(rms_apply, source, gain_one)
    _, norm_back_two = jax.vjp(rms_apply, after_self, gain_two)
    _, norm_back_three = jax.vjp(rms_apply, after_cross, gain_three)
    normed_one, normed_two, normed_three = (turned[k][:, :256].T for k in (0, 2, 4))
    hidden = hidden.transpose(1, 0, 2).reshape(256, 3072)
    slope = slope.transpose(1, 0, 2).reshape(256, 3072)
    output = (after_cross + product(hidden, weight_down)).astype(jnp.bfloat16)
    grad_low = grad_out.astype(jnp.bfloat16)
    grad_down_weight = outer_sum(hidden, grad_low)
    grad_hidden = back_project(grad_low, weight_down)
    grad_before = (grad_hidden * slope.astype(jnp.float32)).astype(jnp.bfloat16)
    grad_in_weight = outer_sum(normed_three, grad_before)
    grad_normed_three = sum(back_project(grad_before[:, 768 * k : 768 * k + 768], weight_in[k]) for k in range(4))
    grad_cross_part, grad_gain_three = norm_back_three(grad_normed_three)
    grad_cross = grad_out + grad_cross_part
    grad_cross_low = grad_cross.astype(jnp.bfloat16)
    grad_cross_out_weight = outer_sum(context_two, grad_cross_low)
    grad_context_two = back_project(grad_cross_low, cross_weight_out).astype(jnp.bfloat16)
    grad_query_two, grad_keys_two, grad_values_two, unused_extra = attend_backward(
        query_two,
        keys_two,
        values_two,
        None,
        memory_visible,
        seq_count,
        totals_two,
        grad_context_two,
    )
    grad_cross_query_weight = outer_sum(normed_two, grad_query_two)
    grad_cross_key_weight = outer_sum(memory, grad_keys_two)
    grad_cross_value_weight = outer_sum(memory, grad_values_two)
    memory_grad = back_project(grad_keys_two, cross_weight_key) + back_project(
        grad_values_two, cross_weight_value
    )
    grad_self_part, grad_gain_two = norm_back_two(back_project(grad_query_two, cross_weight_query))
    grad_self = grad_cross + grad_self_part
    grad_self_low = grad_self.astype(jnp.bfloat16)
    grad_out_weight = outer_sum(context_one, grad_self_low)
    grad_context_one = back_project(grad_self_low, weight_out).astype(jnp.bfloat16)
    grad_query_one, grad_keys_one, grad_values_one, grad_relative = attend_backward(
        query_one,
        keys_one,
        values_one,
        relative,
        self_visible,
        seq_count,
        totals_one,
        grad_context_one,
    )
    table_term = jnp.einsum("hij,ijb->bh", grad_relative, one_hot, precision=lax.Precision.HIGHEST)
    grad_query_weight = outer_sum(normed_one, grad_query_one)
    grad_key_weight = outer_sum(normed_one, grad_keys_one)
    grad_value_weight = outer_sum(normed_one, grad_values_one)
    grad_normed_one = (
        back_project(grad_query_one, weight_query)
        + back_project(grad_keys_one, weight_key)
        + back_project(grad_values_one, weight_value)
    )
    grad_source_part, grad_gain_one = norm_back_one(grad_normed_one)
    input_grad = grad_self + grad_source_part
    mat_grads = jnp.stack(
        [
            term.astype(jnp.bfloat16)
            for term in (
                grad_query_weight,
                grad_key_weight,
                grad_value_weight,
                grad_out_weight,
                grad_cross_query_weight,
                grad_cross_key_weight,
                grad_cross_value_weight,
                grad_cross_out_weight,
                grad_in_weight[:, :768],
                grad_in_weight[:, 768:1536],
                grad_in_weight[:, 1536:2304],
                grad_in_weight[:, 2304:],
            )
        ]
    ).reshape(12, 4, 2, 2, 2, 24, 768)
    down_grads = grad_down_weight.astype(jnp.bfloat16).reshape(4, 2, 2, 2, 96, 768)
    table_rows = jnp.pad(table_term.T, ((0, 4), (0, 768 - NB)))
    extra = jnp.concatenate([jnp.stack([grad_gain_one, grad_gain_two, grad_gain_three]), jnp.zeros((5, 768), jnp.float32), table_rows])
    mat_sums, ffn_out_grad, extra = scatter(mat_grads, down_grads, extra)
    position_table_grad = extra[8:20, :NB].T
    own = lax.dynamic_slice(extra, (0, rank * 24), (8, 24))
    self_gain_grad, cross_gain_grad, ffn_gain_grad = own[0], own[1], own[2]
    (self_query_grad, self_key_grad, self_value_grad, self_out_grad, cross_query_grad, cross_key_grad, cross_value_grad, cross_out_grad) = (
        mat_sums[k] for k in range(8)
    )
    ffn_in_grad = jnp.concatenate([mat_sums[8 + k] for k in range(4)], axis=1)
    return (
        output,
        input_grad,
        memory_grad,
        self_gain_grad,
        self_query_grad,
        self_key_grad,
        self_value_grad,
        self_out_grad,
        position_table_grad,
        cross_gain_grad,
        cross_query_grad,
        cross_key_grad,
        cross_value_grad,
        cross_out_grad,
        ffn_gain_grad,
        ffn_in_grad,
        ffn_out_grad,
    )


def solution(mesh):
    whole = (mesh.shape["wide"], mesh.shape["narrow"]) == (8, 4)
    placed = (
        P(("wide", "narrow"), None),
        P(("wide", "narrow"), None),
        P(("wide", "narrow"), None),
        P(("wide", "narrow")),
        P(("wide", "narrow")),
        P(("wide", "narrow")),
        P(("wide", "narrow"), None),
        P(("wide", "narrow"), None),
        P(("wide", "narrow"), None),
        P(("wide", "narrow"), None),
        P(),
        P(("wide", "narrow")),
        P(("wide", "narrow"), None),
        P(("wide", "narrow"), None),
        P(("wide", "narrow"), None),
        P(("wide", "narrow"), None),
        P(("wide", "narrow")),
        P(("wide", "narrow"), None),
        P(("wide", "narrow"), None),
    )
    return jax.shard_map(
        body if whole else plain_body,
        mesh=mesh,
        in_specs=placed,
        out_specs=(
            P(("wide", "narrow"), None),
            P(("wide", "narrow"), None),
            P(("wide", "narrow"), None),
            P(("wide", "narrow")),
            P(("wide", "narrow"), None),
            P(("wide", "narrow"), None),
            P(("wide", "narrow"), None),
            P(("wide", "narrow"), None),
            P(),
            P(("wide", "narrow")),
            P(("wide", "narrow"), None),
            P(("wide", "narrow"), None),
            P(("wide", "narrow"), None),
            P(("wide", "narrow"), None),
            P(("wide", "narrow")),
            P(("wide", "narrow"), None),
            P(("wide", "narrow"), None),
        ),
        check_vma=False,
    )
```

```python
import math

import jax
import jax.numpy as jnp
from jax import lax
from jax.experimental import pallas as pl
from jax.experimental.pallas import tpu as pltpu
from jax.sharding import PartitionSpec as P

DH = 64
NB = 32
MAXDIST = 128


AXES = ("wide", "narrow")
EPSILON = 1e-06
NEGATIVE = -1e30


def bucket_index(length):
    offsets = jnp.arange(length, dtype=jnp.int32)
    distance = jnp.maximum(offsets[:, None] - offsets[None, :], 0)
    exact_part = NB // 2
    bucket = jnp.minimum(distance, exact_part)
    for step in range(1, NB - exact_part):
        bound = math.ceil(exact_part * (MAXDIST / exact_part) ** (step / (NB - exact_part)))
        bucket = bucket + (distance >= bound).astype(jnp.int32)
    return bucket


def rms_apply(field, gain):
    inverse = lax.rsqrt(jnp.mean(field * field, axis=-1, keepdims=True) + EPSILON)
    return field * inverse * gain


def gelu_smooth(field):
    return jax.nn.gelu(field, approximate=True)


def product(left, right):
    return jnp.dot(left, right, preferred_element_type=jnp.float32)


def outer_sum(left, right):
    return jnp.einsum("rd,re->de", left, right, preferred_element_type=jnp.float32)


def back_project(left, right):
    return jnp.einsum("re,de->rd", left, right, preferred_element_type=jnp.float32)


def pack_rows(arrays, devices):
    return jnp.concatenate([array.reshape(devices, -1) for array in arrays], axis=1)


def unpack_rows(packed_row, arrays, devices):
    results = []
    offset = 0
    for array in arrays:
        shard_shape = (array.shape[0] // devices,) + array.shape[1:]
        count = array.size // devices
        results.append(packed_row[offset : offset + count].reshape(shard_shape))
        offset = offset + count
    return tuple(results)


def head_blocks(array, index, seq_count):
    block = lax.dynamic_slice_in_dim(array, index * 2 * DH, 2 * DH, 1)
    return block.reshape(seq_count, -1, 2, DH)


def flat_block(block):
    return block.reshape(-1, 2 * DH)


def scored(query_block, keys_block, extra, visible, index):
    scores = jnp.einsum(
        "sqhd,skhd->shqk", query_block, keys_block, preferred_element_type=jnp.float32
    ) * DH ** (-0.5)
    if extra is not None:
        scores = scores + lax.dynamic_slice_in_dim(extra, index * 2, 2, 0)[None]
    return jnp.where(visible[:, None], scores, NEGATIVE)


def attend_forward(query, keys, values, extra, visible, seq_count):
    pairs = query.shape[1] // (2 * DH)
    start_context = jnp.zeros(query.shape, jnp.bfloat16)
    start_totals = jnp.zeros((seq_count, 2 * pairs, query.shape[0] // seq_count), jnp.float32)

    def one_pair(index, carry):
        context, log_total = carry
        query_block = head_blocks(query, index, seq_count)
        scores = scored(query_block, head_blocks(keys, index, seq_count), extra, visible, index)
        peak = jnp.max(scores, axis=-1, keepdims=True)
        raised = jnp.exp(scores - peak)
        total = jnp.sum(raised, axis=-1, keepdims=True)
        attend = (raised / total).astype(jnp.bfloat16)
        mixed = jnp.einsum(
            "shqk,skhd->sqhd",
            attend,
            head_blocks(values, index, seq_count),
            preferred_element_type=jnp.float32,
        )
        context = lax.dynamic_update_slice_in_dim(
            context, flat_block(mixed.astype(jnp.bfloat16)), index * 2 * DH, 1
        )
        log_total = lax.dynamic_update_slice_in_dim(
            log_total, (peak + jnp.log(total))[..., 0], index * 2, 1
        )
        return (context, log_total)

    return lax.fori_loop(0, pairs, one_pair, (start_context, start_totals))


def attend_backward(query, keys, values, extra, visible, seq_count, log_total, grad_context):
    pairs = query.shape[1] // (2 * DH)
    scale = DH ** (-0.5)
    extra_shape = extra.shape if extra is not None else (1,)
    start_grads = (
        jnp.zeros(query.shape, jnp.bfloat16),
        jnp.zeros(keys.shape, jnp.bfloat16),
        jnp.zeros(values.shape, jnp.bfloat16),
        jnp.zeros(extra_shape, jnp.float32),
    )

    def one_pair(index, carry):
        grad_query, grad_keys, grad_values, grad_extra = carry
        query_block = head_blocks(query, index, seq_count)
        keys_block = head_blocks(keys, index, seq_count)
        value_block = head_blocks(values, index, seq_count)
        upstream = head_blocks(grad_context, index, seq_count)
        scores = scored(query_block, keys_block, extra, visible, index)
        attend = jnp.exp(scores - lax.dynamic_slice_in_dim(log_total, index * 2, 2, 1)[..., None])
        grad_attend = jnp.einsum(
            "sqhd,skhd->shqk", upstream, value_block, preferred_element_type=jnp.float32
        )
        value_grad = jnp.einsum(
            "shqk,sqhd->skhd",
            attend.astype(jnp.bfloat16),
            upstream,
            preferred_element_type=jnp.float32,
        ).astype(jnp.bfloat16)
        inner = jnp.sum(attend * grad_attend, axis=-1, keepdims=True)
        grad_score = attend * (grad_attend - inner)
        rounded = grad_score.astype(jnp.bfloat16)
        query_grad = (
            jnp.einsum("shqk,skhd->sqhd", rounded, keys_block, preferred_element_type=jnp.float32)
            * scale
        ).astype(jnp.bfloat16)
        keys_grad = (
            jnp.einsum("shqk,sqhd->skhd", rounded, query_block, preferred_element_type=jnp.float32)
            * scale
        ).astype(jnp.bfloat16)
        offset = index * 2 * DH
        grad_query = lax.dynamic_update_slice_in_dim(grad_query, flat_block(query_grad), offset, 1)
        grad_keys = lax.dynamic_update_slice_in_dim(grad_keys, flat_block(keys_grad), offset, 1)
        grad_values = lax.dynamic_update_slice_in_dim(
            grad_values, flat_block(value_grad), offset, 1
        )
        if extra is not None:
            grad_extra = lax.dynamic_update_slice_in_dim(
                grad_extra, jnp.sum(grad_score, axis=0), index * 2, 0
            )
        return (grad_query, grad_keys, grad_values, grad_extra)

    return lax.fori_loop(0, pairs, one_pair, start_grads)


MESH = pl.DeviceIdType.MESH
HALF = 384
ROWS = 256
LOW, FULL = jnp.bfloat16, jnp.float32
EVERY = slice(None)


def place():
    wide = lax.axis_index(AXES[0])
    narrow = lax.axis_index(AXES[1])
    return wide // 2, lax.rem(wide, 2), narrow // 2, lax.rem(narrow, 2)


def device(z, x, y, c):
    return (z * 2 + x, y * 2 + c)


def partners(z, x, y, c):
    return (
        device(z ^ 1, x, y, c),
        device(z ^ 2, x, y, c),
        device(z ^ 3, x, y, c),
        device(z, 1 - x, y, c),
        device(z, x, 1 - y, c),
        device(z, x, y, 1 - c),
    )


def enter(everyone):
    barrier = pltpu.get_barrier_semaphore()
    for other in everyone:
        pl.semaphore_signal(barrier, inc=1, device_id=other, device_id_type=MESH)
    pl.semaphore_wait(barrier, len(everyone))


class Post:
    def __init__(self, send, recv, near):
        self.send, self.recv, self.near = send, recv, near
        self.used, self.used_near, self.started, self.open = 0, 0, [], []

    def copy(self, source, target, where):
        made = pltpu.make_async_remote_copy(
            src_ref=source,
            dst_ref=target,
            send_sem=self.send.at[self.used],
            recv_sem=self.recv.at[self.used],
            device_id=where,
            device_id_type=MESH,
        )
        self.used += 1
        made.start()
        self.started.append(made)
        return made

    def local(self, source, target, keep=False):
        made = pltpu.make_async_copy(source, target, self.near.at[self.used_near])
        self.used_near += 1
        made.start()
        if not keep:
            self.open.append(made)
        return made

    def finish(self):
        for made in self.started:
            made.wait_send()
        for made in self.open:
            made.wait()


def arrived(copies):
    for made in copies:
        made.wait_recv()


def dot(left, right):
    return jnp.dot(left, right, preferred_element_type=FULL)


def dot_last(left, right):
    return lax.dot_general(left, right, (((1,), (1,)), ((), ())), preferred_element_type=FULL)


def dot_first(left, right):
    return lax.dot_general(left, right, (((0,), (0,)), ((), ())), preferred_element_type=FULL)


def square(ref, index):
    return ref[index].reshape(768, 768)


def bucket_rows():
    distance = lax.broadcasted_iota(jnp.int32, (NB, ROWS), 1)
    row = lax.broadcasted_iota(jnp.int32, (NB, ROWS), 0)
    exact_part = NB // 2
    bucket = jnp.minimum(distance, exact_part)
    for step in range(1, NB - exact_part):
        bound = math.ceil(exact_part * (MAXDIST / exact_part) ** (step / (NB - exact_part)))
        bucket = bucket + (distance >= bound).astype(jnp.int32)
    return (bucket == row).astype(LOW)


def self_mask(length):
    key = lax.broadcasted_iota(jnp.int32, (ROWS, ROWS), 0)
    query = lax.broadcasted_iota(jnp.int32, (ROWS, ROWS), 1)
    return jnp.where((key <= query) & (key < length), 0.0, NEGATIVE)


def memory_mask(length, rows):
    key = lax.broadcasted_iota(jnp.int32, (rows, 1), 0)
    return jnp.where(key < length, 0.0, NEGATIVE)


def slanted(row):
    return pltpu.roll(jnp.broadcast_to(row, (ROWS, ROWS)), 0, 1, stride=1, stride_axis=0)


def one_head(block, head):
    lane = lax.broadcasted_iota(jnp.int32, block.shape, 1)
    return jnp.where((lane < DH) if head == 0 else (lane >= DH), block, jnp.zeros_like(block))


def inverse_rms(field):
    return lax.rsqrt(jnp.mean(field * field, axis=-1, keepdims=True) + EPSILON)


PAIRS = [("gains", 0, 1), (2, 3), (4, 7), (5, 6), (8, 9), (10, 11), ((0, 0), (0, 1))]
LATE = ((1, 0), (1, 1))
ORDERS = {"gains": "zxy", (0, 0): "zxy", (0, 1): "zyx", (1, 0): "xyz", (1, 1): "yxz"}
for _pair in PAIRS[:-1]:
    for _unit, _order in zip(_pair[-2:], ("zxy", "zyx")):
        ORDERS[_unit] = _order


def forward_schedule(ahead=5):
    events = [(unit, 0) for unit in PAIRS[0]] + [(unit, 0) for unit in LATE]
    for pair in PAIRS[1:ahead]:
        events += [(unit, 0) for unit in pair]
    count = len(PAIRS)
    for step in range(count + 4):
        for stage in (1, 0, None, 2, 3, 4):
            if stage is None:
                if step in (0, 2):
                    events += [(unit, 1 + step // 2) for unit in LATE]
                continue
            index = step + ahead if stage == 0 else step - stage + 1
            if (stage > 0 or index >= ahead) and 0 <= index < count:
                events += [(unit, stage) for unit in PAIRS[index]]
    return events + [(unit, stage) for stage in (3, 4) for unit in LATE]


class Gather:
    def __init__(self, post, mats, down, gains, kept, spot, everyone):
        self.post, self.mats, self.down, self.gains, self.kept = post, mats, down, gains, kept
        self.spot, self.everyone = spot, everyone
        self.events = forward_schedule()
        self.waits, self.near, self.ready = {}, {}, set()

    def at(self, unit, *where):
        if unit == "gains":
            return self.gains.at[where]
        if isinstance(unit, tuple):
            return self.down.at[where + (pl.ds(unit[0] * 48, 48), pl.ds(unit[1] * HALF, HALF))]
        return self.mats.at[(unit,) + where]

    def forward(self, unit, where, targets):
        return [self.post.copy(self.at(unit, *where), self.at(unit, *where), target) for target in targets]

    def run(self, unit, stage):
        z, x, y, c = self.spot
        across, along, sibling = self.everyone[3:]
        order = ORDERS[unit]
        if stage == 0:
            targets = {"z": self.everyone[:3], "x": (across,), "y": (along,)}[order[0]]
            self.near[unit] = []
            self.waits[unit] = self.forward(unit, self.spot, targets)
            return
        if stage == 4:
            arrived(self.near[unit])
            self.ready.add(unit)
            if isinstance(unit, int):
                self.post.local(self.mats.at[unit], self.kept[0].at[unit])
            if unit == LATE[-1]:
                self.post.local(self.down, self.kept[1])
            return
        arrived(self.waits[unit])
        steps = {
            "zxy": (
                ((EVERY, x, y, c), (across,), (EVERY, x, y, c)),
                ((EVERY, EVERY, y, c), (along,), (EVERY, 1 - x, y, c)),
                (None, (), (EVERY, EVERY, 1 - y, c)),
            ),
            "zyx": (
                ((EVERY, x, y, c), (along,), (EVERY, x, y, c)),
                ((EVERY, x, EVERY, c), (across,), (EVERY, x, 1 - y, c)),
                (None, (), (EVERY, 1 - x, EVERY, c)),
            ),
            "xyz": (
                ((z, EVERY, y, c), (along,), None),
                ((z, EVERY, EVERY, c), self.everyone[:3], (z, EVERY, EVERY, c)),
                (None, (), "others"),
            ),
            "yxz": (
                ((z, x, EVERY, c), (across,), None),
                ((z, EVERY, EVERY, c), self.everyone[:3], (z, EVERY, EVERY, c)),
                (None, (), "others"),
            ),
        }
        where, targets, near = steps[order][stage - 1]
        self.waits[unit] = self.forward(unit, where, targets) if targets else []
        if near == "others":
            for k in range(3):
                self.near[unit] += self.forward(unit, (z ^ (k + 1), EVERY, EVERY, c), (sibling,))
        elif near is not None:
            self.near[unit] += self.forward(unit, near, (sibling,))

    def pump(self, count):
        for _ in range(count):
            if self.events:
                self.run(*self.events.pop(0))

    def require(self, *units):
        for unit in units:
            while unit not in self.ready:
                self.pump(1)


def forward_kernel(*refs):
    shards, (tokens, memory, cotangent, table, lengths, memory_lengths) = refs[:11], refs[11:17]
    kept_mats, kept_down, gain_rows = refs[17:20]
    (turned, memory_turned, small, keys_out, values_out, self_out, cross_out, hidden_out, slope_out, grads_out) = refs[20:30]
    self_log, cross_log = refs[30:32]
    (gains, mats, down, keep, keys, values, stage, memory_stage, hidden, slope) = refs[32:42]
    (hidden_turned, after_self, after_cross, own_cut, other_cut, grads, near, send, recv) = refs[42:]
    spot = place()
    everyone = partners(*spot)
    sibling = everyone[5]
    post = Post(send, recv, near)
    comm = Gather(post, mats, down, gains, (kept_mats, kept_down), spot, everyone)
    for index in range(8):
        mats.at[(index,) + spot][...] = shards[index][...]
    for index in range(4):
        mats.at[(8 + index,) + spot][...] = shards[8][:, index * 768 : (index + 1) * 768]
    down.at[spot][...] = shards[9][...]
    gains.at[spot][...] = shards[10][...]
    enter(everyone)
    comm.pump(9)
    from_sibling = []

    def turn(block, staged, target, lanes=ROWS):
        staged[...] = block.T
        post.local(staged, target.at[:, pl.ds(0, lanes)])
        from_sibling.append(post.copy(staged, target.at[:, pl.ds(lanes, lanes)], sibling))

    for block in range(4):
        turn(memory[block * ROWS : (block + 1) * ROWS], memory_stage.at[block], memory_turned.at[block])
        comm.pump(1)
    live = lax.broadcasted_iota(jnp.int32, (ROWS, 1), 0) < lengths[0]
    grad_low = jnp.where(live, cotangent[...], jnp.zeros_like(cotangent[...]))
    left, right = grad_low[:, :HALF], grad_low[:, HALF:]
    core = spot[3]
    own_cut[0] = jnp.where(core == 0, left, right)
    other_cut[...] = jnp.where(core == 0, right, left)
    from_sibling.append(post.copy(other_cut, own_cut.at[1], sibling))
    source = tokens[...].astype(FULL)
    inverse = inverse_rms(source)
    one_hot = bucket_rows()
    bias = dot_first(table[...], one_hot)
    visible = self_mask(lengths[0])
    comm.require("gains")
    gain_rows[...] = jnp.sum(gains[...].astype(FULL).reshape(32, 8, 768), axis=0)
    normed = (source * inverse * gain_rows[0:1]).astype(LOW)
    turn(normed, stage.at[0], turned.at[0])

    def project(unit, slot, block):
        comm.require(unit)
        keep[slot] = dot(block, square(mats, unit)).astype(LOW)
        post.local(keep.at[slot], small.at[slot])

    project(0, 0, normed)
    project(1, 1, normed)
    project(2, 2, normed)

    def attend(pair, head, query, key_block, value_block, extra, log_ref):
        scores = dot_last(key_block, one_head(query, head)) + extra
        peak = jnp.max(scores, axis=0, keepdims=True)
        raised = jnp.exp(scores - peak)
        total = jnp.sum(raised, axis=0, keepdims=True)
        mixed = dot_first(value_block, raised.astype(LOW)) / total
        log_ref[pair * 2 + head : pair * 2 + head + 1] = peak + jnp.log(total)
        return mixed[head * DH : head * DH + DH]

    for pair in range(6):
        span = slice(pair * 128, pair * 128 + 128)
        query = keep[0, :, span] * 0.125
        mixed = [
            attend(
                pair,
                head,
                query,
                keep[1, :, span],
                keep[2, :, span],
                slanted(bias[pair * 2 + head : pair * 2 + head + 1]) + visible,
                self_log,
            )
            for head in range(2)
        ]
        keep[3, :, span] = jnp.concatenate(mixed, axis=0).T.astype(LOW)
        comm.pump(2)
    post.local(keep.at[3], small.at[3])
    context = keep[3]
    turn(context, stage.at[1], turned.at[1])
    comm.require(3)
    after_self[...] = source + dot(context, square(mats, 3))
    post.local(after_self, self_out)
    normed = (after_self[...] * inverse_rms(after_self[...]) * gain_rows[1:2]).astype(LOW)
    turn(normed, stage.at[2], turned.at[2])
    project(4, 4, normed)
    for unit, held, out in ((5, keys, keys_out), (6, values, values_out)):
        comm.require(unit)
        for block in range(4):
            held[block] = dot(memory[block * ROWS : (block + 1) * ROWS], square(mats, unit)).astype(LOW)
            comm.pump(1)
        post.local(held, out)
    shown = memory_mask(memory_lengths[0], 1024)
    for pair in range(6):
        span = slice(pair * 128, pair * 128 + 128)
        query = keep[4, :, span] * 0.125
        mixed = [
            attend(pair, head, query, keys[:, :, span].reshape(1024, 128), values[:, :, span].reshape(1024, 128), shown, cross_log) for head in range(2)
        ]
        keep[5, :, span] = jnp.concatenate(mixed, axis=0).T.astype(LOW)
        comm.pump(2)
    post.local(keep.at[5], small.at[5])
    context = keep[5]
    turn(context, stage.at[3], turned.at[3])
    comm.require(7)
    after_cross[...] = after_self[...] + dot(context, square(mats, 7))
    post.local(after_cross, cross_out)
    normed = (after_cross[...] * inverse_rms(after_cross[...]) * gain_rows[2:3]).astype(LOW)
    turn(normed, stage.at[4], turned.at[4])
    root = math.sqrt(2.0 / math.pi)
    for block in range(4):
        comm.require(8 + block)
        before = dot(normed, square(mats, 8 + block))
        squared = before * before
        bent = jnp.tanh(root * before * (1.0 + 0.044715 * squared))
        lifted = 0.5 * (1.0 + bent)
        value = (before * lifted).astype(LOW)
        hidden[block] = value
        slope[block] = (
            lifted + 0.5 * root * before * (1.0 - bent * bent) * (1.0 + 3 * 0.044715 * squared)
        ).astype(LOW)
        post.local(hidden.at[block], hidden_out.at[block])
        post.local(slope.at[block], slope_out.at[block])
        hidden_turned[block, :, :ROWS] = value.T
        half = hidden_turned.at[block, :, pl.ds(0, ROWS)]
        from_sibling.append(post.copy(half, hidden_turned.at[block, :, pl.ds(ROWS, ROWS)], sibling))
        comm.pump(1)
    arrived(from_sibling)
    for block in range(4):
        comm.pump(1)
        grads[block] = dot(hidden_turned[block], own_cut[...].reshape(512, HALF)).astype(LOW).reshape(2, 2, 2, 96, HALF)
        post.local(grads.at[block], grads_out.at[block])
    while comm.events:
        comm.pump(1)
    post.finish()


def forward_call(shards, *rest):
    kind = jax.ShapeDtypeStruct
    anywhere, vmem = pl.BlockSpec(memory_space=pl.ANY), pl.BlockSpec(memory_space=pltpu.VMEM)
    smem = pl.BlockSpec(memory_space=pltpu.SMEM)
    outs = (
        (kind((12, 4, 2, 2, 2, 24, 768), LOW), anywhere),
        (kind((4, 2, 2, 2, 96, 768), LOW), anywhere),
        (kind((8, 768), FULL), vmem),
        (kind((5, 768, 512), LOW), anywhere),
        (kind((4, 768, 512), LOW), anywhere),
        (kind((6, 256, 768), LOW), anywhere),
        (kind((4, 256, 768), LOW), anywhere),
        (kind((4, 256, 768), LOW), anywhere),
        (kind((256, 768), FULL), anywhere),
        (kind((256, 768), FULL), anywhere),
        (kind((4, 256, 768), LOW), anywhere),
        (kind((4, 256, 768), LOW), anywhere),
        (kind((4, 2, 2, 2, 96, HALF), LOW), anywhere),
        (kind((16, 256), FULL), vmem),
        (kind((16, 256), FULL), vmem),
    )
    return pl.pallas_call(
        forward_kernel,
        out_shape=tuple(out[0] for out in outs),
        in_specs=[vmem] * 15 + [smem] * 2,
        out_specs=tuple(out[1] for out in outs),
        scratch_shapes=[
            pltpu.VMEM((4, 2, 2, 2, 8, 768), LOW),
            pltpu.VMEM((12, 4, 2, 2, 2, 24, 768), LOW),
            pltpu.VMEM((4, 2, 2, 2, 96, 768), LOW),
            pltpu.VMEM((6, 256, 768), LOW),
            pltpu.VMEM((4, 256, 768), LOW),
            pltpu.VMEM((4, 256, 768), LOW),
            pltpu.VMEM((5, 768, 256), LOW),
            pltpu.VMEM((4, 768, 256), LOW),
            pltpu.VMEM((4, 256, 768), LOW),
            pltpu.VMEM((4, 256, 768), LOW),
            pltpu.VMEM((4, 768, 512), LOW),
            pltpu.VMEM((256, 768), FULL),
            pltpu.VMEM((256, 768), FULL),
            pltpu.VMEM((2, 256, HALF), LOW),
            pltpu.VMEM((256, HALF), LOW),
            pltpu.VMEM((4, 2, 2, 2, 96, HALF), LOW),
            pltpu.SemaphoreType.DMA((80,)),
            pltpu.SemaphoreType.DMA((180,)),
            pltpu.SemaphoreType.DMA((180,)),
        ],
        compiler_params=pltpu.CompilerParams(
            collective_id=0, has_side_effects=True, vmem_limit_bytes=60 * 2**20
        ),
    )(*shards, *rest)


Z_FIRST = (8, 9)


class Scatter:
    def __init__(self, post, grads, inboxes, done, outs, spot, everyone):
        self.post, self.grads, self.inboxes, self.done, self.outs = post, grads, inboxes, done, outs
        self.spot, self.everyone = spot, everyone
        self.queue, self.waits, self.sent, self.slot, self.flipped, self.count = [], {}, {}, {}, {}, 0

    def at(self, kind, unit, *where):
        mats, down = kind
        if isinstance(unit, int):
            return mats.at[(unit,) + where]
        where += (EVERY,) * (len(down.shape) - 2 - len(where))
        return down.at[where + (pl.ds(0 if unit == "down0" else 48, 48),)]

    def grad(self, unit, *where):
        return self.at(self.grads, self.slot[unit], *where)

    def box(self, number, unit, *where):
        return self.at(self.inboxes[number], unit, *where)

    def begin(self, unit, slot):
        z, x, y, c = self.spot
        self.slot[unit], self.sent[unit] = slot, []
        self.flipped[unit] = self.count % 2 == 1
        self.count += 1
        if unit in Z_FIRST:
            first = Z_FIRST.index(unit)
            self.send(
                unit, 0, [(self.grad(unit, z ^ (k + 1)), self.inboxes[3].at[first, k], self.everyone[k]) for k in range(3)]
            )
        elif self.flipped[unit]:
            self.send(unit, 0, [(self.grad(unit, EVERY, 1 - x, EVERY, EVERY), self.box(0, unit), self.everyone[3])])
        else:
            self.send(unit, 0, [(self.grad(unit, EVERY, EVERY, 1 - y, EVERY), self.box(0, unit), self.everyone[4])])

    def send(self, unit, stage, copies):
        self.waits[unit] = [self.post.copy(*copy) for copy in copies]
        self.sent[unit] += self.waits[unit]
        self.queue.append((unit, stage + 1))

    def add(self, target, *terms):
        total = target[...].astype(FULL)
        for term in terms:
            total = total + term[...].astype(FULL)
        target[...] = total.astype(LOW)

    def run(self, unit, stage):
        z, x, y, c = self.spot
        across, along, sibling = self.everyone[3:]
        flipped, early = self.flipped[unit], unit in Z_FIRST
        arrived(self.waits[unit])
        if stage == 1 and early:
            box = self.inboxes[3].at[Z_FIRST.index(unit)]
            self.add(self.grad(unit, z), *(box.at[k] for k in range(3)))
            if flipped:
                source, target = (z, 1 - x, EVERY, EVERY), across
            else:
                source, target = (z, EVERY, 1 - y, EVERY), along
            self.send(unit, 1, [(self.grad(unit, *source), self.box(0, unit, 0), target)])
        if stage == 2 and early:
            if flipped:
                self.add(self.grad(unit, z, x), self.box(0, unit, 0))
                source, target = (z, x, 1 - y, EVERY), along
            else:
                self.add(self.grad(unit, z, EVERY, y), self.box(0, unit, 0))
                source, target = (z, 1 - x, y, EVERY), across
            self.send(unit, 2, [(self.grad(unit, *source), self.box(1, unit, 0), target)])
        if stage == 1 and not early:
            if flipped:
                self.add(self.grad(unit, EVERY, x, EVERY, EVERY), self.box(0, unit))
                source, target = (EVERY, x, 1 - y, EVERY), along
            else:
                self.add(self.grad(unit, EVERY, EVERY, y, EVERY), self.box(0, unit))
                source, target = (EVERY, 1 - x, y, EVERY), across
            self.send(unit, 1, [(self.grad(unit, *source), self.box(1, unit), target)])
        if stage == 2 and not early:
            self.add(self.grad(unit, EVERY, x, y, EVERY), self.box(1, unit))
            self.send(
                unit,
                2,
                [(self.grad(unit, z ^ (k + 1), x, y, EVERY), self.box(2, unit, k), self.everyone[k]) for k in range(3)],
            )
        if stage == 3:
            total = []
            for core in (c, 1 - c):
                part = self.grad(unit, z, x, y, core)[...].astype(FULL)
                for k in range(1 if early else 3):
                    part = part + (self.box(1, unit, 0, core) if early else self.box(2, unit, k, core))[...].astype(FULL)
                total.append(part)
            mine = pl.ds(pl.multiple_of(c * HALF, 128), HALF)
            if isinstance(unit, int):
                target = self.outs[0].at[unit, :, mine]
            else:
                target = self.outs[1].at[pl.ds(0 if unit == "down0" else 48, 48), mine]
            target[...] = total[0]
            self.at(self.done, unit)[...] = total[1]
            self.send(unit, 3, [(self.at(self.done, unit), target, sibling)])

    def pump(self, count):
        for _ in range(count):
            if self.queue:
                self.run(*self.queue.pop(0))

    def settle(self, unit):
        while (unit, 1) in self.queue or (unit, 2) in self.queue or (unit, 3) in self.queue:
            self.pump(1)
        for made in self.sent[unit][:5]:
            made.wait_send()
            self.post.started = [left for left in self.post.started if left is not made]


def rms_back(upstream, field, gain):
    inverse = inverse_rms(field)
    scaled = gain * upstream
    shift = inverse * inverse * inverse * jnp.mean(scaled * field, axis=-1, keepdims=True)
    return inverse * scaled - field * shift, jnp.sum(upstream * field * inverse, axis=0, keepdims=True)


def split_dot(dotted, left, right):
    high = left.astype(LOW)
    return dotted(right, high) + dotted(right, (left - high.astype(FULL)).astype(LOW))


def backward_kernel(*refs):
    (mats, down, turned, memory_turned, grads_in) = refs[:5]
    (keys_in, values_in, hidden_in, slope_in, after_self, after_cross) = refs[5:11]
    (gains, small, tokens, cotangent, table, self_log, cross_log) = refs[11:18]
    lengths, memory_lengths = refs[18:20]
    (output, input_grad, memory_grad, mats_out, down_out, extra) = refs[20:26]
    (pool_a, pool_b, big, turned_box, wide_a, wide_b, rows_out) = refs[26:33]
    (own_cut, other_cut, own_long, other_long, rows_d, rows_bias, rows_distance) = refs[33:40]
    (grads, grads_down, box_one, box_one_down, box_two, box_two_down, box_three, box_three_down, box_early) = refs[40:49]
    (done, done_down, field, extra_box, stage, near, send, recv) = refs[49:]
    spot = z, x, y, c = place()
    everyone = partners(*spot)
    sibling = everyone[5]
    post = Post(send, recv, near)
    comm = Scatter(
        post,
        (grads, grads_down),
        ((box_one, box_one_down), (box_two, box_two_down), (box_three, box_three_down), box_early),
        (done, done_down),
        (mats_out, down_out),
        spot,
        everyone,
    )

    def fetch(source, target):
        return post.local(source, target, keep=True)

    def weight(ref, index):
        return ref[index * 32 : index * 32 + 32].reshape(768, 768)

    def fetch_weight(index, pool, slot):
        return fetch(mats.at[pl.ds(index * 32, 32)], pool.at[pl.ds(slot * 32, 32)])

    loads = {
        "grads": fetch(grads_in, grads_down),
        "down": fetch(down, pool_a),
        "slope": fetch(slope_in, wide_b),
        "hidden": fetch(hidden_in, wide_a),
        "in": fetch(mats.at[pl.ds(256, 128)], pool_b),
        "memory_turned": fetch(memory_turned, big),
        "turned4": fetch(turned.at[4], turned_box.at[0]),
        "turned3": fetch(turned.at[3], turned_box.at[1]),
        "turned2": fetch(turned.at[2], turned_box.at[2]),
        "after_cross": fetch(after_cross, field),
    }

    def need(*names):
        for name in names:
            loads.pop(name).wait()

    def halves(value):
        left, right = value[:, :HALF], value[:, HALF:]
        return jnp.where(c == 0, left, right), jnp.where(c == 0, right, left)

    def whole(mine, other):
        return jnp.concatenate([jnp.where(c == 0, mine, other), jnp.where(c == 0, other, mine)], axis=1)

    hand = {}

    def share(slot, value):
        mine, other = halves(value)
        own_cut[slot, 0] = mine
        other_cut[slot] = other
        hand[slot] = post.copy(other_cut.at[slot], own_cut.at[slot, 1], sibling)

    def shared(slot):
        hand.pop(slot).wait_recv()
        return own_cut[slot].reshape(512, HALF)

    def both(slot):
        return whole(own_cut[slot, 0], other_cut[slot])

    def settle_into(slot, left, right):
        grads[slot] = dot(left, right).astype(LOW).reshape(4, 2, 2, 2, 24, HALF)

    live = lax.broadcasted_iota(jnp.int32, (ROWS, 1), 0) < lengths[0]
    grad_out = jnp.where(live, cotangent[...].astype(FULL), 0.0)
    grad_low = grad_out.astype(LOW)
    enter(everyone)
    need("grads")
    comm.begin("down0", "down0")
    comm.begin("down1", "down1")
    need("down", "slope")
    for block in range(4):
        grad_hidden = dot_last(grad_low, weight(pool_a, block))
        share(1 + block, (grad_hidden * wide_b[block].astype(FULL)).astype(LOW))
    need("hidden", "after_cross")
    total = field[...]
    for block in range(4):
        total = total + dot(wide_a[block], weight(pool_a, block))
    output[...] = total.astype(LOW)
    loads["keys"] = fetch(keys_in, wide_a)
    for slot, index in enumerate((7, 4, 5, 6)):
        loads[index] = fetch_weight(index, pool_a, slot)
    loads["values"] = fetch(values_in, wide_b)
    need("turned4", "in")
    upstream = 0.0
    for block in range(4):
        settle_into(8 + block, turned_box[0], shared(1 + block))
        comm.begin(8 + block, 8 + block)
        upstream = upstream + dot_last(both(1 + block), weight(pool_b, block))
        comm.pump(1)
    loads["turned1"] = fetch(turned.at[1], turned_box.at[0])
    for slot, index in enumerate((3, 0, 1, 2)):
        loads[index] = fetch_weight(index, pool_b, slot)
    step, gain_three = rms_back(upstream, field[...], gains[2:3])
    extra[...] = jnp.zeros((8, 768), FULL)
    extra[2:3] = gain_three
    input_grad[...] = grad_out + step
    grad_low = input_grad[...].astype(LOW)
    share(5, grad_low)
    loads["after_self"] = fetch(after_self, field)
    need(7)
    upstream = dot_last(grad_low, weight(pool_a, 0)).astype(LOW)
    need("turned3")
    settle_into(7, turned_box[1], shared(5))
    comm.begin(7, 7)
    loads["turned0"] = fetch(turned.at[0], turned_box.at[1])

    heads = (
        lax.broadcasted_iota(jnp.int32, (16, 768), 1) // DH == lax.broadcasted_iota(jnp.int32, (16, 768), 0)
    ).astype(LOW)

    def inner_rows(context):
        rows_d[...] = split_dot(dot_last, upstream_ref[...].astype(FULL) * context.astype(FULL), heads)

    upstream_ref = stage
    upstream_ref[...] = upstream
    inner_rows(small[5])

    def attend_back(pair, query_block, key_block, value_block, log_ref, extra_of, visit):
        span = pl.ds(pl.multiple_of(pair * 128, 128), 128)
        query, handed = query_block(span) * 0.125, upstream_ref[:, span]
        grad_values, grad_keys, grad_query = 0.0, 0.0, []
        key_block, value_block = key_block(span), value_block(span)
        for head in range(2):
            row = pl.ds(pair * 2 + head, 1)
            query_part, handed_part = one_head(query, head), one_head(handed, head)
            attended = jnp.exp(dot_last(key_block, query_part) + extra_of(row) - log_ref[row])
            grad_scores = attended * (dot_last(value_block, handed_part) - rows_d[row])
            visit(row, grad_scores)
            rounded = grad_scores.astype(LOW)
            grad_values = grad_values + dot(attended.astype(LOW), handed_part)
            grad_keys = grad_keys + dot(rounded, query_part)
            grad_query.append(dot_first(key_block, rounded)[head * DH : head * DH + DH])
        grad_query = jnp.concatenate(grad_query, axis=0).T * 0.125
        return grad_query.astype(LOW), grad_keys.astype(LOW), grad_values.astype(LOW)

    need("keys", "values")
    shown = memory_mask(memory_lengths[0], 1024)
    for turn in range(6):
        mine, lane = turn >= 3, slice(turn % 3 * 128, turn % 3 * 128 + 128)
        pair = (c if mine else 1 - c) * 3 + turn % 3
        grad_query, grad_keys, grad_values = attend_back(
            pair,
            lambda span: small[4, :, span],
            lambda span: wide_a[:, :, span].reshape(1024, 128),
            lambda span: wide_b[:, :, span].reshape(1024, 128),
            cross_log,
            lambda row: shown,
            lambda row, value: None,
        )
        grad_keys, grad_values = grad_keys.reshape(4, ROWS, 128), grad_values.reshape(4, ROWS, 128)
        if mine:
            own_cut[6, 0, :, lane] = grad_query
            own_long[0, :, 0, :, lane] = grad_keys
            own_long[1, :, 0, :, lane] = grad_values
        else:
            other_cut[6, :, lane] = grad_query
            other_long[0, :, :, lane] = grad_keys
            other_long[1, :, :, lane] = grad_values
        if turn == 2:
            hand[6] = post.copy(other_cut.at[6], own_cut.at[6, 1], sibling)
            for kind in range(2):
                hand["long", kind] = post.copy(other_long.at[kind], own_long.at[kind, :, 1], sibling)
        comm.pump(1)
    need(4, 5, 6)
    need("turned2", "after_self")
    upstream = dot_last(both(6), weight(pool_a, 1))
    step, gain_two = rms_back(upstream, field[...], gains[1:2])
    extra[1:2] = gain_two
    input_grad[...] = input_grad[...] + step
    grad_low = input_grad[...].astype(LOW)
    share(7, grad_low)
    comm.pump(1)
    need("memory_turned")
    for kind, unit in ((0, 5), (1, 6)):
        hand.pop(("long", kind)).wait_recv()
        total = 0.0
        for block in range(4):
            total = total + dot(big[block], own_long[kind, block].reshape(512, HALF))
        grads[unit] = total.astype(LOW).reshape(4, 2, 2, 2, 24, HALF)
        comm.begin(unit, unit)
        comm.pump(1)
    settle_into(4, turned_box[2], shared(6))
    comm.begin(4, 4)
    comm.pump(1)
    need(3, "turned1")
    upstream_ref[...] = dot_last(grad_low, weight(pool_b, 0)).astype(LOW)
    inner_rows(small[3])
    comm.settle(8)
    settle_into(8, turned_box[0], shared(7))
    comm.begin(3, 8)
    one_hot = bucket_rows()
    rows_bias[0:12] = dot_first(table[...], one_hot)
    visible = self_mask(lengths[0])

    def by_distance(row, value):
        eight = value[:8]
        for first in range(8, ROWS, 8):
            eight = eight + pltpu.roll(value[first : first + 8], ROWS - first, 1)
        total = eight[:1]
        for first in range(1, 8):
            total = total + pltpu.roll(eight, ROWS - first, 1)[first : first + 1]
        rows_distance[row] = total

    rows_distance[...] = jnp.zeros((16, ROWS), FULL)
    for turn in range(6):
        mine, lane = turn >= 3, slice(turn % 3 * 128, turn % 3 * 128 + 128)
        pair = (c if mine else 1 - c) * 3 + turn % 3
        parts = attend_back(
            pair,
            lambda span: small[0, :, span],
            lambda span: small[1, :, span],
            lambda span: small[2, :, span],
            self_log,
            lambda row: slanted(rows_bias[row]) + visible,
            by_distance,
        )
        for slot, part in zip((8, 9, 10), parts):
            if mine:
                own_cut[slot, 0, :, lane] = part
            else:
                other_cut[slot, :, lane] = part
        if turn == 2:
            for slot in (8, 9, 10):
                hand[slot] = post.copy(other_cut.at[slot], own_cut.at[slot, 1], sibling)
        comm.pump(2)
    need("turned0", 0, 1, 2)
    for unit in range(3):
        comm.settle(9 + unit)
        settle_into(9 + unit, turned_box[1], shared(8 + unit))
        comm.begin(unit, 9 + unit)
        comm.pump(1)
    upstream = 0.0
    for unit in range(3):
        upstream = upstream + dot_last(both(8 + unit), weight(pool_b, 1 + unit))
    step, gain_one = rms_back(upstream, tokens[...].astype(FULL), gains[0:1])
    extra[0:1] = gain_one
    high = rows_distance[...].astype(LOW)
    many = jnp.concatenate([one_hot] * 16, axis=0)
    sums = dot_last(high, many) + dot_last((rows_distance[...] - high.astype(FULL)).astype(LOW), many)
    own_head = lax.broadcasted_iota(jnp.int32, (16, 512), 1) // NB == lax.broadcasted_iota(jnp.int32, (16, 512), 0)
    extra[3:4, :512] = jnp.sum(jnp.where(own_head, sums, 0.0), axis=0, keepdims=True)
    input_grad[...] = input_grad[...] + step
    hops = ((everyone[4],), (everyone[3],), everyone[:3], (sibling,))
    boxes, shown_rows = 0, []
    for hop, targets in enumerate(hops):
        waits = [post.copy(extra, extra_box.at[boxes + k], target) for k, target in enumerate(targets)]
        comm.pump(2)
        if hop < 4:
            value = dot_last(
                whole(own_long[0, hop, 0], other_long[0, hop]), weight(pool_a, 2)
            ) + dot_last(whole(own_long[1, hop, 0], other_long[1, hop]), weight(pool_a, 3))
            if hop >= 2:
                shown_rows[hop - 2].wait()
            rows_out[hop % 2] = value
            shown_rows.append(fetch(rows_out.at[hop % 2], memory_grad.at[pl.ds(hop * ROWS, ROWS)]))
        comm.pump(1)
        arrived(waits)
        total = extra[...]
        for k in range(len(targets)):
            total = total + extra_box[boxes + k]
        for made in waits:
            made.wait_send()
            post.started = [left for left in post.started if left is not made]
        extra[...] = total
        boxes += len(targets)
    while comm.queue:
        comm.pump(1)
    for made in shown_rows[2:]:
        made.wait()
    post.finish()


def backward_call(*args):
    kind = jax.ShapeDtypeStruct
    anywhere, vmem = pl.BlockSpec(memory_space=pl.ANY), pl.BlockSpec(memory_space=pltpu.VMEM)
    smem = pl.BlockSpec(memory_space=pltpu.SMEM)
    vm, dma = pltpu.VMEM, pltpu.SemaphoreType.DMA
    return pl.pallas_call(
        backward_kernel,
        out_shape=(
            kind((256, 768), LOW),
            kind((256, 768), FULL),
            kind((1024, 768), FULL),
            kind((12, 24, 768), FULL),
            kind((96, 768), FULL),
            kind((8, 768), FULL),
        ),
        in_specs=[anywhere] * 11 + [vmem] * 7 + [smem] * 2,
        out_specs=(vmem, vmem, anywhere, vmem, vmem, vmem),
        scratch_shapes=[
            vm((128, 24, 768), LOW),
            vm((128, 24, 768), LOW),
            vm((4, 768, 512), LOW),
            vm((3, 768, 512), LOW),
            vm((4, 256, 768), LOW),
            vm((4, 256, 768), LOW),
            vm((2, 256, 768), FULL),
            vm((11, 2, 256, HALF), LOW),
            vm((11, 256, HALF), LOW),
            vm((2, 4, 2, 256, HALF), LOW),
            vm((2, 4, 256, HALF), LOW),
            vm((16, 256), FULL),
            vm((16, 256), FULL),
            vm((16, 256), FULL),
            vm((12, 4, 2, 2, 2, 24, HALF), LOW),
            vm((4, 2, 2, 2, 96, HALF), LOW),
            vm((12, 4, 2, 2, 24, HALF), LOW),
            vm((4, 2, 2, 96, HALF), LOW),
            vm((12, 4, 2, 24, HALF), LOW),
            vm((4, 2, 96, HALF), LOW),
            vm((12, 3, 2, 24, HALF), LOW),
            vm((3, 2, 96, HALF), LOW),
            vm((len(Z_FIRST), 3, 2, 2, 2, 24, HALF), LOW),
            vm((12, 24, HALF), FULL),
            vm((96, HALF), FULL),
            vm((256, 768), FULL),
            vm((6, 8, 768), FULL),
            vm((256, 768), LOW),
            dma((60,)),
            dma((150,)),
            dma((150,)),
        ],
        compiler_params=pltpu.CompilerParams(
            collective_id=1, has_side_effects=True, vmem_limit_bytes=60 * 2**20
        ),
    )(*args)


def finish_kernel(*refs):
    (output, input_grad, memory_grad, mats, down), outs = refs[:5], refs[5:]
    for source, target in zip((output, input_grad, memory_grad, down), outs):
        target[...] = source[...]
    for index in range(8):
        outs[4 + index][...] = mats[index]
    for index in range(4):
        outs[12][:, index * 768 : (index + 1) * 768] = mats[8 + index]


def finish(*args):
    kind = jax.ShapeDtypeStruct
    block = lambda *shape: pl.BlockSpec(shape, lambda step: (step, 0))
    whole = lambda *shape: pl.BlockSpec(shape, lambda step: (0,) * len(shape))
    rows = [block(64, 768), block(64, 768), block(256, 768)]
    return pl.pallas_call(
        finish_kernel,
        grid=(4,),
        out_shape=(
            kind((256, 768), LOW),
            kind((256, 768), FULL),
            kind((1024, 768), FULL),
            kind((96, 768), FULL),
            *[kind((24, 768), FULL)] * 8,
            kind((24, 3072), FULL),
        ),
        in_specs=rows + [whole(12, 24, 768), whole(96, 768)],
        out_specs=rows + [whole(96, 768)] + [whole(24, 768)] * 8 + [whole(24, 3072)],
    )(*args)


def plain_body(
    tokens,
    memory,
    cotangent,
    target_lengths,
    memory_lengths,
    self_gain,
    self_query,
    self_key,
    self_value,
    self_out,
    position_table,
    cross_gain,
    cross_query,
    cross_key,
    cross_value,
    cross_out,
    ffn_gain,
    ffn_in,
    ffn_out,
):
    wide_count = lax.axis_size(AXES[0])
    narrow_count = lax.axis_size(AXES[1])
    devices = wide_count * narrow_count
    seq_count = target_lengths.shape[0]
    target_rows = tokens.shape[0] // seq_count
    memory_rows = memory.shape[0] // seq_count
    positions = jnp.arange(target_rows, dtype=jnp.int32)
    live_rows = positions[None, :] < target_lengths[:, None]
    causal = positions[None, :] <= positions[:, None]
    self_visible = causal[None] & live_rows[:, None, :]
    memory_visible = (jnp.arange(memory_rows, dtype=jnp.int32)[None, :] < memory_lengths[:, None])[
        :, None, :
    ]
    grad_out = jnp.where(live_rows.reshape(-1, 1), cotangent.astype(jnp.float32), 0.0)
    bucket = bucket_index(target_rows)
    one_hot = (bucket[:, :, None] == jnp.arange(NB, dtype=jnp.int32)[None, None, :]).astype(
        jnp.float32
    )
    relative = jnp.einsum(
        "ijb,bh->hij", one_hot, position_table.astype(jnp.float32), precision=lax.Precision.HIGHEST
    )
    gain_one, weight_query, weight_key, weight_value, weight_out = (
        lax.all_gather(self_gain, AXES, axis=0, tiled=True),
        lax.all_gather(self_query, AXES, axis=0, tiled=True),
        lax.all_gather(self_key, AXES, axis=0, tiled=True),
        lax.all_gather(self_value, AXES, axis=0, tiled=True),
        lax.all_gather(self_out, AXES, axis=0, tiled=True),
    )
    source = tokens.astype(jnp.float32)
    normed_value, norm_back_one = jax.vjp(rms_apply, source, gain_one.astype(jnp.float32))
    normed_one = normed_value.astype(jnp.bfloat16)
    query_one = product(normed_one, weight_query).astype(jnp.bfloat16)
    keys_one = product(normed_one, weight_key).astype(jnp.bfloat16)
    values_one = product(normed_one, weight_value).astype(jnp.bfloat16)
    context_one, totals_one = attend_forward(
        query_one, keys_one, values_one, relative, self_visible, seq_count
    )
    after_self = source + product(context_one, weight_out)
    gain_two, cross_weight_query, cross_weight_key, cross_weight_value, cross_weight_out = (
        lax.all_gather(cross_gain, AXES, axis=0, tiled=True),
        lax.all_gather(cross_query, AXES, axis=0, tiled=True),
        lax.all_gather(cross_key, AXES, axis=0, tiled=True),
        lax.all_gather(cross_value, AXES, axis=0, tiled=True),
        lax.all_gather(cross_out, AXES, axis=0, tiled=True),
    )
    normed_value, norm_back_two = jax.vjp(rms_apply, after_self, gain_two.astype(jnp.float32))
    normed_two = normed_value.astype(jnp.bfloat16)
    query_two = product(normed_two, cross_weight_query).astype(jnp.bfloat16)
    keys_two = product(memory, cross_weight_key).astype(jnp.bfloat16)
    values_two = product(memory, cross_weight_value).astype(jnp.bfloat16)
    context_two, totals_two = attend_forward(
        query_two, keys_two, values_two, None, memory_visible, seq_count
    )
    after_cross = after_self + product(context_two, cross_weight_out)
    gain_three, weight_in, weight_down = (
        lax.all_gather(ffn_gain, AXES, axis=0, tiled=True),
        lax.all_gather(ffn_in, AXES, axis=0, tiled=True),
        lax.all_gather(ffn_out, AXES, axis=0, tiled=True),
    )
    normed_value, norm_back_three = jax.vjp(rms_apply, after_cross, gain_three.astype(jnp.float32))
    normed_three = normed_value.astype(jnp.bfloat16)
    before = product(normed_three, weight_in)
    gelu_value, gelu_back = jax.vjp(gelu_smooth, before)
    hidden = gelu_value.astype(jnp.bfloat16)
    output = (after_cross + product(hidden, weight_down)).astype(jnp.bfloat16)
    back_in, back_down = (
        lax.all_gather(ffn_in, AXES, axis=0, tiled=True),
        lax.all_gather(ffn_out, AXES, axis=0, tiled=True),
    )
    grad_low = grad_out.astype(jnp.bfloat16)
    grad_down_weight = outer_sum(hidden, grad_low)
    grad_hidden = back_project(grad_low, back_down)
    grad_before = gelu_back(grad_hidden)[0].astype(jnp.bfloat16)
    grad_in_weight = outer_sum(normed_three, grad_before)
    grad_normed_three = back_project(grad_before, back_in)
    grad_cross_part, grad_gain_three = norm_back_three(grad_normed_three)
    grad_cross = grad_out + grad_cross_part
    ffn_terms = (grad_gain_three, grad_in_weight, grad_down_weight)
    summed_ffn = lax.psum_scatter(
        pack_rows(ffn_terms, devices), AXES, scatter_dimension=0, tiled=True
    )
    ffn_gain_grad, ffn_in_grad, ffn_out_grad = unpack_rows(summed_ffn[0], ffn_terms, devices)
    back_cross_query, back_cross_key, back_cross_value, back_cross_out = (
        lax.all_gather(cross_query, AXES, axis=0, tiled=True),
        lax.all_gather(cross_key, AXES, axis=0, tiled=True),
        lax.all_gather(cross_value, AXES, axis=0, tiled=True),
        lax.all_gather(cross_out, AXES, axis=0, tiled=True),
    )
    grad_cross_low = grad_cross.astype(jnp.bfloat16)
    grad_cross_out_weight = outer_sum(context_two, grad_cross_low)
    grad_context_two = back_project(grad_cross_low, back_cross_out).astype(jnp.bfloat16)
    grad_query_two, grad_keys_two, grad_values_two, unused_extra = attend_backward(
        query_two,
        keys_two,
        values_two,
        None,
        memory_visible,
        seq_count,
        totals_two,
        grad_context_two,
    )
    grad_cross_query_weight = outer_sum(normed_two, grad_query_two)
    grad_cross_key_weight = outer_sum(memory, grad_keys_two)
    grad_cross_value_weight = outer_sum(memory, grad_values_two)
    memory_grad = back_project(grad_keys_two, back_cross_key) + back_project(
        grad_values_two, back_cross_value
    )
    grad_self_part, grad_gain_two = norm_back_two(back_project(grad_query_two, back_cross_query))
    grad_self = grad_cross + grad_self_part
    cross_terms = (
        grad_gain_two,
        grad_cross_query_weight,
        grad_cross_key_weight,
        grad_cross_value_weight,
        grad_cross_out_weight,
    )
    summed_cross = lax.psum_scatter(
        pack_rows(cross_terms, devices), AXES, scatter_dimension=0, tiled=True
    )
    cross_gain_grad, cross_query_grad, cross_key_grad, cross_value_grad, cross_out_grad = (
        unpack_rows(summed_cross[0], cross_terms, devices)
    )
    back_query, back_key, back_value, back_out = (
        lax.all_gather(self_query, AXES, axis=0, tiled=True),
        lax.all_gather(self_key, AXES, axis=0, tiled=True),
        lax.all_gather(self_value, AXES, axis=0, tiled=True),
        lax.all_gather(self_out, AXES, axis=0, tiled=True),
    )
    grad_self_low = grad_self.astype(jnp.bfloat16)
    grad_out_weight = outer_sum(context_one, grad_self_low)
    grad_context_one = back_project(grad_self_low, back_out).astype(jnp.bfloat16)
    grad_query_one, grad_keys_one, grad_values_one, grad_relative = attend_backward(
        query_one,
        keys_one,
        values_one,
        relative,
        self_visible,
        seq_count,
        totals_one,
        grad_context_one,
    )
    table_term = jnp.einsum("hij,ijb->bh", grad_relative, one_hot, precision=lax.Precision.HIGHEST)
    position_table_grad = lax.psum(table_term, AXES)
    grad_query_weight = outer_sum(normed_one, grad_query_one)
    grad_key_weight = outer_sum(normed_one, grad_keys_one)
    grad_value_weight = outer_sum(normed_one, grad_values_one)
    grad_normed_one = (
        back_project(grad_query_one, back_query)
        + back_project(grad_keys_one, back_key)
        + back_project(grad_values_one, back_value)
    )
    grad_source_part, grad_gain_one = norm_back_one(grad_normed_one)
    input_grad = grad_self + grad_source_part
    self_terms = (
        grad_gain_one,
        grad_query_weight,
        grad_key_weight,
        grad_value_weight,
        grad_out_weight,
    )
    summed_self = lax.psum_scatter(
        pack_rows(self_terms, devices), AXES, scatter_dimension=0, tiled=True
    )
    self_gain_grad, self_query_grad, self_key_grad, self_value_grad, self_out_grad = unpack_rows(
        summed_self[0], self_terms, devices
    )
    return (
        output,
        input_grad,
        memory_grad,
        self_gain_grad,
        self_query_grad,
        self_key_grad,
        self_value_grad,
        self_out_grad,
        position_table_grad,
        cross_gain_grad,
        cross_query_grad,
        cross_key_grad,
        cross_value_grad,
        cross_out_grad,
        ffn_gain_grad,
        ffn_in_grad,
        ffn_out_grad,
    )


def body(
    tokens,
    memory,
    cotangent,
    target_lengths,
    memory_lengths,
    self_gain,
    self_query,
    self_key,
    self_value,
    self_out,
    position_table,
    cross_gain,
    cross_query,
    cross_key,
    cross_value,
    cross_out,
    ffn_gain,
    ffn_in,
    ffn_out,
):
    rank = lax.axis_index(AXES[0]) * lax.axis_size(AXES[1]) + lax.axis_index(AXES[1])
    own_gains = jnp.stack([self_gain, cross_gain, ffn_gain])
    spread = lax.dynamic_update_slice(jnp.zeros((8, 768), LOW), own_gains, (0, rank * 24))
    shards = (self_query, self_key, self_value, self_out, cross_query, cross_key, cross_value, cross_out, ffn_in, ffn_out)
    (
        mats,
        down,
        gains,
        turned,
        memory_turned,
        small,
        keys,
        values,
        after_self,
        after_cross,
        hidden,
        slope,
        down_grads,
        self_log,
        cross_log,
    ) = forward_call(
        shards + (spread,), tokens, memory, cotangent, position_table, target_lengths, memory_lengths
    )
    output, input_grad, memory_grad, mats_grad, down_grad, extra = backward_call(
        mats.reshape(384, 24, 768),
        down.reshape(128, 24, 768),
        turned,
        memory_turned,
        down_grads,
        keys,
        values,
        hidden,
        slope,
        after_self,
        after_cross,
        gains,
        small,
        tokens,
        cotangent,
        position_table,
        self_log,
        cross_log,
        target_lengths,
        memory_lengths,
    )
    output, input_grad, memory_grad, down_grad, *square_grads, ffn_in_grad = finish(
        output, input_grad, memory_grad, mats_grad, down_grad
    )
    own = lax.dynamic_slice(extra, (0, rank * 24), (3, 24))
    return (
        output,
        input_grad,
        memory_grad,
        own[0],
        *square_grads[:4],
        extra[3, : 12 * NB].reshape(12, NB).T,
        own[1],
        *square_grads[4:],
        own[2],
        ffn_in_grad,
        down_grad,
    )


def solution(mesh):
    whole = (mesh.shape[AXES[0]], mesh.shape[AXES[1]]) == (8, 4)
    placed = (
        P(AXES, None),
        P(AXES, None),
        P(AXES, None),
        P(AXES),
        P(AXES),
        P(AXES),
        P(AXES, None),
        P(AXES, None),
        P(AXES, None),
        P(AXES, None),
        P(),
        P(AXES),
        P(AXES, None),
        P(AXES, None),
        P(AXES, None),
        P(AXES, None),
        P(AXES),
        P(AXES, None),
        P(AXES, None),
    )
    return jax.shard_map(
        body if whole else plain_body,
        mesh=mesh,
        in_specs=placed,
        out_specs=(
            P(AXES, None),
            P(AXES, None),
            P(AXES, None),
            P(AXES),
            P(AXES, None),
            P(AXES, None),
            P(AXES, None),
            P(AXES, None),
            P(),
            P(AXES),
            P(AXES, None),
            P(AXES, None),
            P(AXES, None),
            P(AXES, None),
            P(AXES),
            P(AXES, None),
            P(AXES, None),
        ),
        check_vma=False,
    )
```

```python
import math

import jax
import jax.numpy as jnp
from jax import lax
from jax.experimental import pallas as pl
from jax.experimental.pallas import tpu as pltpu
from jax.sharding import PartitionSpec as P

DH = 64
NB = 32
MAXDIST = 128


AXES = ("wide", "narrow")
EPSILON = 1e-06
NEGATIVE = -1e30


def bucket_index(length):
    offsets = jnp.arange(length, dtype=jnp.int32)
    distance = jnp.maximum(offsets[:, None] - offsets[None, :], 0)
    exact_part = NB // 2
    bucket = jnp.minimum(distance, exact_part)
    for step in range(1, NB - exact_part):
        bound = math.ceil(exact_part * (MAXDIST / exact_part) ** (step / (NB - exact_part)))
        bucket = bucket + (distance >= bound).astype(jnp.int32)
    return bucket


def rms_apply(field, gain):
    inverse = lax.rsqrt(jnp.mean(field * field, axis=-1, keepdims=True) + EPSILON)
    return field * inverse * gain


def gelu_smooth(field):
    return jax.nn.gelu(field, approximate=True)


def product(left, right):
    return jnp.dot(left, right, preferred_element_type=jnp.float32)


def outer_sum(left, right):
    return jnp.einsum("rd,re->de", left, right, preferred_element_type=jnp.float32)


def back_project(left, right):
    return jnp.einsum("re,de->rd", left, right, preferred_element_type=jnp.float32)


def pack_rows(arrays, devices):
    return jnp.concatenate([array.reshape(devices, -1) for array in arrays], axis=1)


def unpack_rows(packed_row, arrays, devices):
    results = []
    offset = 0
    for array in arrays:
        shard_shape = (array.shape[0] // devices,) + array.shape[1:]
        count = array.size // devices
        results.append(packed_row[offset : offset + count].reshape(shard_shape))
        offset = offset + count
    return tuple(results)


def head_blocks(array, index, seq_count):
    block = lax.dynamic_slice_in_dim(array, index * 2 * DH, 2 * DH, 1)
    return block.reshape(seq_count, -1, 2, DH)


def flat_block(block):
    return block.reshape(-1, 2 * DH)


def scored(query_block, keys_block, extra, visible, index):
    scores = jnp.einsum(
        "sqhd,skhd->shqk", query_block, keys_block, preferred_element_type=jnp.float32
    ) * DH ** (-0.5)
    if extra is not None:
        scores = scores + lax.dynamic_slice_in_dim(extra, index * 2, 2, 0)[None]
    return jnp.where(visible[:, None], scores, NEGATIVE)


def attend_forward(query, keys, values, extra, visible, seq_count):
    pairs = query.shape[1] // (2 * DH)
    start_context = jnp.zeros(query.shape, jnp.bfloat16)
    start_totals = jnp.zeros((seq_count, 2 * pairs, query.shape[0] // seq_count), jnp.float32)

    def one_pair(index, carry):
        context, log_total = carry
        query_block = head_blocks(query, index, seq_count)
        scores = scored(query_block, head_blocks(keys, index, seq_count), extra, visible, index)
        peak = jnp.max(scores, axis=-1, keepdims=True)
        raised = jnp.exp(scores - peak)
        total = jnp.sum(raised, axis=-1, keepdims=True)
        attend = (raised / total).astype(jnp.bfloat16)
        mixed = jnp.einsum(
            "shqk,skhd->sqhd",
            attend,
            head_blocks(values, index, seq_count),
            preferred_element_type=jnp.float32,
        )
        context = lax.dynamic_update_slice_in_dim(
            context, flat_block(mixed.astype(jnp.bfloat16)), index * 2 * DH, 1
        )
        log_total = lax.dynamic_update_slice_in_dim(
            log_total, (peak + jnp.log(total))[..., 0], index * 2, 1
        )
        return (context, log_total)

    return lax.fori_loop(0, pairs, one_pair, (start_context, start_totals))


def attend_backward(query, keys, values, extra, visible, seq_count, log_total, grad_context):
    pairs = query.shape[1] // (2 * DH)
    scale = DH ** (-0.5)
    extra_shape = extra.shape if extra is not None else (1,)
    start_grads = (
        jnp.zeros(query.shape, jnp.bfloat16),
        jnp.zeros(keys.shape, jnp.bfloat16),
        jnp.zeros(values.shape, jnp.bfloat16),
        jnp.zeros(extra_shape, jnp.float32),
    )

    def one_pair(index, carry):
        grad_query, grad_keys, grad_values, grad_extra = carry
        query_block = head_blocks(query, index, seq_count)
        keys_block = head_blocks(keys, index, seq_count)
        value_block = head_blocks(values, index, seq_count)
        upstream = head_blocks(grad_context, index, seq_count)
        scores = scored(query_block, keys_block, extra, visible, index)
        attend = jnp.exp(scores - lax.dynamic_slice_in_dim(log_total, index * 2, 2, 1)[..., None])
        grad_attend = jnp.einsum(
            "sqhd,skhd->shqk", upstream, value_block, preferred_element_type=jnp.float32
        )
        value_grad = jnp.einsum(
            "shqk,sqhd->skhd",
            attend.astype(jnp.bfloat16),
            upstream,
            preferred_element_type=jnp.float32,
        ).astype(jnp.bfloat16)
        inner = jnp.sum(attend * grad_attend, axis=-1, keepdims=True)
        grad_score = attend * (grad_attend - inner)
        rounded = grad_score.astype(jnp.bfloat16)
        query_grad = (
            jnp.einsum("shqk,skhd->sqhd", rounded, keys_block, preferred_element_type=jnp.float32)
            * scale
        ).astype(jnp.bfloat16)
        keys_grad = (
            jnp.einsum("shqk,sqhd->skhd", rounded, query_block, preferred_element_type=jnp.float32)
            * scale
        ).astype(jnp.bfloat16)
        offset = index * 2 * DH
        grad_query = lax.dynamic_update_slice_in_dim(grad_query, flat_block(query_grad), offset, 1)
        grad_keys = lax.dynamic_update_slice_in_dim(grad_keys, flat_block(keys_grad), offset, 1)
        grad_values = lax.dynamic_update_slice_in_dim(
            grad_values, flat_block(value_grad), offset, 1
        )
        if extra is not None:
            grad_extra = lax.dynamic_update_slice_in_dim(
                grad_extra, jnp.sum(grad_score, axis=0), index * 2, 0
            )
        return (grad_query, grad_keys, grad_values, grad_extra)

    return lax.fori_loop(0, pairs, one_pair, start_grads)


MESH = pl.DeviceIdType.MESH
HALF = 384
ROWS = 256
LOW, FULL = jnp.bfloat16, jnp.float32
EVERY = slice(None)


def place():
    wide = lax.axis_index(AXES[0])
    narrow = lax.axis_index(AXES[1])
    return wide // 2, lax.rem(wide, 2), narrow // 2, lax.rem(narrow, 2)


def device(z, x, y, c):
    return (z * 2 + x, y * 2 + c)


def partners(z, x, y, c):
    return (
        device(z ^ 1, x, y, c),
        device(z ^ 2, x, y, c),
        device(z ^ 3, x, y, c),
        device(z, 1 - x, y, c),
        device(z, x, 1 - y, c),
        device(z, x, y, 1 - c),
    )


def enter(everyone):
    barrier = pltpu.get_barrier_semaphore()
    for other in everyone:
        pl.semaphore_signal(barrier, inc=1, device_id=other, device_id_type=MESH)
    pl.semaphore_wait(barrier, len(everyone))


class Post:
    def __init__(self, send, recv, near):
        self.send, self.recv, self.near = send, recv, near
        self.used, self.used_near, self.started, self.open = 0, 0, [], []

    def copy(self, source, target, where):
        made = pltpu.make_async_remote_copy(
            src_ref=source,
            dst_ref=target,
            send_sem=self.send.at[self.used],
            recv_sem=self.recv.at[self.used],
            device_id=where,
            device_id_type=MESH,
        )
        self.used += 1
        made.start()
        self.started.append(made)
        return made

    def local(self, source, target, keep=False):
        made = pltpu.make_async_copy(source, target, self.near.at[self.used_near])
        self.used_near += 1
        made.start()
        if not keep:
            self.open.append(made)
        return made

    def finish(self):
        for made in self.started:
            made.wait_send()
        for made in self.open:
            made.wait()


def arrived(copies):
    for made in copies:
        made.wait_recv()


def dot(left, right):
    return jnp.dot(left, right, preferred_element_type=FULL)


def dot_last(left, right):
    return lax.dot_general(left, right, (((1,), (1,)), ((), ())), preferred_element_type=FULL)


def dot_first(left, right):
    return lax.dot_general(left, right, (((0,), (0,)), ((), ())), preferred_element_type=FULL)


def square(ref, index):
    return ref[index].reshape(768, 768)


def bucket_rows():
    distance = lax.broadcasted_iota(jnp.int32, (NB, ROWS), 1)
    row = lax.broadcasted_iota(jnp.int32, (NB, ROWS), 0)
    exact_part = NB // 2
    bucket = jnp.minimum(distance, exact_part)
    for step in range(1, NB - exact_part):
        bound = math.ceil(exact_part * (MAXDIST / exact_part) ** (step / (NB - exact_part)))
        bucket = bucket + (distance >= bound).astype(jnp.int32)
    return (bucket == row).astype(LOW)


def self_mask(length):
    key = lax.broadcasted_iota(jnp.int32, (ROWS, ROWS), 0)
    query = lax.broadcasted_iota(jnp.int32, (ROWS, ROWS), 1)
    return jnp.where((key <= query) & (key < length), 0.0, NEGATIVE)


def memory_mask(length, rows):
    key = lax.broadcasted_iota(jnp.int32, (rows, 1), 0)
    return jnp.where(key < length, 0.0, NEGATIVE)


def slanted(row):
    return pltpu.roll(jnp.broadcast_to(row, (ROWS, ROWS)), 0, 1, stride=1, stride_axis=0)


def one_head(block, head):
    lane = lax.broadcasted_iota(jnp.int32, block.shape, 1)
    return jnp.where((lane < DH) if head == 0 else (lane >= DH), block, jnp.zeros_like(block))


def inverse_rms(field):
    return lax.rsqrt(jnp.mean(field * field, axis=-1, keepdims=True) + EPSILON)


PAIRS = [("gains", 0, 1), (2, 3), (4, 7), (5, 6), (8, 9), (10, 11), ((0, 0), (0, 1))]
LATE = ((1, 0), (1, 1))
ORDERS = {"gains": "zxy", (0, 0): "zxy", (0, 1): "zyx", (1, 0): "xyz", (1, 1): "yxz"}
for _pair in PAIRS[:-1]:
    for _unit, _order in zip(_pair[-2:], ("zxy", "zyx")):
        ORDERS[_unit] = _order


def forward_schedule(ahead=5):
    events = [(unit, 0) for unit in PAIRS[0]] + [(unit, 0) for unit in LATE]
    for pair in PAIRS[1:ahead]:
        events += [(unit, 0) for unit in pair]
    count = len(PAIRS)
    for step in range(count + 4):
        for stage in (1, 0, None, 2, 3, 4):
            if stage is None:
                if step in (0, 2):
                    events += [(unit, 1 + step // 2) for unit in LATE]
                continue
            index = step + ahead if stage == 0 else step - stage + 1
            if (stage > 0 or index >= ahead) and 0 <= index < count:
                events += [(unit, stage) for unit in PAIRS[index]]
    return events + [(unit, stage) for stage in (3, 4) for unit in LATE]


class Gather:
    def __init__(self, post, mats, down, gains, kept, spot, everyone):
        self.post, self.mats, self.down, self.gains, self.kept = post, mats, down, gains, kept
        self.spot, self.everyone = spot, everyone
        self.events = forward_schedule()
        self.waits, self.near, self.ready = {}, {}, set()

    def at(self, unit, *where):
        if unit == "gains":
            return self.gains.at[where]
        if isinstance(unit, tuple):
            return self.down.at[where + (pl.ds(unit[0] * 48, 48), pl.ds(unit[1] * HALF, HALF))]
        return self.mats.at[(unit,) + where]

    def forward(self, unit, where, targets):
        return [self.post.copy(self.at(unit, *where), self.at(unit, *where), target) for target in targets]

    def run(self, unit, stage):
        z, x, y, c = self.spot
        across, along, sibling = self.everyone[3:]
        order = ORDERS[unit]
        if stage == 0:
            targets = {"z": self.everyone[:3], "x": (across,), "y": (along,)}[order[0]]
            self.near[unit] = []
            self.waits[unit] = self.forward(unit, self.spot, targets)
            return
        if stage == 4:
            arrived(self.near[unit])
            self.ready.add(unit)
            if isinstance(unit, int):
                self.post.local(self.mats.at[unit], self.kept[0].at[unit])
            if unit in ((0, 1), (1, 1)):
                rows = (EVERY,) * 4 + (pl.ds(unit[0] * 48, 48),)
                self.post.local(self.down.at[rows], self.kept[1].at[rows])
            return
        arrived(self.waits[unit])
        steps = {
            "zxy": (
                ((EVERY, x, y, c), (across,), (EVERY, x, y, c)),
                ((EVERY, EVERY, y, c), (along,), (EVERY, 1 - x, y, c)),
                (None, (), (EVERY, EVERY, 1 - y, c)),
            ),
            "zyx": (
                ((EVERY, x, y, c), (along,), (EVERY, x, y, c)),
                ((EVERY, x, EVERY, c), (across,), (EVERY, x, 1 - y, c)),
                (None, (), (EVERY, 1 - x, EVERY, c)),
            ),
            "xyz": (
                ((z, EVERY, y, c), (along,), None),
                ((z, EVERY, EVERY, c), self.everyone[:3], (z, EVERY, EVERY, c)),
                (None, (), "others"),
            ),
            "yxz": (
                ((z, x, EVERY, c), (across,), None),
                ((z, EVERY, EVERY, c), self.everyone[:3], (z, EVERY, EVERY, c)),
                (None, (), "others"),
            ),
        }
        where, targets, near = steps[order][stage - 1]
        self.waits[unit] = self.forward(unit, where, targets) if targets else []
        if near == "others":
            for k in range(3):
                self.near[unit] += self.forward(unit, (z ^ (k + 1), EVERY, EVERY, c), (sibling,))
        elif near is not None:
            self.near[unit] += self.forward(unit, near, (sibling,))

    def pump(self, count):
        for _ in range(count):
            if self.events:
                self.run(*self.events.pop(0))

    def require(self, *units):
        for unit in units:
            while unit not in self.ready:
                self.pump(1)


def forward_kernel(*refs):
    shards, (tokens, memory, cotangent, table, lengths, memory_lengths) = refs[:11], refs[11:17]
    kept_mats, kept_down, gain_rows = refs[17:20]
    (turned, memory_turned, small, keys_out, values_out, self_out, cross_out, hidden_out, slope_out, grads_out) = refs[20:30]
    self_log, cross_log = refs[30:32]
    (gains, mats, down, keep, keys, values, stage, memory_stage, hidden, slope) = refs[32:42]
    (hidden_turned, after_self, after_cross, own_cut, other_cut, grads, near, send, recv) = refs[42:]
    spot = place()
    everyone = partners(*spot)
    sibling = everyone[5]
    post = Post(send, recv, near)
    comm = Gather(post, mats, down, gains, (kept_mats, kept_down), spot, everyone)
    for index in range(8):
        mats.at[(index,) + spot][...] = shards[index][...]
    for index in range(4):
        mats.at[(8 + index,) + spot][...] = shards[8][:, index * 768 : (index + 1) * 768]
    down.at[spot][...] = shards[9][...]
    gains.at[spot][...] = shards[10][...]
    enter(everyone)
    comm.pump(9)
    from_sibling = []

    def turn(block, staged, target, lanes=ROWS):
        staged[...] = block.T
        post.local(staged, target.at[:, pl.ds(0, lanes)])
        from_sibling.append(post.copy(staged, target.at[:, pl.ds(lanes, lanes)], sibling))

    for block in range(4):
        turn(memory[block * ROWS : (block + 1) * ROWS], memory_stage.at[block], memory_turned.at[block])
        comm.pump(1)
    live = lax.broadcasted_iota(jnp.int32, (ROWS, 1), 0) < lengths[0]
    grad_low = jnp.where(live, cotangent[...], jnp.zeros_like(cotangent[...]))
    left, right = grad_low[:, :HALF], grad_low[:, HALF:]
    core = spot[3]
    own_cut[0] = jnp.where(core == 0, left, right)
    other_cut[...] = jnp.where(core == 0, right, left)
    from_sibling.append(post.copy(other_cut, own_cut.at[1], sibling))
    source = tokens[...].astype(FULL)
    inverse = inverse_rms(source)
    one_hot = bucket_rows()
    bias = dot(table[...], one_hot)
    visible = self_mask(lengths[0])
    comm.require("gains")
    gain_rows[...] = jnp.sum(gains[...].astype(FULL).reshape(32, 8, 768), axis=0)
    normed = (source * inverse * gain_rows[0:1]).astype(LOW)
    turn(normed, stage.at[0], turned.at[0])

    def project(unit, slot, block):
        comm.require(unit)
        keep[slot] = dot(block, square(mats, unit)).astype(LOW)
        post.local(keep.at[slot], small.at[slot])

    project(0, 0, normed)
    project(1, 1, normed)
    project(2, 2, normed)

    def attend(pair, head, query, key_block, value_block, extra, log_ref):
        scores = dot_last(key_block, one_head(query, head)) + extra
        peak = jnp.max(scores, axis=0, keepdims=True)
        raised = jnp.exp(scores - peak)
        total = jnp.sum(raised, axis=0, keepdims=True)
        mixed = dot_first(value_block, raised.astype(LOW)) / total
        log_ref[pair * 2 + head : pair * 2 + head + 1] = peak + jnp.log(total)
        return mixed[head * DH : head * DH + DH]

    for pair in range(6):
        span = slice(pair * 128, pair * 128 + 128)
        query = keep[0, :, span] * 0.125
        mixed = [
            attend(
                pair,
                head,
                query,
                keep[1, :, span],
                keep[2, :, span],
                slanted(bias[pair * 2 + head : pair * 2 + head + 1]) + visible,
                self_log,
            )
            for head in range(2)
        ]
        keep[3, :, span] = jnp.concatenate(mixed, axis=0).T.astype(LOW)
        comm.pump(2)
    post.local(keep.at[3], small.at[3])
    context = keep[3]
    turn(context, stage.at[1], turned.at[1])
    comm.require(3)
    after_self[...] = source + dot(context, square(mats, 3))
    post.local(after_self, self_out)
    normed = (after_self[...] * inverse_rms(after_self[...]) * gain_rows[1:2]).astype(LOW)
    turn(normed, stage.at[2], turned.at[2])
    project(4, 4, normed)
    for unit, held, out in ((5, keys, keys_out), (6, values, values_out)):
        comm.require(unit)
        for block in range(4):
            held[block] = dot(memory[block * ROWS : (block + 1) * ROWS], square(mats, unit)).astype(LOW)
            comm.pump(1)
        post.local(held, out)
    shown = memory_mask(memory_lengths[0], 1024)
    for pair in range(6):
        span = slice(pair * 128, pair * 128 + 128)
        query = keep[4, :, span] * 0.125
        mixed = [
            attend(pair, head, query, keys[:, :, span].reshape(1024, 128), values[:, :, span].reshape(1024, 128), shown, cross_log) for head in range(2)
        ]
        keep[5, :, span] = jnp.concatenate(mixed, axis=0).T.astype(LOW)
        comm.pump(2)
    post.local(keep.at[5], small.at[5])
    context = keep[5]
    turn(context, stage.at[3], turned.at[3])
    comm.require(7)
    after_cross[...] = after_self[...] + dot(context, square(mats, 7))
    post.local(after_cross, cross_out)
    normed = (after_cross[...] * inverse_rms(after_cross[...]) * gain_rows[2:3]).astype(LOW)
    turn(normed, stage.at[4], turned.at[4])
    root = math.sqrt(2.0 / math.pi)
    for block in range(4):
        comm.require(8 + block)
        before = dot(normed, square(mats, 8 + block))
        squared = before * before
        bent = jnp.tanh(root * before * (1.0 + 0.044715 * squared))
        lifted = 0.5 * (1.0 + bent)
        value = (before * lifted).astype(LOW)
        hidden[block] = value
        slope[block] = (
            lifted + 0.5 * root * before * (1.0 - bent * bent) * (1.0 + 3 * 0.044715 * squared)
        ).astype(LOW)
        post.local(hidden.at[block], hidden_out.at[block])
        post.local(slope.at[block], slope_out.at[block])
        hidden_turned[block, :, :ROWS] = value.T
        half = hidden_turned.at[block, :, pl.ds(0, ROWS)]
        from_sibling.append(post.copy(half, hidden_turned.at[block, :, pl.ds(ROWS, ROWS)], sibling))
        comm.pump(1)
    arrived(from_sibling)
    for block in range(4):
        comm.pump(1)
        grads[block] = dot(hidden_turned[block], own_cut[...].reshape(512, HALF)).astype(LOW).reshape(2, 2, 2, 96, HALF)
        post.local(grads.at[block], grads_out.at[block])
    while comm.events:
        comm.pump(1)
    post.finish()


def forward_call(shards, *rest):
    kind = jax.ShapeDtypeStruct
    anywhere, vmem = pl.BlockSpec(memory_space=pl.ANY), pl.BlockSpec(memory_space=pltpu.VMEM)
    smem = pl.BlockSpec(memory_space=pltpu.SMEM)
    outs = (
        (kind((12, 4, 2, 2, 2, 24, 768), LOW), anywhere),
        (kind((4, 2, 2, 2, 96, 768), LOW), anywhere),
        (kind((8, 768), FULL), vmem),
        (kind((5, 768, 512), LOW), anywhere),
        (kind((4, 768, 512), LOW), anywhere),
        (kind((6, 256, 768), LOW), anywhere),
        (kind((4, 256, 768), LOW), anywhere),
        (kind((4, 256, 768), LOW), anywhere),
        (kind((256, 768), FULL), anywhere),
        (kind((256, 768), FULL), anywhere),
        (kind((4, 256, 768), LOW), anywhere),
        (kind((4, 256, 768), LOW), anywhere),
        (kind((4, 2, 2, 2, 96, HALF), LOW), anywhere),
        (kind((16, 256), FULL), vmem),
        (kind((16, 256), FULL), vmem),
    )
    return pl.pallas_call(
        forward_kernel,
        out_shape=tuple(out[0] for out in outs),
        in_specs=[vmem] * 15 + [smem] * 2,
        out_specs=tuple(out[1] for out in outs),
        scratch_shapes=[
            pltpu.VMEM((4, 2, 2, 2, 8, 768), LOW),
            pltpu.VMEM((12, 4, 2, 2, 2, 24, 768), LOW),
            pltpu.VMEM((4, 2, 2, 2, 96, 768), LOW),
            pltpu.VMEM((6, 256, 768), LOW),
            pltpu.VMEM((4, 256, 768), LOW),
            pltpu.VMEM((4, 256, 768), LOW),
            pltpu.VMEM((5, 768, 256), LOW),
            pltpu.VMEM((4, 768, 256), LOW),
            pltpu.VMEM((4, 256, 768), LOW),
            pltpu.VMEM((4, 256, 768), LOW),
            pltpu.VMEM((4, 768, 512), LOW),
            pltpu.VMEM((256, 768), FULL),
            pltpu.VMEM((256, 768), FULL),
            pltpu.VMEM((2, 256, HALF), LOW),
            pltpu.VMEM((256, HALF), LOW),
            pltpu.VMEM((4, 2, 2, 2, 96, HALF), LOW),
            pltpu.SemaphoreType.DMA((80,)),
            pltpu.SemaphoreType.DMA((180,)),
            pltpu.SemaphoreType.DMA((180,)),
        ],
        compiler_params=pltpu.CompilerParams(
            collective_id=0, has_side_effects=True, vmem_limit_bytes=60 * 2**20
        ),
    )(*shards, *rest)


Z_FIRST = (8, 9)


class Scatter:
    def __init__(self, post, grads, inboxes, done, sums, outs, spot, everyone):
        self.post, self.grads, self.inboxes, self.done, self.sums, self.outs = post, grads, inboxes, done, sums, outs
        self.spot, self.everyone = spot, everyone
        self.queue, self.waits, self.flipped, self.count = [], {(0, "sum"): []}, {}, 0

    def at(self, kind, unit, *where):
        mats, down = kind
        if isinstance(unit, int):
            return mats.at[(unit,) + where]
        where += (EVERY,) * (len(down.shape) - 2 - len(where))
        return down.at[where + (pl.ds(0 if unit == "down0" else 48, 48),)]

    def grad(self, unit, *where):
        return self.at(self.grads, unit, *where)

    def box(self, number, unit, *where):
        return self.at(self.inboxes[number], unit, *where)

    def begin(self, unit):
        z, x, y, c = self.spot
        self.flipped[unit] = self.count % 2 == 1
        self.count += 1
        if unit in Z_FIRST:
            first = Z_FIRST.index(unit)
            self.send(
                unit, 0, [(self.grad(unit, z ^ (k + 1)), self.inboxes[3].at[first, k], self.everyone[k]) for k in range(3)]
            )
        elif self.flipped[unit]:
            self.send(unit, 0, [(self.grad(unit, EVERY, 1 - x, EVERY, EVERY), self.box(0, unit), self.everyone[3])])
        else:
            self.send(unit, 0, [(self.grad(unit, EVERY, EVERY, 1 - y, EVERY), self.box(0, unit), self.everyone[4])])

    def send(self, unit, stage, copies):
        self.waits[unit] = [self.post.copy(*copy) for copy in copies]
        self.queue.append((unit, stage + 1))

    def add(self, target, *terms):
        total = target[...].astype(FULL)
        for term in terms:
            total = total + term[...].astype(FULL)
        target[...] = total.astype(LOW)

    def run(self, unit, stage):
        z, x, y, c = self.spot
        across, along, sibling = self.everyone[3:]
        flipped, early = self.flipped[unit], unit in Z_FIRST
        arrived(self.waits[unit])
        if stage == 1 and early:
            box = self.inboxes[3].at[Z_FIRST.index(unit)]
            self.add(self.grad(unit, z), *(box.at[k] for k in range(3)))
            if flipped:
                source, target = (z, 1 - x, EVERY, EVERY), across
            else:
                source, target = (z, EVERY, 1 - y, EVERY), along
            self.send(unit, 1, [(self.grad(unit, *source), self.box(0, unit, 0), target)])
        if stage == 2 and early:
            if flipped:
                self.add(self.grad(unit, z, x), self.box(0, unit, 0))
                source, target = (z, x, 1 - y, EVERY), along
            else:
                self.add(self.grad(unit, z, EVERY, y), self.box(0, unit, 0))
                source, target = (z, 1 - x, y, EVERY), across
            self.send(unit, 2, [(self.grad(unit, *source), self.box(1, unit, 0), target)])
        if stage == 1 and not early:
            if flipped:
                self.add(self.grad(unit, EVERY, x, EVERY, EVERY), self.box(0, unit))
                source, target = (EVERY, x, 1 - y, EVERY), along
            else:
                self.add(self.grad(unit, EVERY, EVERY, y, EVERY), self.box(0, unit))
                source, target = (EVERY, 1 - x, y, EVERY), across
            self.send(unit, 1, [(self.grad(unit, *source), self.box(1, unit), target)])
        if stage == 2 and not early:
            self.add(self.grad(unit, EVERY, x, y, EVERY), self.box(1, unit))
            self.send(
                unit,
                2,
                [(self.grad(unit, z ^ (k + 1), x, y, EVERY), self.box(2, unit, k), self.everyone[k]) for k in range(3)],
            )
        if stage == 3:
            total = []
            for core in (c, 1 - c):
                part = self.grad(unit, z, x, y, core)[...].astype(FULL)
                for k in range(1 if early else 3):
                    part = part + (self.box(1, unit, 0, core) if early else self.box(2, unit, k, core))[...].astype(FULL)
                total.append(part)
            mine = pl.ds(pl.multiple_of(c * HALF, 128), HALF)
            if isinstance(unit, int):
                target = self.outs[0].at[unit, :, mine]
            else:
                target = self.outs[1].at[pl.ds(0 if unit == "down0" else 48, 48), mine]
            target[...] = total[0]
            self.at(self.done, unit)[...] = total[1]
            self.send(unit, 3, [(self.at(self.done, unit), target, sibling)])

    def small_sum(self, hop):
        sums, boxes = self.sums
        hops = ((self.everyone[4],), (self.everyone[3],), self.everyone[:3], (self.everyone[5],))
        arrived(self.waits[0, "sum"])
        if hop in (1, 2, 4):
            sums[hop] = sums[hop - 1] + boxes[(0, 0, 1, 0, 5)[hop]]
        if hop == 3:
            sums[hop] = (sums[hop - 1] + boxes[2]) + (boxes[3] + boxes[4])
        if hop < 4:
            first = (0, 1, 2, 5)[hop]
            self.waits[0, "sum"] = [
                self.post.copy(sums.at[hop], boxes.at[first + k], target) for k, target in enumerate(hops[hop])
            ]
            self.queue.append(("sum", hop + 1))

    def pump(self, count):
        for _ in range(count):
            if self.queue:
                unit, stage = self.queue.pop(0)
                if unit == "sum":
                    self.small_sum(stage)
                else:
                    self.run(unit, stage)


def rms_back(upstream, field, gain):
    inverse = inverse_rms(field)
    scaled = gain * upstream
    shift = inverse * inverse * inverse * jnp.mean(scaled * field, axis=-1, keepdims=True)
    return inverse * scaled - field * shift, jnp.sum(upstream * field * inverse, axis=0, keepdims=True)


def split_dot(dotted, left, right):
    high = left.astype(LOW)
    return dotted(right, high) + dotted(right, (left - high.astype(FULL)).astype(LOW))


def backward_kernel(*refs):
    (mats, down, turned, memory_turned, grads_in) = refs[:5]
    (keys_in, values_in, hidden_in, slope_in, after_self, after_cross) = refs[5:11]
    (small_in, gains, tokens, cotangent, table, self_log, cross_log) = refs[11:18]
    lengths, memory_lengths = refs[18:20]
    (output, input_grad, memory_grad, mats_out, down_out, extra_out) = refs[20:26]
    (pool_a, pool_b, big, turned_box, wide_a, wide_b, rows_out) = refs[26:33]
    (own_cut, other_cut, own_long, other_long, rows_d, rows_bias, rows_distance) = refs[33:40]
    (grads, grads_down, box_one, box_one_down, box_two, box_two_down, box_three, box_three_down, box_early) = refs[40:49]
    (done, done_down, field, extra, extra_box, stage, small, near, send, recv) = refs[49:]
    spot = z, x, y, c = place()
    everyone = partners(*spot)
    sibling = everyone[5]
    post = Post(send, recv, near)
    comm = Scatter(
        post,
        (grads, grads_down),
        ((box_one, box_one_down), (box_two, box_two_down), (box_three, box_three_down), box_early),
        (done, done_down),
        (extra, extra_box),
        (mats_out, down_out),
        spot,
        everyone,
    )

    def fetch(source, target):
        return post.local(source, target, keep=True)

    def weight(ref, index):
        return ref[index * 32 : index * 32 + 32].reshape(768, 768)

    def fetch_weight(index, pool, slot):
        return fetch(mats.at[pl.ds(index * 32, 32)], pool.at[pl.ds(slot * 32, 32)])

    loads = {
        "grads": fetch(grads_in, grads_down),
        "down": fetch(down, pool_a),
        "slope": fetch(slope_in, wide_b),
        "hidden": fetch(hidden_in, wide_a),
        "in": fetch(mats.at[pl.ds(256, 128)], pool_b),
        "memory_turned": fetch(memory_turned, big),
        "turned4": fetch(turned.at[4], turned_box.at[0]),
        "turned3": fetch(turned.at[3], turned_box.at[1]),
        "turned2": fetch(turned.at[2], turned_box.at[2]),
        "after_cross": fetch(after_cross, field),
        "small": fetch(small_in, small),
    }

    def need(*names):
        for name in names:
            loads.pop(name).wait()

    def halves(value):
        left, right = value[:, :HALF], value[:, HALF:]
        return jnp.where(c == 0, left, right), jnp.where(c == 0, right, left)

    def whole(mine, other):
        return jnp.concatenate([jnp.where(c == 0, mine, other), jnp.where(c == 0, other, mine)], axis=1)

    hand = {}

    def share(slot, value):
        mine, other = halves(value)
        own_cut[slot, 0] = mine
        other_cut[slot] = other
        hand[slot] = post.copy(other_cut.at[slot], own_cut.at[slot, 1], sibling)

    def shared(slot):
        hand.pop(slot).wait_recv()
        return own_cut[slot].reshape(512, HALF)

    def both(slot):
        return whole(own_cut[slot, 0], other_cut[slot])

    def sum_rows(slot, left, right):
        grads[slot] = dot(left, right).astype(LOW).reshape(4, 2, 2, 2, 24, HALF)

    live = lax.broadcasted_iota(jnp.int32, (ROWS, 1), 0) < lengths[0]
    grad_out = jnp.where(live, cotangent[...].astype(FULL), 0.0)
    grad_low = grad_out.astype(LOW)
    enter(everyone)
    need("grads")
    comm.begin("down0")
    comm.begin("down1")
    need("down", "slope")
    for block in range(4):
        grad_hidden = dot_last(grad_low, weight(pool_a, block))
        share(1 + block, (grad_hidden * wide_b[block].astype(FULL)).astype(LOW))
    need("hidden", "after_cross")
    total = field[...]
    for block in range(4):
        total = total + dot(wide_a[block], weight(pool_a, block))
    output[...] = total.astype(LOW)
    loads["keys"] = fetch(keys_in, wide_a)
    for slot, index in enumerate((7, 4, 5, 6)):
        loads[index] = fetch_weight(index, pool_a, slot)
    loads["values"] = fetch(values_in, wide_b)
    need("turned4", "in")
    upstream = 0.0
    for block in range(4):
        sum_rows(8 + block, turned_box[0], shared(1 + block))
        comm.begin(8 + block)
        upstream = upstream + dot_last(both(1 + block), weight(pool_b, block))
    loads["turned1"] = fetch(turned.at[1], turned_box.at[0])
    for slot, index in enumerate((3, 0, 1, 2)):
        loads[index] = fetch_weight(index, pool_b, slot)
    step, gain_three = rms_back(upstream, field[...], gains[2:3])
    extra[0] = jnp.zeros((8, 768), FULL)
    extra[0, 2:3] = gain_three
    input_grad[...] = grad_out + step
    grad_low = input_grad[...].astype(LOW)
    share(5, grad_low)
    loads["after_self"] = fetch(after_self, field)
    need(7)
    upstream = dot_last(grad_low, weight(pool_a, 0)).astype(LOW)
    need("turned3")
    sum_rows(7, turned_box[1], shared(5))
    comm.begin(7)
    loads["turned0"] = fetch(turned.at[0], turned_box.at[1])

    heads = (
        lax.broadcasted_iota(jnp.int32, (16, 768), 1) // DH == lax.broadcasted_iota(jnp.int32, (16, 768), 0)
    ).astype(LOW)

    def inner_rows(context):
        rows_d[...] = split_dot(dot_last, upstream_ref[...].astype(FULL) * context.astype(FULL), heads)

    upstream_ref = stage
    upstream_ref[...] = upstream
    need("small")
    inner_rows(small[5])

    def attend_back(pair, query_block, key_block, value_block, log_ref, extra_of, visit):
        span = pl.ds(pl.multiple_of(pair * 128, 128), 128)
        query, handed = query_block(span) * 0.125, upstream_ref[:, span]
        grad_values, grad_keys, grad_query = 0.0, 0.0, []
        key_block, value_block = key_block(span), value_block(span)
        for head in range(2):
            row = pl.ds(pair * 2 + head, 1)
            query_part, handed_part = one_head(query, head), one_head(handed, head)
            attended = jnp.exp(dot_last(key_block, query_part) + extra_of(row) - log_ref[row])
            grad_scores = attended * (dot_last(value_block, handed_part) - rows_d[row])
            visit(row, grad_scores)
            rounded = grad_scores.astype(LOW)
            grad_values = grad_values + dot(attended.astype(LOW), handed_part)
            grad_keys = grad_keys + dot(rounded, query_part)
            grad_query.append(dot_first(key_block, rounded)[head * DH : head * DH + DH])
        grad_query = jnp.concatenate(grad_query, axis=0).T * 0.125
        return grad_query.astype(LOW), grad_keys.astype(LOW), grad_values.astype(LOW)

    need("keys", "values")
    shown = memory_mask(memory_lengths[0], 1024)
    for turn in range(6):
        mine, lane = turn >= 3, slice(turn % 3 * 128, turn % 3 * 128 + 128)
        pair = (c if mine else 1 - c) * 3 + turn % 3
        grad_query, grad_keys, grad_values = attend_back(
            pair,
            lambda span: small[4, :, span],
            lambda span: wide_a[:, :, span].reshape(1024, 128),
            lambda span: wide_b[:, :, span].reshape(1024, 128),
            cross_log,
            lambda row: shown,
            lambda row, value: None,
        )
        grad_keys, grad_values = grad_keys.reshape(4, ROWS, 128), grad_values.reshape(4, ROWS, 128)
        if mine:
            own_cut[6, 0, :, lane] = grad_query
            own_long[0, :, 0, :, lane] = grad_keys
            own_long[1, :, 0, :, lane] = grad_values
        else:
            other_cut[6, :, lane] = grad_query
            other_long[0, :, :, lane] = grad_keys
            other_long[1, :, :, lane] = grad_values
        if turn == 2:
            hand[6] = post.copy(other_cut.at[6], own_cut.at[6, 1], sibling)
            for kind in range(2):
                hand["long", kind] = post.copy(other_long.at[kind], own_long.at[kind, :, 1], sibling)
        comm.pump(1)
    need(4, 5, 6)
    need("turned2", "after_self")
    upstream = dot_last(both(6), weight(pool_a, 1))
    step, gain_two = rms_back(upstream, field[...], gains[1:2])
    extra[0, 1:2] = gain_two
    input_grad[...] = input_grad[...] + step
    grad_low = input_grad[...].astype(LOW)
    share(7, grad_low)
    comm.pump(1)
    need("memory_turned")
    for kind, unit in ((0, 5), (1, 6)):
        hand.pop(("long", kind)).wait_recv()
        total = 0.0
        for block in range(4):
            total = total + dot(big[block], own_long[kind, block].reshape(512, HALF))
        grads[unit] = total.astype(LOW).reshape(4, 2, 2, 2, 24, HALF)
        comm.begin(unit)
        comm.pump(1)
    sum_rows(4, turned_box[2], shared(6))
    comm.begin(4)
    comm.pump(1)
    need(3, "turned1")
    upstream_ref[...] = dot_last(grad_low, weight(pool_b, 0)).astype(LOW)
    inner_rows(small[3])
    sum_rows(3, turned_box[0], shared(7))
    comm.begin(3)
    one_hot = bucket_rows()
    rows_bias[0:12] = dot(table[...], one_hot)
    visible = self_mask(lengths[0])

    def by_distance(row, value):
        eight = value[:8]
        for first in range(8, ROWS, 8):
            eight = eight + pltpu.roll(value[first : first + 8], ROWS - first, 1)
        total = eight[:1]
        for first in range(1, 8):
            total = total + pltpu.roll(eight, ROWS - first, 1)[first : first + 1]
        rows_distance[row] = total

    rows_distance[...] = jnp.zeros((16, ROWS), FULL)
    for turn in range(6):
        mine, lane = turn >= 3, slice(turn % 3 * 128, turn % 3 * 128 + 128)
        pair = (c if mine else 1 - c) * 3 + turn % 3
        parts = attend_back(
            pair,
            lambda span: small[0, :, span],
            lambda span: small[1, :, span],
            lambda span: small[2, :, span],
            self_log,
            lambda row: slanted(rows_bias[row]) + visible,
            by_distance,
        )
        for slot, part in zip((8, 9, 10), parts):
            if mine:
                own_cut[slot, 0, :, lane] = part
            else:
                other_cut[slot, :, lane] = part
        if turn == 2:
            for slot in (8, 9, 10):
                hand[slot] = post.copy(other_cut.at[slot], own_cut.at[slot, 1], sibling)
        comm.pump(2)
    need("turned0", 0, 1, 2)
    for unit in range(3):
        sum_rows(unit, turned_box[1], shared(8 + unit))
        comm.begin(unit)
        comm.pump(1)
    upstream = 0.0
    for unit in range(3):
        upstream = upstream + dot_last(both(8 + unit), weight(pool_b, 1 + unit))
    step, gain_one = rms_back(upstream, tokens[...].astype(FULL), gains[0:1])
    extra[0, 0:1] = gain_one
    high = rows_distance[...].astype(LOW)
    many = jnp.concatenate([one_hot] * 16, axis=0)
    sums = dot_last(high, many) + dot_last((rows_distance[...] - high.astype(FULL)).astype(LOW), many)
    own_head = lax.broadcasted_iota(jnp.int32, (16, 512), 1) // NB == lax.broadcasted_iota(jnp.int32, (16, 512), 0)
    extra[0, 3:4, :512] = jnp.sum(jnp.where(own_head, sums, 0.0), axis=0, keepdims=True)
    input_grad[...] = input_grad[...] + step
    comm.small_sum(0)
    shown_rows = []
    for block in range(4):
        comm.pump(3)
        if block >= 2:
            shown_rows[block - 2].wait()
        rows_out[block % 2] = dot_last(
            whole(own_long[0, block, 0], other_long[0, block]), weight(pool_a, 2)
        ) + dot_last(whole(own_long[1, block, 0], other_long[1, block]), weight(pool_a, 3))
        shown_rows.append(fetch(rows_out.at[block % 2], memory_grad.at[pl.ds(block * ROWS, ROWS)]))
    while comm.queue:
        comm.pump(1)
    for made in shown_rows[2:]:
        made.wait()
    extra_out[...] = extra[4]
    post.finish()


def backward_call(*args):
    kind = jax.ShapeDtypeStruct
    anywhere, vmem = pl.BlockSpec(memory_space=pl.ANY), pl.BlockSpec(memory_space=pltpu.VMEM)
    smem = pl.BlockSpec(memory_space=pltpu.SMEM)
    vm, dma = pltpu.VMEM, pltpu.SemaphoreType.DMA
    return pl.pallas_call(
        backward_kernel,
        out_shape=(
            kind((256, 768), LOW),
            kind((256, 768), FULL),
            kind((1024, 768), FULL),
            kind((12, 24, 768), FULL),
            kind((96, 768), FULL),
            kind((8, 768), FULL),
        ),
        in_specs=[anywhere] * 12 + [vmem] * 6 + [smem] * 2,
        out_specs=(vmem, vmem, anywhere, vmem, vmem, vmem),
        scratch_shapes=[
            vm((128, 24, 768), LOW),
            vm((128, 24, 768), LOW),
            vm((4, 768, 512), LOW),
            vm((3, 768, 512), LOW),
            vm((4, 256, 768), LOW),
            vm((4, 256, 768), LOW),
            vm((2, 256, 768), FULL),
            vm((11, 2, 256, HALF), LOW),
            vm((11, 256, HALF), LOW),
            vm((2, 4, 2, 256, HALF), LOW),
            vm((2, 4, 256, HALF), LOW),
            vm((16, 256), FULL),
            vm((16, 256), FULL),
            vm((16, 256), FULL),
            vm((12, 4, 2, 2, 2, 24, HALF), LOW),
            vm((4, 2, 2, 2, 96, HALF), LOW),
            vm((12, 4, 2, 2, 24, HALF), LOW),
            vm((4, 2, 2, 96, HALF), LOW),
            vm((12, 4, 2, 24, HALF), LOW),
            vm((4, 2, 96, HALF), LOW),
            vm((12, 3, 2, 24, HALF), LOW),
            vm((3, 2, 96, HALF), LOW),
            vm((len(Z_FIRST), 3, 2, 2, 2, 24, HALF), LOW),
            vm((12, 24, HALF), FULL),
            vm((96, HALF), FULL),
            vm((256, 768), FULL),
            vm((5, 8, 768), FULL),
            vm((6, 8, 768), FULL),
            vm((256, 768), LOW),
            vm((6, 256, 768), LOW),
            dma((60,)),
            dma((150,)),
            dma((150,)),
        ],
        compiler_params=pltpu.CompilerParams(
            collective_id=1, has_side_effects=True, vmem_limit_bytes=60 * 2**20
        ),
    )(*args)


def finish_kernel(*refs):
    (output, input_grad, memory_grad, mats, down, extra), outs = refs[:6], refs[6:]
    for source, target in zip((output, input_grad, memory_grad, down), outs):
        target[...] = source[...]
    for index in range(8):
        outs[4 + index][...] = mats[index]
    for index in range(4):
        outs[12][:, index * 768 : (index + 1) * 768] = mats[8 + index]
    rank = lax.axis_index(AXES[0]) * lax.axis_size(AXES[1]) + lax.axis_index(AXES[1])
    own = pltpu.roll(extra[...], 768 - rank * 24, 1)
    for index in range(3):
        outs[13 + index][...] = own[index : index + 1, :24]
    for head in range(12):
        outs[16][head : head + 1] = extra[3:4, head * NB : head * NB + NB]


def finish(*args):
    kind = jax.ShapeDtypeStruct
    block = lambda *shape: pl.BlockSpec(shape, lambda step: (step, 0))
    whole = lambda *shape: pl.BlockSpec(shape, lambda step: (0,) * len(shape))
    rows = [block(64, 768), block(64, 768), block(256, 768)]
    single = [(96, 768)] + [(24, 768)] * 8 + [(24, 3072)] + [(1, 24)] * 3 + [(12, NB)]
    return pl.pallas_call(
        finish_kernel,
        grid=(4,),
        out_shape=(
            kind((256, 768), LOW),
            kind((256, 768), FULL),
            kind((1024, 768), FULL),
            *[kind(shape, FULL) for shape in single],
        ),
        in_specs=rows + [whole(12, 24, 768), whole(96, 768), whole(8, 768)],
        out_specs=rows + [whole(*shape) for shape in single],
    )(*args)


def plain_body(
    tokens,
    memory,
    cotangent,
    target_lengths,
    memory_lengths,
    self_gain,
    self_query,
    self_key,
    self_value,
    self_out,
    position_table,
    cross_gain,
    cross_query,
    cross_key,
    cross_value,
    cross_out,
    ffn_gain,
    ffn_in,
    ffn_out,
):
    wide_count = lax.axis_size(AXES[0])
    narrow_count = lax.axis_size(AXES[1])
    devices = wide_count * narrow_count
    seq_count = target_lengths.shape[0]
    target_rows = tokens.shape[0] // seq_count
    memory_rows = memory.shape[0] // seq_count
    positions = jnp.arange(target_rows, dtype=jnp.int32)
    live_rows = positions[None, :] < target_lengths[:, None]
    causal = positions[None, :] <= positions[:, None]
    self_visible = causal[None] & live_rows[:, None, :]
    memory_visible = (jnp.arange(memory_rows, dtype=jnp.int32)[None, :] < memory_lengths[:, None])[
        :, None, :
    ]
    grad_out = jnp.where(live_rows.reshape(-1, 1), cotangent.astype(jnp.float32), 0.0)
    bucket = bucket_index(target_rows)
    one_hot = (bucket[:, :, None] == jnp.arange(NB, dtype=jnp.int32)[None, None, :]).astype(
        jnp.float32
    )
    relative = jnp.einsum(
        "ijb,bh->hij", one_hot, position_table.astype(jnp.float32), precision=lax.Precision.HIGHEST
    )
    gain_one, weight_query, weight_key, weight_value, weight_out = (
        lax.all_gather(self_gain, AXES, axis=0, tiled=True),
        lax.all_gather(self_query, AXES, axis=0, tiled=True),
        lax.all_gather(self_key, AXES, axis=0, tiled=True),
        lax.all_gather(self_value, AXES, axis=0, tiled=True),
        lax.all_gather(self_out, AXES, axis=0, tiled=True),
    )
    source = tokens.astype(jnp.float32)
    normed_value, norm_back_one = jax.vjp(rms_apply, source, gain_one.astype(jnp.float32))
    normed_one = normed_value.astype(jnp.bfloat16)
    query_one = product(normed_one, weight_query).astype(jnp.bfloat16)
    keys_one = product(normed_one, weight_key).astype(jnp.bfloat16)
    values_one = product(normed_one, weight_value).astype(jnp.bfloat16)
    context_one, totals_one = attend_forward(
        query_one, keys_one, values_one, relative, self_visible, seq_count
    )
    after_self = source + product(context_one, weight_out)
    gain_two, cross_weight_query, cross_weight_key, cross_weight_value, cross_weight_out = (
        lax.all_gather(cross_gain, AXES, axis=0, tiled=True),
        lax.all_gather(cross_query, AXES, axis=0, tiled=True),
        lax.all_gather(cross_key, AXES, axis=0, tiled=True),
        lax.all_gather(cross_value, AXES, axis=0, tiled=True),
        lax.all_gather(cross_out, AXES, axis=0, tiled=True),
    )
    normed_value, norm_back_two = jax.vjp(rms_apply, after_self, gain_two.astype(jnp.float32))
    normed_two = normed_value.astype(jnp.bfloat16)
    query_two = product(normed_two, cross_weight_query).astype(jnp.bfloat16)
    keys_two = product(memory, cross_weight_key).astype(jnp.bfloat16)
    values_two = product(memory, cross_weight_value).astype(jnp.bfloat16)
    context_two, totals_two = attend_forward(
        query_two, keys_two, values_two, None, memory_visible, seq_count
    )
    after_cross = after_self + product(context_two, cross_weight_out)
    gain_three, weight_in, weight_down = (
        lax.all_gather(ffn_gain, AXES, axis=0, tiled=True),
        lax.all_gather(ffn_in, AXES, axis=0, tiled=True),
        lax.all_gather(ffn_out, AXES, axis=0, tiled=True),
    )
    normed_value, norm_back_three = jax.vjp(rms_apply, after_cross, gain_three.astype(jnp.float32))
    normed_three = normed_value.astype(jnp.bfloat16)
    before = product(normed_three, weight_in)
    gelu_value, gelu_back = jax.vjp(gelu_smooth, before)
    hidden = gelu_value.astype(jnp.bfloat16)
    output = (after_cross + product(hidden, weight_down)).astype(jnp.bfloat16)
    back_in, back_down = (
        lax.all_gather(ffn_in, AXES, axis=0, tiled=True),
        lax.all_gather(ffn_out, AXES, axis=0, tiled=True),
    )
    grad_low = grad_out.astype(jnp.bfloat16)
    grad_down_weight = outer_sum(hidden, grad_low)
    grad_hidden = back_project(grad_low, back_down)
    grad_before = gelu_back(grad_hidden)[0].astype(jnp.bfloat16)
    grad_in_weight = outer_sum(normed_three, grad_before)
    grad_normed_three = back_project(grad_before, back_in)
    grad_cross_part, grad_gain_three = norm_back_three(grad_normed_three)
    grad_cross = grad_out + grad_cross_part
    ffn_terms = (grad_gain_three, grad_in_weight, grad_down_weight)
    summed_ffn = lax.psum_scatter(
        pack_rows(ffn_terms, devices), AXES, scatter_dimension=0, tiled=True
    )
    ffn_gain_grad, ffn_in_grad, ffn_out_grad = unpack_rows(summed_ffn[0], ffn_terms, devices)
    back_cross_query, back_cross_key, back_cross_value, back_cross_out = (
        lax.all_gather(cross_query, AXES, axis=0, tiled=True),
        lax.all_gather(cross_key, AXES, axis=0, tiled=True),
        lax.all_gather(cross_value, AXES, axis=0, tiled=True),
        lax.all_gather(cross_out, AXES, axis=0, tiled=True),
    )
    grad_cross_low = grad_cross.astype(jnp.bfloat16)
    grad_cross_out_weight = outer_sum(context_two, grad_cross_low)
    grad_context_two = back_project(grad_cross_low, back_cross_out).astype(jnp.bfloat16)
    grad_query_two, grad_keys_two, grad_values_two, unused_extra = attend_backward(
        query_two,
        keys_two,
        values_two,
        None,
        memory_visible,
        seq_count,
        totals_two,
        grad_context_two,
    )
    grad_cross_query_weight = outer_sum(normed_two, grad_query_two)
    grad_cross_key_weight = outer_sum(memory, grad_keys_two)
    grad_cross_value_weight = outer_sum(memory, grad_values_two)
    memory_grad = back_project(grad_keys_two, back_cross_key) + back_project(
        grad_values_two, back_cross_value
    )
    grad_self_part, grad_gain_two = norm_back_two(back_project(grad_query_two, back_cross_query))
    grad_self = grad_cross + grad_self_part
    cross_terms = (
        grad_gain_two,
        grad_cross_query_weight,
        grad_cross_key_weight,
        grad_cross_value_weight,
        grad_cross_out_weight,
    )
    summed_cross = lax.psum_scatter(
        pack_rows(cross_terms, devices), AXES, scatter_dimension=0, tiled=True
    )
    cross_gain_grad, cross_query_grad, cross_key_grad, cross_value_grad, cross_out_grad = (
        unpack_rows(summed_cross[0], cross_terms, devices)
    )
    back_query, back_key, back_value, back_out = (
        lax.all_gather(self_query, AXES, axis=0, tiled=True),
        lax.all_gather(self_key, AXES, axis=0, tiled=True),
        lax.all_gather(self_value, AXES, axis=0, tiled=True),
        lax.all_gather(self_out, AXES, axis=0, tiled=True),
    )
    grad_self_low = grad_self.astype(jnp.bfloat16)
    grad_out_weight = outer_sum(context_one, grad_self_low)
    grad_context_one = back_project(grad_self_low, back_out).astype(jnp.bfloat16)
    grad_query_one, grad_keys_one, grad_values_one, grad_relative = attend_backward(
        query_one,
        keys_one,
        values_one,
        relative,
        self_visible,
        seq_count,
        totals_one,
        grad_context_one,
    )
    table_term = jnp.einsum("hij,ijb->bh", grad_relative, one_hot, precision=lax.Precision.HIGHEST)
    position_table_grad = lax.psum(table_term, AXES)
    grad_query_weight = outer_sum(normed_one, grad_query_one)
    grad_key_weight = outer_sum(normed_one, grad_keys_one)
    grad_value_weight = outer_sum(normed_one, grad_values_one)
    grad_normed_one = (
        back_project(grad_query_one, back_query)
        + back_project(grad_keys_one, back_key)
        + back_project(grad_values_one, back_value)
    )
    grad_source_part, grad_gain_one = norm_back_one(grad_normed_one)
    input_grad = grad_self + grad_source_part
    self_terms = (
        grad_gain_one,
        grad_query_weight,
        grad_key_weight,
        grad_value_weight,
        grad_out_weight,
    )
    summed_self = lax.psum_scatter(
        pack_rows(self_terms, devices), AXES, scatter_dimension=0, tiled=True
    )
    self_gain_grad, self_query_grad, self_key_grad, self_value_grad, self_out_grad = unpack_rows(
        summed_self[0], self_terms, devices
    )
    return (
        output,
        input_grad,
        memory_grad,
        self_gain_grad,
        self_query_grad,
        self_key_grad,
        self_value_grad,
        self_out_grad,
        position_table_grad,
        cross_gain_grad,
        cross_query_grad,
        cross_key_grad,
        cross_value_grad,
        cross_out_grad,
        ffn_gain_grad,
        ffn_in_grad,
        ffn_out_grad,
    )


def body(
    tokens,
    memory,
    cotangent,
    target_lengths,
    memory_lengths,
    self_gain,
    self_query,
    self_key,
    self_value,
    self_out,
    position_table,
    cross_gain,
    cross_query,
    cross_key,
    cross_value,
    cross_out,
    ffn_gain,
    ffn_in,
    ffn_out,
):
    rank = lax.axis_index(AXES[0]) * lax.axis_size(AXES[1]) + lax.axis_index(AXES[1])
    own_gains = jnp.stack([self_gain, cross_gain, ffn_gain])
    spread = lax.dynamic_update_slice(jnp.zeros((8, 768), LOW), own_gains, (0, rank * 24))
    shards = (self_query, self_key, self_value, self_out, cross_query, cross_key, cross_value, cross_out, ffn_in, ffn_out)
    (
        mats,
        down,
        gains,
        turned,
        memory_turned,
        small,
        keys,
        values,
        after_self,
        after_cross,
        hidden,
        slope,
        down_grads,
        self_log,
        cross_log,
    ) = forward_call(
        shards + (spread,), tokens, memory, cotangent, position_table.T, target_lengths, memory_lengths
    )
    output, input_grad, memory_grad, mats_grad, down_grad, extra = backward_call(
        mats.reshape(384, 24, 768),
        down.reshape(128, 24, 768),
        turned,
        memory_turned,
        down_grads,
        keys,
        values,
        hidden,
        slope,
        after_self,
        after_cross,
        small,
        gains,
        tokens,
        cotangent,
        position_table.T,
        self_log,
        cross_log,
        target_lengths,
        memory_lengths,
    )
    output, input_grad, memory_grad, down_grad, *square_grads, ffn_in_grad, gain_one, gain_two, gain_three, table = finish(
        output, input_grad, memory_grad, mats_grad, down_grad, extra
    )
    return (
        output,
        input_grad,
        memory_grad,
        gain_one.reshape(24),
        *square_grads[:4],
        table.T,
        gain_two.reshape(24),
        *square_grads[4:],
        gain_three.reshape(24),
        ffn_in_grad,
        down_grad,
    )


def solution(mesh):
    whole = (mesh.shape[AXES[0]], mesh.shape[AXES[1]]) == (8, 4)
    placed = (
        P(AXES, None),
        P(AXES, None),
        P(AXES, None),
        P(AXES),
        P(AXES),
        P(AXES),
        P(AXES, None),
        P(AXES, None),
        P(AXES, None),
        P(AXES, None),
        P(),
        P(AXES),
        P(AXES, None),
        P(AXES, None),
        P(AXES, None),
        P(AXES, None),
        P(AXES),
        P(AXES, None),
        P(AXES, None),
    )
    return jax.shard_map(
        body if whole else plain_body,
        mesh=mesh,
        in_specs=placed,
        out_specs=(
            P(AXES, None),
            P(AXES, None),
            P(AXES, None),
            P(AXES),
            P(AXES, None),
            P(AXES, None),
            P(AXES, None),
            P(AXES, None),
            P(),
            P(AXES),
            P(AXES, None),
            P(AXES, None),
            P(AXES, None),
            P(AXES, None),
            P(AXES),
            P(AXES, None),
            P(AXES, None),
        ),
        check_vma=False,
    )
```

```python
import math

import jax
import jax.numpy as jnp
from jax import lax
from jax.experimental import pallas as pl
from jax.experimental.pallas import tpu as pltpu
from jax.sharding import PartitionSpec as P

DH = 64
NB = 32
MAXDIST = 128


AXES = ("wide", "narrow")
EPSILON = 1e-06
NEGATIVE = -1e30


def bucket_index(length):
    offsets = jnp.arange(length, dtype=jnp.int32)
    distance = jnp.maximum(offsets[:, None] - offsets[None, :], 0)
    exact_part = NB // 2
    bucket = jnp.minimum(distance, exact_part)
    for step in range(1, NB - exact_part):
        bound = math.ceil(exact_part * (MAXDIST / exact_part) ** (step / (NB - exact_part)))
        bucket = bucket + (distance >= bound).astype(jnp.int32)
    return bucket


def rms_apply(field, gain):
    inverse = lax.rsqrt(jnp.mean(field * field, axis=-1, keepdims=True) + EPSILON)
    return field * inverse * gain


def gelu_smooth(field):
    return jax.nn.gelu(field, approximate=True)


def product(left, right):
    return jnp.dot(left, right, preferred_element_type=jnp.float32)


def outer_sum(left, right):
    return jnp.einsum("rd,re->de", left, right, preferred_element_type=jnp.float32)


def back_project(left, right):
    return jnp.einsum("re,de->rd", left, right, preferred_element_type=jnp.float32)


def pack_rows(arrays, devices):
    return jnp.concatenate([array.reshape(devices, -1) for array in arrays], axis=1)


def unpack_rows(packed_row, arrays, devices):
    results = []
    offset = 0
    for array in arrays:
        shard_shape = (array.shape[0] // devices,) + array.shape[1:]
        count = array.size // devices
        results.append(packed_row[offset : offset + count].reshape(shard_shape))
        offset = offset + count
    return tuple(results)


def head_blocks(array, index, seq_count):
    block = lax.dynamic_slice_in_dim(array, index * 2 * DH, 2 * DH, 1)
    return block.reshape(seq_count, -1, 2, DH)


def flat_block(block):
    return block.reshape(-1, 2 * DH)


def scored(query_block, keys_block, extra, visible, index):
    scores = jnp.einsum(
        "sqhd,skhd->shqk", query_block, keys_block, preferred_element_type=jnp.float32
    ) * DH ** (-0.5)
    if extra is not None:
        scores = scores + lax.dynamic_slice_in_dim(extra, index * 2, 2, 0)[None]
    return jnp.where(visible[:, None], scores, NEGATIVE)


def attend_forward(query, keys, values, extra, visible, seq_count):
    pairs = query.shape[1] // (2 * DH)
    start_context = jnp.zeros(query.shape, jnp.bfloat16)
    start_totals = jnp.zeros((seq_count, 2 * pairs, query.shape[0] // seq_count), jnp.float32)

    def one_pair(index, carry):
        context, log_total = carry
        query_block = head_blocks(query, index, seq_count)
        scores = scored(query_block, head_blocks(keys, index, seq_count), extra, visible, index)
        peak = jnp.max(scores, axis=-1, keepdims=True)
        raised = jnp.exp(scores - peak)
        total = jnp.sum(raised, axis=-1, keepdims=True)
        attend = (raised / total).astype(jnp.bfloat16)
        mixed = jnp.einsum(
            "shqk,skhd->sqhd",
            attend,
            head_blocks(values, index, seq_count),
            preferred_element_type=jnp.float32,
        )
        context = lax.dynamic_update_slice_in_dim(
            context, flat_block(mixed.astype(jnp.bfloat16)), index * 2 * DH, 1
        )
        log_total = lax.dynamic_update_slice_in_dim(
            log_total, (peak + jnp.log(total))[..., 0], index * 2, 1
        )
        return (context, log_total)

    return lax.fori_loop(0, pairs, one_pair, (start_context, start_totals))


def attend_backward(query, keys, values, extra, visible, seq_count, log_total, grad_context):
    pairs = query.shape[1] // (2 * DH)
    scale = DH ** (-0.5)
    extra_shape = extra.shape if extra is not None else (1,)
    start_grads = (
        jnp.zeros(query.shape, jnp.bfloat16),
        jnp.zeros(keys.shape, jnp.bfloat16),
        jnp.zeros(values.shape, jnp.bfloat16),
        jnp.zeros(extra_shape, jnp.float32),
    )

    def one_pair(index, carry):
        grad_query, grad_keys, grad_values, grad_extra = carry
        query_block = head_blocks(query, index, seq_count)
        keys_block = head_blocks(keys, index, seq_count)
        value_block = head_blocks(values, index, seq_count)
        upstream = head_blocks(grad_context, index, seq_count)
        scores = scored(query_block, keys_block, extra, visible, index)
        attend = jnp.exp(scores - lax.dynamic_slice_in_dim(log_total, index * 2, 2, 1)[..., None])
        grad_attend = jnp.einsum(
            "sqhd,skhd->shqk", upstream, value_block, preferred_element_type=jnp.float32
        )
        value_grad = jnp.einsum(
            "shqk,sqhd->skhd",
            attend.astype(jnp.bfloat16),
            upstream,
            preferred_element_type=jnp.float32,
        ).astype(jnp.bfloat16)
        inner = jnp.sum(attend * grad_attend, axis=-1, keepdims=True)
        grad_score = attend * (grad_attend - inner)
        rounded = grad_score.astype(jnp.bfloat16)
        query_grad = (
            jnp.einsum("shqk,skhd->sqhd", rounded, keys_block, preferred_element_type=jnp.float32)
            * scale
        ).astype(jnp.bfloat16)
        keys_grad = (
            jnp.einsum("shqk,sqhd->skhd", rounded, query_block, preferred_element_type=jnp.float32)
            * scale
        ).astype(jnp.bfloat16)
        offset = index * 2 * DH
        grad_query = lax.dynamic_update_slice_in_dim(grad_query, flat_block(query_grad), offset, 1)
        grad_keys = lax.dynamic_update_slice_in_dim(grad_keys, flat_block(keys_grad), offset, 1)
        grad_values = lax.dynamic_update_slice_in_dim(
            grad_values, flat_block(value_grad), offset, 1
        )
        if extra is not None:
            grad_extra = lax.dynamic_update_slice_in_dim(
                grad_extra, jnp.sum(grad_score, axis=0), index * 2, 0
            )
        return (grad_query, grad_keys, grad_values, grad_extra)

    return lax.fori_loop(0, pairs, one_pair, start_grads)


MESH = pl.DeviceIdType.MESH
HALF = 384
ROWS = 256
LOW, FULL = jnp.bfloat16, jnp.float32
EVERY = slice(None)


def place():
    wide = lax.axis_index(AXES[0])
    narrow = lax.axis_index(AXES[1])
    return wide // 2, lax.rem(wide, 2), narrow // 2, lax.rem(narrow, 2)


def device(z, x, y, c):
    return (z * 2 + x, y * 2 + c)


def partners(z, x, y, c):
    return (
        device(z ^ 1, x, y, c),
        device(z ^ 2, x, y, c),
        device(z ^ 3, x, y, c),
        device(z, 1 - x, y, c),
        device(z, x, 1 - y, c),
        device(z, x, y, 1 - c),
    )


def enter(everyone):
    barrier = pltpu.get_barrier_semaphore()
    for other in everyone:
        pl.semaphore_signal(barrier, inc=1, device_id=other, device_id_type=MESH)
    pl.semaphore_wait(barrier, len(everyone))


class Post:
    def __init__(self, send, recv, near):
        self.send, self.recv, self.near = send, recv, near
        self.used, self.used_near, self.started, self.open = 0, 0, [], []

    def copy(self, source, target, where):
        made = pltpu.make_async_remote_copy(
            src_ref=source,
            dst_ref=target,
            send_sem=self.send.at[self.used],
            recv_sem=self.recv.at[self.used],
            device_id=where,
            device_id_type=MESH,
        )
        self.used += 1
        made.start()
        self.started.append(made)
        return made

    def local(self, source, target, keep=False):
        made = pltpu.make_async_copy(source, target, self.near.at[self.used_near])
        self.used_near += 1
        made.start()
        if not keep:
            self.open.append(made)
        return made

    def finish(self):
        for made in self.started:
            made.wait_send()
        for made in self.open:
            made.wait()


def arrived(copies):
    for made in copies:
        made.wait_recv()


def dot(left, right):
    return jnp.dot(left, right, preferred_element_type=FULL)


def dot_last(left, right):
    return lax.dot_general(left, right, (((1,), (1,)), ((), ())), preferred_element_type=FULL)


def dot_first(left, right):
    return lax.dot_general(left, right, (((0,), (0,)), ((), ())), preferred_element_type=FULL)


def square(ref, index):
    return ref[index].reshape(768, 768)


def bucket_rows():
    distance = lax.broadcasted_iota(jnp.int32, (NB, ROWS), 1)
    row = lax.broadcasted_iota(jnp.int32, (NB, ROWS), 0)
    exact_part = NB // 2
    bucket = jnp.minimum(distance, exact_part)
    for step in range(1, NB - exact_part):
        bound = math.ceil(exact_part * (MAXDIST / exact_part) ** (step / (NB - exact_part)))
        bucket = bucket + (distance >= bound).astype(jnp.int32)
    return (bucket == row).astype(LOW)


def self_mask(length):
    key = lax.broadcasted_iota(jnp.int32, (ROWS, ROWS), 0)
    query = lax.broadcasted_iota(jnp.int32, (ROWS, ROWS), 1)
    return jnp.where((key <= query) & (key < length), 0.0, NEGATIVE)


def memory_mask(length, rows):
    key = lax.broadcasted_iota(jnp.int32, (rows, 1), 0)
    return jnp.where(key < length, 0.0, NEGATIVE)


def slanted(row):
    return pltpu.roll(jnp.broadcast_to(row, (ROWS, ROWS)), 0, 1, stride=1, stride_axis=0)


def one_head(block, head):
    lane = lax.broadcasted_iota(jnp.int32, block.shape, 1)
    return jnp.where((lane < DH) if head == 0 else (lane >= DH), block, jnp.zeros_like(block))


def inverse_rms(field):
    return lax.rsqrt(jnp.mean(field * field, axis=-1, keepdims=True) + EPSILON)


PAIRS = [("gains", 0, 1), (2, 3), (4, 7), (5, 6), (8, 9), (10, 11), ((0, 0), (0, 1))]
LATE = ((1, 0), (1, 1))
ORDERS = {"gains": "zxy", (0, 0): "zxy", (0, 1): "zyx", (1, 0): "xyz", (1, 1): "yxz"}
for _pair in PAIRS[:-1]:
    for _unit, _order in zip(_pair[-2:], ("zxy", "zyx")):
        ORDERS[_unit] = _order


def forward_schedule(ahead=5):
    events = [(unit, 0) for unit in PAIRS[0]] + [(unit, 0) for unit in LATE]
    for pair in PAIRS[1:ahead]:
        events += [(unit, 0) for unit in pair]
    count = len(PAIRS)
    for step in range(count + 4):
        for stage in (1, 0, None, 2, 3, 4):
            if stage is None:
                if step in (0, 2):
                    events += [(unit, 1 + step // 2) for unit in LATE]
                continue
            index = step + ahead if stage == 0 else step - stage + 1
            if (stage > 0 or index >= ahead) and 0 <= index < count:
                events += [(unit, stage) for unit in PAIRS[index]]
    return events + [(unit, stage) for stage in (3, 4) for unit in LATE]


class Gather:
    def __init__(self, post, mats, down, gains, kept, spot, everyone):
        self.post, self.mats, self.down, self.gains, self.kept = post, mats, down, gains, kept
        self.spot, self.everyone = spot, everyone
        self.events = forward_schedule()
        self.waits, self.near, self.ready = {}, {}, set()

    def at(self, unit, *where):
        if unit == "gains":
            return self.gains.at[where]
        if isinstance(unit, tuple):
            return self.down.at[where + (pl.ds(unit[0] * 48, 48), pl.ds(unit[1] * HALF, HALF))]
        return self.mats.at[(unit,) + where]

    def forward(self, unit, where, targets):
        return [self.post.copy(self.at(unit, *where), self.at(unit, *where), target) for target in targets]

    def run(self, unit, stage):
        z, x, y, c = self.spot
        across, along, sibling = self.everyone[3:]
        order = ORDERS[unit]
        if stage == 0:
            targets = {"z": self.everyone[:3], "x": (across,), "y": (along,)}[order[0]]
            self.near[unit] = []
            self.waits[unit] = self.forward(unit, self.spot, targets)
            return
        if stage == 4:
            arrived(self.near[unit])
            self.ready.add(unit)
            if isinstance(unit, int):
                self.post.local(self.mats.at[unit], self.kept[0].at[unit])
            if unit in ((0, 1), (1, 1)):
                rows = (EVERY,) * 4 + (pl.ds(unit[0] * 48, 48),)
                self.post.local(self.down.at[rows], self.kept[1].at[rows])
            return
        arrived(self.waits[unit])
        steps = {
            "zxy": (
                ((EVERY, x, y, c), (across,), (EVERY, x, y, c)),
                ((EVERY, EVERY, y, c), (along,), (EVERY, 1 - x, y, c)),
                (None, (), (EVERY, EVERY, 1 - y, c)),
            ),
            "zyx": (
                ((EVERY, x, y, c), (along,), (EVERY, x, y, c)),
                ((EVERY, x, EVERY, c), (across,), (EVERY, x, 1 - y, c)),
                (None, (), (EVERY, 1 - x, EVERY, c)),
            ),
            "xyz": (
                ((z, EVERY, y, c), (along,), None),
                ((z, EVERY, EVERY, c), self.everyone[:3], (z, EVERY, EVERY, c)),
                (None, (), "others"),
            ),
            "yxz": (
                ((z, x, EVERY, c), (across,), None),
                ((z, EVERY, EVERY, c), self.everyone[:3], (z, EVERY, EVERY, c)),
                (None, (), "others"),
            ),
        }
        where, targets, near = steps[order][stage - 1]
        self.waits[unit] = self.forward(unit, where, targets) if targets else []
        if near == "others":
            for k in range(3):
                self.near[unit] += self.forward(unit, (z ^ (k + 1), EVERY, EVERY, c), (sibling,))
        elif near is not None:
            self.near[unit] += self.forward(unit, near, (sibling,))

    def pump(self, count):
        for _ in range(count):
            if self.events:
                self.run(*self.events.pop(0))

    def require(self, *units):
        for unit in units:
            while unit not in self.ready:
                self.pump(1)


def forward_kernel(*refs):
    shards, (tokens, memory, cotangent, table, lengths, memory_lengths) = refs[:11], refs[11:17]
    kept_mats, kept_down, gain_rows = refs[17:20]
    (turned, memory_turned, small, keys_out, values_out, self_out, cross_out, hidden_out, slope_out, grads_out) = refs[20:30]
    self_log, cross_log = refs[30:32]
    (gains, mats, down, keep, keys, values, stage, memory_stage, hidden, slope) = refs[32:42]
    (hidden_turned, after_self, after_cross, own_cut, other_cut, grads, near, send, recv) = refs[42:]
    spot = place()
    everyone = partners(*spot)
    sibling = everyone[5]
    post = Post(send, recv, near)
    comm = Gather(post, mats, down, gains, (kept_mats, kept_down), spot, everyone)
    for index in range(8):
        mats.at[(index,) + spot][...] = shards[index][...]
    for index in range(4):
        mats.at[(8 + index,) + spot][...] = shards[8][:, index * 768 : (index + 1) * 768]
    down.at[spot][...] = shards[9][...]
    gains.at[spot][...] = shards[10][...]
    enter(everyone)
    comm.pump(9)
    from_sibling = []

    def turn(block, staged, target, lanes=ROWS):
        staged[...] = block.T
        post.local(staged, target.at[:, pl.ds(0, lanes)])
        from_sibling.append(post.copy(staged, target.at[:, pl.ds(lanes, lanes)], sibling))

    for block in range(4):
        turn(memory[block * ROWS : (block + 1) * ROWS], memory_stage.at[block], memory_turned.at[block])
        comm.pump(1)
    live = lax.broadcasted_iota(jnp.int32, (ROWS, 1), 0) < lengths[0]
    grad_low = jnp.where(live, cotangent[...], jnp.zeros_like(cotangent[...]))
    left, right = grad_low[:, :HALF], grad_low[:, HALF:]
    core = spot[3]
    own_cut[0] = jnp.where(core == 0, left, right)
    other_cut[...] = jnp.where(core == 0, right, left)
    from_sibling.append(post.copy(other_cut, own_cut.at[1], sibling))
    source = tokens[...].astype(FULL)
    inverse = inverse_rms(source)
    one_hot = bucket_rows()
    bias = dot(table[...], one_hot)
    visible = self_mask(lengths[0])
    comm.require("gains")
    gain_rows[...] = jnp.sum(gains[...].astype(FULL).reshape(32, 8, 768), axis=0)
    normed = (source * inverse * gain_rows[0:1]).astype(LOW)
    turn(normed, stage.at[0], turned.at[0])

    def project(unit, slot, block):
        comm.require(unit)
        keep[slot] = dot(block, square(mats, unit)).astype(LOW)
        post.local(keep.at[slot], small.at[slot])

    project(0, 0, normed)
    project(1, 1, normed)
    project(2, 2, normed)

    def attend(pair, head, query, key_block, value_block, extra, log_ref):
        scores = dot_last(key_block, one_head(query, head)) + extra
        peak = jnp.max(scores, axis=0, keepdims=True)
        raised = jnp.exp(scores - peak)
        total = jnp.sum(raised, axis=0, keepdims=True)
        mixed = dot_first(value_block, raised.astype(LOW)) / total
        log_ref[pair * 2 + head : pair * 2 + head + 1] = peak + jnp.log(total)
        return mixed[head * DH : head * DH + DH]

    for pair in range(6):
        span = slice(pair * 128, pair * 128 + 128)
        query = keep[0, :, span] * 0.125
        mixed = [
            attend(
                pair,
                head,
                query,
                keep[1, :, span],
                keep[2, :, span],
                slanted(bias[pair * 2 + head : pair * 2 + head + 1]) + visible,
                self_log,
            )
            for head in range(2)
        ]
        keep[3, :, span] = jnp.concatenate(mixed, axis=0).T.astype(LOW)
        comm.pump(2)
    post.local(keep.at[3], small.at[3])
    context = keep[3]
    turn(context, stage.at[1], turned.at[1])
    comm.require(3)
    after_self[...] = source + dot(context, square(mats, 3))
    post.local(after_self, self_out)
    normed = (after_self[...] * inverse_rms(after_self[...]) * gain_rows[1:2]).astype(LOW)
    turn(normed, stage.at[2], turned.at[2])
    project(4, 4, normed)
    for unit, held, out in ((5, keys, keys_out), (6, values, values_out)):
        comm.require(unit)
        for block in range(4):
            held[block] = dot(memory[block * ROWS : (block + 1) * ROWS], square(mats, unit)).astype(LOW)
        post.local(held, out)
    shown = memory_mask(memory_lengths[0], 1024)
    for pair in range(6):
        span = slice(pair * 128, pair * 128 + 128)
        query = keep[4, :, span] * 0.125
        mixed = [
            attend(pair, head, query, keys[:, :, span].reshape(1024, 128), values[:, :, span].reshape(1024, 128), shown, cross_log) for head in range(2)
        ]
        keep[5, :, span] = jnp.concatenate(mixed, axis=0).T.astype(LOW)
        comm.pump(2)
    post.local(keep.at[5], small.at[5])
    context = keep[5]
    turn(context, stage.at[3], turned.at[3])
    comm.require(7)
    after_cross[...] = after_self[...] + dot(context, square(mats, 7))
    post.local(after_cross, cross_out)
    normed = (after_cross[...] * inverse_rms(after_cross[...]) * gain_rows[2:3]).astype(LOW)
    turn(normed, stage.at[4], turned.at[4])
    root = math.sqrt(2.0 / math.pi)
    for block in range(4):
        comm.require(8 + block)
        before = dot(normed, square(mats, 8 + block))
        squared = before * before
        bent = jnp.tanh(root * before * (1.0 + 0.044715 * squared))
        lifted = 0.5 * (1.0 + bent)
        value = (before * lifted).astype(LOW)
        hidden[block] = value
        slope[block] = (
            lifted + 0.5 * root * before * (1.0 - bent * bent) * (1.0 + 3 * 0.044715 * squared)
        ).astype(LOW)
        post.local(hidden.at[block], hidden_out.at[block])
        post.local(slope.at[block], slope_out.at[block])
        hidden_turned[block, :, :ROWS] = value.T
        half = hidden_turned.at[block, :, pl.ds(0, ROWS)]
        from_sibling.append(post.copy(half, hidden_turned.at[block, :, pl.ds(ROWS, ROWS)], sibling))
        comm.pump(1)
    arrived(from_sibling)
    for block in range(4):
        comm.pump(1)
        grads[block] = dot(hidden_turned[block], own_cut[...].reshape(512, HALF)).astype(LOW).reshape(2, 2, 2, 96, HALF)
        post.local(grads.at[block], grads_out.at[block])
    while comm.events:
        comm.pump(1)
    post.finish()


def forward_call(shards, *rest):
    kind = jax.ShapeDtypeStruct
    anywhere, vmem = pl.BlockSpec(memory_space=pl.ANY), pl.BlockSpec(memory_space=pltpu.VMEM)
    smem = pl.BlockSpec(memory_space=pltpu.SMEM)
    outs = (
        (kind((12, 4, 2, 2, 2, 24, 768), LOW), anywhere),
        (kind((4, 2, 2, 2, 96, 768), LOW), anywhere),
        (kind((8, 768), FULL), vmem),
        (kind((5, 768, 512), LOW), anywhere),
        (kind((4, 768, 512), LOW), anywhere),
        (kind((6, 256, 768), LOW), anywhere),
        (kind((4, 256, 768), LOW), anywhere),
        (kind((4, 256, 768), LOW), anywhere),
        (kind((256, 768), FULL), anywhere),
        (kind((256, 768), FULL), anywhere),
        (kind((4, 256, 768), LOW), anywhere),
        (kind((4, 256, 768), LOW), anywhere),
        (kind((4, 2, 2, 2, 96, HALF), LOW), anywhere),
        (kind((16, 256), FULL), vmem),
        (kind((16, 256), FULL), vmem),
    )
    return pl.pallas_call(
        forward_kernel,
        out_shape=tuple(out[0] for out in outs),
        in_specs=[vmem] * 15 + [smem] * 2,
        out_specs=tuple(out[1] for out in outs),
        scratch_shapes=[
            pltpu.VMEM((4, 2, 2, 2, 8, 768), LOW),
            pltpu.VMEM((12, 4, 2, 2, 2, 24, 768), LOW),
            pltpu.VMEM((4, 2, 2, 2, 96, 768), LOW),
            pltpu.VMEM((6, 256, 768), LOW),
            pltpu.VMEM((4, 256, 768), LOW),
            pltpu.VMEM((4, 256, 768), LOW),
            pltpu.VMEM((5, 768, 256), LOW),
            pltpu.VMEM((4, 768, 256), LOW),
            pltpu.VMEM((4, 256, 768), LOW),
            pltpu.VMEM((4, 256, 768), LOW),
            pltpu.VMEM((4, 768, 512), LOW),
            pltpu.VMEM((256, 768), FULL),
            pltpu.VMEM((256, 768), FULL),
            pltpu.VMEM((2, 256, HALF), LOW),
            pltpu.VMEM((256, HALF), LOW),
            pltpu.VMEM((4, 2, 2, 2, 96, HALF), LOW),
            pltpu.SemaphoreType.DMA((80,)),
            pltpu.SemaphoreType.DMA((180,)),
            pltpu.SemaphoreType.DMA((180,)),
        ],
        compiler_params=pltpu.CompilerParams(
            collective_id=0, has_side_effects=True, vmem_limit_bytes=60 * 2**20
        ),
    )(*shards, *rest)


Z_FIRST = (8, 9)


class Scatter:
    def __init__(self, post, grads, inboxes, done, sums, outs, spot, everyone):
        self.post, self.grads, self.inboxes, self.done, self.sums, self.outs = post, grads, inboxes, done, sums, outs
        self.spot, self.everyone = spot, everyone
        self.queue, self.waits, self.flipped, self.count = [], {(0, "sum"): []}, {}, 0

    def at(self, kind, unit, *where):
        mats, down = kind
        if isinstance(unit, int):
            return mats.at[(unit,) + where]
        where += (EVERY,) * (len(down.shape) - 2 - len(where))
        return down.at[where + (pl.ds(0 if unit == "down0" else 48, 48),)]

    def grad(self, unit, *where):
        return self.at(self.grads, unit, *where)

    def box(self, number, unit, *where):
        return self.at(self.inboxes[number], unit, *where)

    def begin(self, unit):
        z, x, y, c = self.spot
        self.flipped[unit] = self.count % 2 == 1
        self.count += 1
        if unit in Z_FIRST:
            first = Z_FIRST.index(unit)
            self.send(
                unit, 0, [(self.grad(unit, z ^ (k + 1)), self.inboxes[3].at[first, k], self.everyone[k]) for k in range(3)]
            )
        elif self.flipped[unit]:
            self.send(unit, 0, [(self.grad(unit, EVERY, 1 - x, EVERY, EVERY), self.box(0, unit), self.everyone[3])])
        else:
            self.send(unit, 0, [(self.grad(unit, EVERY, EVERY, 1 - y, EVERY), self.box(0, unit), self.everyone[4])])

    def send(self, unit, stage, copies):
        self.waits[unit] = [self.post.copy(*copy) for copy in copies]
        self.queue.append((unit, stage + 1))

    def add(self, target, *terms):
        total = target[...].astype(FULL)
        for term in terms:
            total = total + term[...].astype(FULL)
        target[...] = total.astype(LOW)

    def run(self, unit, stage):
        z, x, y, c = self.spot
        across, along, sibling = self.everyone[3:]
        flipped, early = self.flipped[unit], unit in Z_FIRST
        arrived(self.waits[unit])
        if stage == 1 and early:
            box = self.inboxes[3].at[Z_FIRST.index(unit)]
            self.add(self.grad(unit, z), *(box.at[k] for k in range(3)))
            if flipped:
                source, target = (z, 1 - x, EVERY, EVERY), across
            else:
                source, target = (z, EVERY, 1 - y, EVERY), along
            self.send(unit, 1, [(self.grad(unit, *source), self.box(0, unit, 0), target)])
        if stage == 2 and early:
            if flipped:
                self.add(self.grad(unit, z, x), self.box(0, unit, 0))
                source, target = (z, x, 1 - y, EVERY), along
            else:
                self.add(self.grad(unit, z, EVERY, y), self.box(0, unit, 0))
                source, target = (z, 1 - x, y, EVERY), across
            self.send(unit, 2, [(self.grad(unit, *source), self.box(1, unit, 0), target)])
        if stage == 1 and not early:
            if flipped:
                self.add(self.grad(unit, EVERY, x, EVERY, EVERY), self.box(0, unit))
                source, target = (EVERY, x, 1 - y, EVERY), along
            else:
                self.add(self.grad(unit, EVERY, EVERY, y, EVERY), self.box(0, unit))
                source, target = (EVERY, 1 - x, y, EVERY), across
            self.send(unit, 1, [(self.grad(unit, *source), self.box(1, unit), target)])
        if stage == 2 and not early:
            self.add(self.grad(unit, EVERY, x, y, EVERY), self.box(1, unit))
            self.send(
                unit,
                2,
                [(self.grad(unit, z ^ (k + 1), x, y, EVERY), self.box(2, unit, k), self.everyone[k]) for k in range(3)],
            )
        if stage == 3:
            total = []
            for core in (c, 1 - c):
                part = self.grad(unit, z, x, y, core)[...].astype(FULL)
                for k in range(1 if early else 3):
                    part = part + (self.box(1, unit, 0, core) if early else self.box(2, unit, k, core))[...].astype(FULL)
                total.append(part)
            mine = pl.ds(pl.multiple_of(c * HALF, 128), HALF)
            if isinstance(unit, int):
                target = self.outs[0].at[unit, :, mine]
            else:
                target = self.outs[1].at[pl.ds(0 if unit == "down0" else 48, 48), mine]
            target[...] = total[0]
            self.at(self.done, unit)[...] = total[1]
            self.send(unit, 3, [(self.at(self.done, unit), target, sibling)])

    def small_sum(self, hop):
        sums, boxes = self.sums
        hops = ((self.everyone[4],), (self.everyone[3],), self.everyone[:3], (self.everyone[5],))
        arrived(self.waits[0, "sum"])
        if hop in (1, 2, 4):
            sums[hop] = sums[hop - 1] + boxes[(0, 0, 1, 0, 5)[hop]]
        if hop == 3:
            sums[hop] = (sums[hop - 1] + boxes[2]) + (boxes[3] + boxes[4])
        if hop < 4:
            first = (0, 1, 2, 5)[hop]
            self.waits[0, "sum"] = [
                self.post.copy(sums.at[hop], boxes.at[first + k], target) for k, target in enumerate(hops[hop])
            ]
            self.queue.append(("sum", hop + 1))

    def pump(self, count):
        for _ in range(count):
            if self.queue:
                unit, stage = self.queue.pop(0)
                if unit == "sum":
                    self.small_sum(stage)
                else:
                    self.run(unit, stage)


def rms_back(upstream, field, gain):
    inverse = inverse_rms(field)
    scaled = gain * upstream
    shift = inverse * inverse * inverse * jnp.mean(scaled * field, axis=-1, keepdims=True)
    return inverse * scaled - field * shift, jnp.sum(upstream * field * inverse, axis=0, keepdims=True)


def split_dot(dotted, left, right):
    high = left.astype(LOW)
    return dotted(right, high) + dotted(right, (left - high.astype(FULL)).astype(LOW))


def backward_kernel(*refs):
    (mats, down, turned, memory_turned, grads_in) = refs[:5]
    (keys_in, values_in, hidden_in, slope_in, after_self, after_cross) = refs[5:11]
    (small_in, gains, tokens, cotangent, table, self_log, cross_log) = refs[11:18]
    lengths, memory_lengths = refs[18:20]
    (output, input_grad, memory_grad, mats_out, down_out, extra_out) = refs[20:26]
    (pool_a, pool_b, big, turned_box, wide_a, wide_b, rows_out) = refs[26:33]
    (own_cut, other_cut, own_long, other_long, rows_d, rows_bias, rows_distance) = refs[33:40]
    (grads, grads_down, box_one, box_one_down, box_two, box_two_down, box_three, box_three_down, box_early) = refs[40:49]
    (done, done_down, field, extra, extra_box, stage, small, near, send, recv) = refs[49:]
    spot = z, x, y, c = place()
    everyone = partners(*spot)
    sibling = everyone[5]
    post = Post(send, recv, near)
    comm = Scatter(
        post,
        (grads, grads_down),
        ((box_one, box_one_down), (box_two, box_two_down), (box_three, box_three_down), box_early),
        (done, done_down),
        (extra, extra_box),
        (mats_out, down_out),
        spot,
        everyone,
    )

    def fetch(source, target):
        return post.local(source, target, keep=True)

    def weight(ref, index):
        return ref[index * 32 : index * 32 + 32].reshape(768, 768)

    def fetch_weight(index, pool, slot):
        return fetch(mats.at[pl.ds(index * 32, 32)], pool.at[pl.ds(slot * 32, 32)])

    loads = {
        "grads": fetch(grads_in, grads_down),
        "down": fetch(down, pool_a),
        "slope": fetch(slope_in, wide_b),
        "turned4": fetch(turned.at[4], turned_box.at[0]),
    }

    def need(*names):
        for name in names:
            loads.pop(name).wait()

    def halves(value):
        left, right = value[:, :HALF], value[:, HALF:]
        return jnp.where(c == 0, left, right), jnp.where(c == 0, right, left)

    def whole(mine, other):
        return jnp.concatenate([jnp.where(c == 0, mine, other), jnp.where(c == 0, other, mine)], axis=1)

    hand = {}

    def share(slot, value):
        mine, other = halves(value)
        own_cut[slot, 0] = mine
        other_cut[slot] = other
        hand[slot] = post.copy(other_cut.at[slot], own_cut.at[slot, 1], sibling)

    def shared(slot):
        hand.pop(slot).wait_recv()
        return own_cut[slot].reshape(512, HALF)

    def both(slot):
        return whole(own_cut[slot, 0], other_cut[slot])

    def sum_rows(slot, left, right):
        grads[slot] = dot(left, right).astype(LOW).reshape(4, 2, 2, 2, 24, HALF)

    live = lax.broadcasted_iota(jnp.int32, (ROWS, 1), 0) < lengths[0]
    grad_out = jnp.where(live, cotangent[...].astype(FULL), 0.0)
    grad_low = grad_out.astype(LOW)
    enter(everyone)
    need("grads")
    comm.begin("down0")
    comm.begin("down1")
    need("down", "slope")
    loads["in"] = fetch(mats.at[pl.ds(256, 128)], pool_b)
    loads["hidden"] = fetch(hidden_in, wide_a)
    loads["after_cross"] = fetch(after_cross, field)
    for block in range(4):
        grad_hidden = dot_last(grad_low, weight(pool_a, block))
        share(1 + block, (grad_hidden * wide_b[block].astype(FULL)).astype(LOW))
    loads["turned3"] = fetch(turned.at[3], turned_box.at[1])
    loads["values"] = fetch(values_in, wide_b)
    need("turned4")
    for block in range(4):
        sum_rows(8 + block, turned_box[0], shared(1 + block))
        comm.begin(8 + block)
    loads["turned1"] = fetch(turned.at[1], turned_box.at[0])
    need("hidden", "after_cross", "in")
    total = field[...]
    for block in range(4):
        total = total + dot(wide_a[block], weight(pool_a, block))
    output[...] = total.astype(LOW)
    comm.pump(1)
    loads["keys"] = fetch(keys_in, wide_a)
    for slot, index in enumerate((7, 4, 5, 6)):
        loads[index] = fetch_weight(index, pool_a, slot)
    loads["small"] = fetch(small_in, small)
    loads["turned2"] = fetch(turned.at[2], turned_box.at[2])
    loads["memory_turned"] = fetch(memory_turned, big)
    upstream = 0.0
    for block in range(4):
        upstream = upstream + dot_last(both(1 + block), weight(pool_b, block))
    for slot, index in enumerate((3, 0, 1, 2)):
        loads[index] = fetch_weight(index, pool_b, slot)
    step, gain_three = rms_back(upstream, field[...], gains[2:3])
    extra[0] = jnp.zeros((8, 768), FULL)
    extra[0, 2:3] = gain_three
    input_grad[...] = grad_out + step
    grad_low = input_grad[...].astype(LOW)
    share(5, grad_low)
    loads["after_self"] = fetch(after_self, field)
    need(7)
    upstream = dot_last(grad_low, weight(pool_a, 0)).astype(LOW)
    need("turned3")
    sum_rows(7, turned_box[1], shared(5))
    comm.begin(7)
    loads["turned0"] = fetch(turned.at[0], turned_box.at[1])

    heads = (
        lax.broadcasted_iota(jnp.int32, (16, 768), 1) // DH == lax.broadcasted_iota(jnp.int32, (16, 768), 0)
    ).astype(LOW)

    def inner_rows(context):
        rows_d[...] = split_dot(dot_last, upstream_ref[...].astype(FULL) * context.astype(FULL), heads)

    upstream_ref = stage
    upstream_ref[...] = upstream
    need("small")
    inner_rows(small[5])

    def attend_back(pair, query_block, key_block, value_block, log_ref, extra_of, visit):
        span = pl.ds(pl.multiple_of(pair * 128, 128), 128)
        query, handed = query_block(span) * 0.125, upstream_ref[:, span]
        grad_values, grad_keys, grad_query = 0.0, 0.0, []
        key_block, value_block = key_block(span), value_block(span)
        for head in range(2):
            row = pl.ds(pair * 2 + head, 1)
            query_part, handed_part = one_head(query, head), one_head(handed, head)
            attended = jnp.exp(dot_last(key_block, query_part) + extra_of(row) - log_ref[row])
            grad_scores = attended * (dot_last(value_block, handed_part) - rows_d[row])
            visit(row, grad_scores)
            rounded = grad_scores.astype(LOW)
            grad_values = grad_values + dot(attended.astype(LOW), handed_part)
            grad_keys = grad_keys + dot(rounded, query_part)
            grad_query.append(dot_first(key_block, rounded)[head * DH : head * DH + DH])
        grad_query = jnp.concatenate(grad_query, axis=0).T * 0.125
        return grad_query.astype(LOW), grad_keys.astype(LOW), grad_values.astype(LOW)

    need("keys", "values")
    shown = memory_mask(memory_lengths[0], 1024)
    for turn in range(6):
        mine, lane = turn >= 3, slice(turn % 3 * 128, turn % 3 * 128 + 128)
        pair = (c if mine else 1 - c) * 3 + turn % 3
        grad_query, grad_keys, grad_values = attend_back(
            pair,
            lambda span: small[4, :, span],
            lambda span: wide_a[:, :, span].reshape(1024, 128),
            lambda span: wide_b[:, :, span].reshape(1024, 128),
            cross_log,
            lambda row: shown,
            lambda row, value: None,
        )
        grad_keys, grad_values = grad_keys.reshape(4, ROWS, 128), grad_values.reshape(4, ROWS, 128)
        if mine:
            own_cut[6, 0, :, lane] = grad_query
            own_long[0, :, 0, :, lane] = grad_keys
            own_long[1, :, 0, :, lane] = grad_values
        else:
            other_cut[6, :, lane] = grad_query
            other_long[0, :, :, lane] = grad_keys
            other_long[1, :, :, lane] = grad_values
        if turn == 2:
            hand[6] = post.copy(other_cut.at[6], own_cut.at[6, 1], sibling)
            for kind in range(2):
                hand["long", kind] = post.copy(other_long.at[kind], own_long.at[kind, :, 1], sibling)
        comm.pump(1)
    need(4, 5, 6)
    need("turned2", "after_self")
    upstream = dot_last(both(6), weight(pool_a, 1))
    step, gain_two = rms_back(upstream, field[...], gains[1:2])
    extra[0, 1:2] = gain_two
    input_grad[...] = input_grad[...] + step
    grad_low = input_grad[...].astype(LOW)
    share(7, grad_low)
    comm.pump(1)
    need("memory_turned")
    for kind, unit in ((0, 5), (1, 6)):
        hand.pop(("long", kind)).wait_recv()
        total = 0.0
        for block in range(4):
            total = total + dot(big[block], own_long[kind, block].reshape(512, HALF))
        grads[unit] = total.astype(LOW).reshape(4, 2, 2, 2, 24, HALF)
        comm.begin(unit)
        comm.pump(1)
    sum_rows(4, turned_box[2], shared(6))
    comm.begin(4)
    comm.pump(1)
    need(3, "turned1")
    upstream_ref[...] = dot_last(grad_low, weight(pool_b, 0)).astype(LOW)
    inner_rows(small[3])
    sum_rows(3, turned_box[0], shared(7))
    comm.begin(3)
    one_hot = bucket_rows()
    rows_bias[0:12] = dot(table[...], one_hot)
    visible = self_mask(lengths[0])

    def by_distance(row, value):
        eight = value[:8]
        for first in range(8, ROWS, 8):
            eight = eight + pltpu.roll(value[first : first + 8], ROWS - first, 1)
        total = eight[:1]
        for first in range(1, 8):
            total = total + pltpu.roll(eight, ROWS - first, 1)[first : first + 1]
        rows_distance[row] = total

    rows_distance[...] = jnp.zeros((16, ROWS), FULL)
    for turn in range(6):
        mine, lane = turn >= 3, slice(turn % 3 * 128, turn % 3 * 128 + 128)
        pair = (c if mine else 1 - c) * 3 + turn % 3
        parts = attend_back(
            pair,
            lambda span: small[0, :, span],
            lambda span: small[1, :, span],
            lambda span: small[2, :, span],
            self_log,
            lambda row: slanted(rows_bias[row]) + visible,
            by_distance,
        )
        for slot, part in zip((8, 9, 10), parts):
            if mine:
                own_cut[slot, 0, :, lane] = part
            else:
                other_cut[slot, :, lane] = part
        if turn == 2:
            for slot in (8, 9, 10):
                hand[slot] = post.copy(other_cut.at[slot], own_cut.at[slot, 1], sibling)
        comm.pump(1 + turn % 2)
    need("turned0", 0, 1, 2)
    for unit in range(3):
        sum_rows(unit, turned_box[1], shared(8 + unit))
        comm.begin(unit)
        comm.pump(2)
    upstream = 0.0
    for unit in range(3):
        upstream = upstream + dot_last(both(8 + unit), weight(pool_b, 1 + unit))
    step, gain_one = rms_back(upstream, tokens[...].astype(FULL), gains[0:1])
    extra[0, 0:1] = gain_one
    high = rows_distance[...].astype(LOW)
    many = jnp.concatenate([one_hot] * 16, axis=0)
    sums = dot_last(high, many) + dot_last((rows_distance[...] - high.astype(FULL)).astype(LOW), many)
    own_head = lax.broadcasted_iota(jnp.int32, (16, 512), 1) // NB == lax.broadcasted_iota(jnp.int32, (16, 512), 0)
    extra[0, 3:4, :512] = jnp.sum(jnp.where(own_head, sums, 0.0), axis=0, keepdims=True)
    input_grad[...] = input_grad[...] + step
    comm.small_sum(0)
    shown_rows = []
    for block in range(4):
        comm.pump(3)
        if block >= 2:
            shown_rows[block - 2].wait()
        rows_out[block % 2] = dot_last(
            whole(own_long[0, block, 0], other_long[0, block]), weight(pool_a, 2)
        ) + dot_last(whole(own_long[1, block, 0], other_long[1, block]), weight(pool_a, 3))
        shown_rows.append(fetch(rows_out.at[block % 2], memory_grad.at[pl.ds(block * ROWS, ROWS)]))
    while comm.queue:
        comm.pump(1)
    for made in shown_rows[2:]:
        made.wait()
    extra_out[...] = extra[4]
    post.finish()


def backward_call(*args):
    kind = jax.ShapeDtypeStruct
    anywhere, vmem = pl.BlockSpec(memory_space=pl.ANY), pl.BlockSpec(memory_space=pltpu.VMEM)
    smem = pl.BlockSpec(memory_space=pltpu.SMEM)
    vm, dma = pltpu.VMEM, pltpu.SemaphoreType.DMA
    return pl.pallas_call(
        backward_kernel,
        out_shape=(
            kind((256, 768), LOW),
            kind((256, 768), FULL),
            kind((1024, 768), FULL),
            kind((12, 24, 768), FULL),
            kind((96, 768), FULL),
            kind((8, 768), FULL),
        ),
        in_specs=[anywhere] * 12 + [vmem] * 6 + [smem] * 2,
        out_specs=(vmem, vmem, anywhere, vmem, vmem, vmem),
        scratch_shapes=[
            vm((128, 24, 768), LOW),
            vm((128, 24, 768), LOW),
            vm((4, 768, 512), LOW),
            vm((3, 768, 512), LOW),
            vm((4, 256, 768), LOW),
            vm((4, 256, 768), LOW),
            vm((2, 256, 768), FULL),
            vm((11, 2, 256, HALF), LOW),
            vm((11, 256, HALF), LOW),
            vm((2, 4, 2, 256, HALF), LOW),
            vm((2, 4, 256, HALF), LOW),
            vm((16, 256), FULL),
            vm((16, 256), FULL),
            vm((16, 256), FULL),
            vm((12, 4, 2, 2, 2, 24, HALF), LOW),
            vm((4, 2, 2, 2, 96, HALF), LOW),
            vm((12, 4, 2, 2, 24, HALF), LOW),
            vm((4, 2, 2, 96, HALF), LOW),
            vm((12, 4, 2, 24, HALF), LOW),
            vm((4, 2, 96, HALF), LOW),
            vm((12, 3, 2, 24, HALF), LOW),
            vm((3, 2, 96, HALF), LOW),
            vm((len(Z_FIRST), 3, 2, 2, 2, 24, HALF), LOW),
            vm((12, 24, HALF), FULL),
            vm((96, HALF), FULL),
            vm((256, 768), FULL),
            vm((5, 8, 768), FULL),
            vm((6, 8, 768), FULL),
            vm((256, 768), LOW),
            vm((6, 256, 768), LOW),
            dma((60,)),
            dma((150,)),
            dma((150,)),
        ],
        compiler_params=pltpu.CompilerParams(
            collective_id=1, has_side_effects=True, vmem_limit_bytes=60 * 2**20
        ),
    )(*args)


def finish_kernel(*refs):
    (output, input_grad, memory_grad, mats, down, extra), outs = refs[:6], refs[6:]
    for source, target in zip((output, input_grad, memory_grad, down), outs):
        target[...] = source[...]
    for index in range(8):
        outs[4 + index][...] = mats[index]
    for index in range(4):
        outs[12][:, index * 768 : (index + 1) * 768] = mats[8 + index]
    rank = lax.axis_index(AXES[0]) * lax.axis_size(AXES[1]) + lax.axis_index(AXES[1])
    own = pltpu.roll(extra[...], 768 - rank * 24, 1)
    for index in range(3):
        outs[13 + index][...] = own[index : index + 1, :24]
    for head in range(12):
        outs[16][head : head + 1] = extra[3:4, head * NB : head * NB + NB]


def finish(*args):
    kind = jax.ShapeDtypeStruct
    block = lambda *shape: pl.BlockSpec(shape, lambda step: (step, 0))
    whole = lambda *shape: pl.BlockSpec(shape, lambda step: (0,) * len(shape))
    rows = [block(64, 768), block(64, 768), block(256, 768)]
    single = [(96, 768)] + [(24, 768)] * 8 + [(24, 3072)] + [(1, 24)] * 3 + [(12, NB)]
    return pl.pallas_call(
        finish_kernel,
        grid=(4,),
        out_shape=(
            kind((256, 768), LOW),
            kind((256, 768), FULL),
            kind((1024, 768), FULL),
            *[kind(shape, FULL) for shape in single],
        ),
        in_specs=rows + [whole(12, 24, 768), whole(96, 768), whole(8, 768)],
        out_specs=rows + [whole(*shape) for shape in single],
    )(*args)


def plain_body(
    tokens,
    memory,
    cotangent,
    target_lengths,
    memory_lengths,
    self_gain,
    self_query,
    self_key,
    self_value,
    self_out,
    position_table,
    cross_gain,
    cross_query,
    cross_key,
    cross_value,
    cross_out,
    ffn_gain,
    ffn_in,
    ffn_out,
):
    wide_count = lax.axis_size(AXES[0])
    narrow_count = lax.axis_size(AXES[1])
    devices = wide_count * narrow_count
    seq_count = target_lengths.shape[0]
    target_rows = tokens.shape[0] // seq_count
    memory_rows = memory.shape[0] // seq_count
    positions = jnp.arange(target_rows, dtype=jnp.int32)
    live_rows = positions[None, :] < target_lengths[:, None]
    causal = positions[None, :] <= positions[:, None]
    self_visible = causal[None] & live_rows[:, None, :]
    memory_visible = (jnp.arange(memory_rows, dtype=jnp.int32)[None, :] < memory_lengths[:, None])[
        :, None, :
    ]
    grad_out = jnp.where(live_rows.reshape(-1, 1), cotangent.astype(jnp.float32), 0.0)
    bucket = bucket_index(target_rows)
    one_hot = (bucket[:, :, None] == jnp.arange(NB, dtype=jnp.int32)[None, None, :]).astype(
        jnp.float32
    )
    relative = jnp.einsum(
        "ijb,bh->hij", one_hot, position_table.astype(jnp.float32), precision=lax.Precision.HIGHEST
    )
    gain_one, weight_query, weight_key, weight_value, weight_out = (
        lax.all_gather(self_gain, AXES, axis=0, tiled=True),
        lax.all_gather(self_query, AXES, axis=0, tiled=True),
        lax.all_gather(self_key, AXES, axis=0, tiled=True),
        lax.all_gather(self_value, AXES, axis=0, tiled=True),
        lax.all_gather(self_out, AXES, axis=0, tiled=True),
    )
    source = tokens.astype(jnp.float32)
    normed_value, norm_back_one = jax.vjp(rms_apply, source, gain_one.astype(jnp.float32))
    normed_one = normed_value.astype(jnp.bfloat16)
    query_one = product(normed_one, weight_query).astype(jnp.bfloat16)
    keys_one = product(normed_one, weight_key).astype(jnp.bfloat16)
    values_one = product(normed_one, weight_value).astype(jnp.bfloat16)
    context_one, totals_one = attend_forward(
        query_one, keys_one, values_one, relative, self_visible, seq_count
    )
    after_self = source + product(context_one, weight_out)
    gain_two, cross_weight_query, cross_weight_key, cross_weight_value, cross_weight_out = (
        lax.all_gather(cross_gain, AXES, axis=0, tiled=True),
        lax.all_gather(cross_query, AXES, axis=0, tiled=True),
        lax.all_gather(cross_key, AXES, axis=0, tiled=True),
        lax.all_gather(cross_value, AXES, axis=0, tiled=True),
        lax.all_gather(cross_out, AXES, axis=0, tiled=True),
    )
    normed_value, norm_back_two = jax.vjp(rms_apply, after_self, gain_two.astype(jnp.float32))
    normed_two = normed_value.astype(jnp.bfloat16)
    query_two = product(normed_two, cross_weight_query).astype(jnp.bfloat16)
    keys_two = product(memory, cross_weight_key).astype(jnp.bfloat16)
    values_two = product(memory, cross_weight_value).astype(jnp.bfloat16)
    context_two, totals_two = attend_forward(
        query_two, keys_two, values_two, None, memory_visible, seq_count
    )
    after_cross = after_self + product(context_two, cross_weight_out)
    gain_three, weight_in, weight_down = (
        lax.all_gather(ffn_gain, AXES, axis=0, tiled=True),
        lax.all_gather(ffn_in, AXES, axis=0, tiled=True),
        lax.all_gather(ffn_out, AXES, axis=0, tiled=True),
    )
    normed_value, norm_back_three = jax.vjp(rms_apply, after_cross, gain_three.astype(jnp.float32))
    normed_three = normed_value.astype(jnp.bfloat16)
    before = product(normed_three, weight_in)
    gelu_value, gelu_back = jax.vjp(gelu_smooth, before)
    hidden = gelu_value.astype(jnp.bfloat16)
    output = (after_cross + product(hidden, weight_down)).astype(jnp.bfloat16)
    back_in, back_down = (
        lax.all_gather(ffn_in, AXES, axis=0, tiled=True),
        lax.all_gather(ffn_out, AXES, axis=0, tiled=True),
    )
    grad_low = grad_out.astype(jnp.bfloat16)
    grad_down_weight = outer_sum(hidden, grad_low)
    grad_hidden = back_project(grad_low, back_down)
    grad_before = gelu_back(grad_hidden)[0].astype(jnp.bfloat16)
    grad_in_weight = outer_sum(normed_three, grad_before)
    grad_normed_three = back_project(grad_before, back_in)
    grad_cross_part, grad_gain_three = norm_back_three(grad_normed_three)
    grad_cross = grad_out + grad_cross_part
    ffn_terms = (grad_gain_three, grad_in_weight, grad_down_weight)
    summed_ffn = lax.psum_scatter(
        pack_rows(ffn_terms, devices), AXES, scatter_dimension=0, tiled=True
    )
    ffn_gain_grad, ffn_in_grad, ffn_out_grad = unpack_rows(summed_ffn[0], ffn_terms, devices)
    back_cross_query, back_cross_key, back_cross_value, back_cross_out = (
        lax.all_gather(cross_query, AXES, axis=0, tiled=True),
        lax.all_gather(cross_key, AXES, axis=0, tiled=True),
        lax.all_gather(cross_value, AXES, axis=0, tiled=True),
        lax.all_gather(cross_out, AXES, axis=0, tiled=True),
    )
    grad_cross_low = grad_cross.astype(jnp.bfloat16)
    grad_cross_out_weight = outer_sum(context_two, grad_cross_low)
    grad_context_two = back_project(grad_cross_low, back_cross_out).astype(jnp.bfloat16)
    grad_query_two, grad_keys_two, grad_values_two, unused_extra = attend_backward(
        query_two,
        keys_two,
        values_two,
        None,
        memory_visible,
        seq_count,
        totals_two,
        grad_context_two,
    )
    grad_cross_query_weight = outer_sum(normed_two, grad_query_two)
    grad_cross_key_weight = outer_sum(memory, grad_keys_two)
    grad_cross_value_weight = outer_sum(memory, grad_values_two)
    memory_grad = back_project(grad_keys_two, back_cross_key) + back_project(
        grad_values_two, back_cross_value
    )
    grad_self_part, grad_gain_two = norm_back_two(back_project(grad_query_two, back_cross_query))
    grad_self = grad_cross + grad_self_part
    cross_terms = (
        grad_gain_two,
        grad_cross_query_weight,
        grad_cross_key_weight,
        grad_cross_value_weight,
        grad_cross_out_weight,
    )
    summed_cross = lax.psum_scatter(
        pack_rows(cross_terms, devices), AXES, scatter_dimension=0, tiled=True
    )
    cross_gain_grad, cross_query_grad, cross_key_grad, cross_value_grad, cross_out_grad = (
        unpack_rows(summed_cross[0], cross_terms, devices)
    )
    back_query, back_key, back_value, back_out = (
        lax.all_gather(self_query, AXES, axis=0, tiled=True),
        lax.all_gather(self_key, AXES, axis=0, tiled=True),
        lax.all_gather(self_value, AXES, axis=0, tiled=True),
        lax.all_gather(self_out, AXES, axis=0, tiled=True),
    )
    grad_self_low = grad_self.astype(jnp.bfloat16)
    grad_out_weight = outer_sum(context_one, grad_self_low)
    grad_context_one = back_project(grad_self_low, back_out).astype(jnp.bfloat16)
    grad_query_one, grad_keys_one, grad_values_one, grad_relative = attend_backward(
        query_one,
        keys_one,
        values_one,
        relative,
        self_visible,
        seq_count,
        totals_one,
        grad_context_one,
    )
    table_term = jnp.einsum("hij,ijb->bh", grad_relative, one_hot, precision=lax.Precision.HIGHEST)
    position_table_grad = lax.psum(table_term, AXES)
    grad_query_weight = outer_sum(normed_one, grad_query_one)
    grad_key_weight = outer_sum(normed_one, grad_keys_one)
    grad_value_weight = outer_sum(normed_one, grad_values_one)
    grad_normed_one = (
        back_project(grad_query_one, back_query)
        + back_project(grad_keys_one, back_key)
        + back_project(grad_values_one, back_value)
    )
    grad_source_part, grad_gain_one = norm_back_one(grad_normed_one)
    input_grad = grad_self + grad_source_part
    self_terms = (
        grad_gain_one,
        grad_query_weight,
        grad_key_weight,
        grad_value_weight,
        grad_out_weight,
    )
    summed_self = lax.psum_scatter(
        pack_rows(self_terms, devices), AXES, scatter_dimension=0, tiled=True
    )
    self_gain_grad, self_query_grad, self_key_grad, self_value_grad, self_out_grad = unpack_rows(
        summed_self[0], self_terms, devices
    )
    return (
        output,
        input_grad,
        memory_grad,
        self_gain_grad,
        self_query_grad,
        self_key_grad,
        self_value_grad,
        self_out_grad,
        position_table_grad,
        cross_gain_grad,
        cross_query_grad,
        cross_key_grad,
        cross_value_grad,
        cross_out_grad,
        ffn_gain_grad,
        ffn_in_grad,
        ffn_out_grad,
    )


def body(
    tokens,
    memory,
    cotangent,
    target_lengths,
    memory_lengths,
    self_gain,
    self_query,
    self_key,
    self_value,
    self_out,
    position_table,
    cross_gain,
    cross_query,
    cross_key,
    cross_value,
    cross_out,
    ffn_gain,
    ffn_in,
    ffn_out,
):
    rank = lax.axis_index(AXES[0]) * lax.axis_size(AXES[1]) + lax.axis_index(AXES[1])
    own_gains = jnp.stack([self_gain, cross_gain, ffn_gain])
    spread = lax.dynamic_update_slice(jnp.zeros((8, 768), LOW), own_gains, (0, rank * 24))
    shards = (self_query, self_key, self_value, self_out, cross_query, cross_key, cross_value, cross_out, ffn_in, ffn_out)
    (
        mats,
        down,
        gains,
        turned,
        memory_turned,
        small,
        keys,
        values,
        after_self,
        after_cross,
        hidden,
        slope,
        down_grads,
        self_log,
        cross_log,
    ) = forward_call(
        shards + (spread,), tokens, memory, cotangent, position_table.T, target_lengths, memory_lengths
    )
    output, input_grad, memory_grad, mats_grad, down_grad, extra = backward_call(
        mats.reshape(384, 24, 768),
        down.reshape(128, 24, 768),
        turned,
        memory_turned,
        down_grads,
        keys,
        values,
        hidden,
        slope,
        after_self,
        after_cross,
        small,
        gains,
        tokens,
        cotangent,
        position_table.T,
        self_log,
        cross_log,
        target_lengths,
        memory_lengths,
    )
    output, input_grad, memory_grad, down_grad, *square_grads, ffn_in_grad, gain_one, gain_two, gain_three, table = finish(
        output, input_grad, memory_grad, mats_grad, down_grad, extra
    )
    return (
        output,
        input_grad,
        memory_grad,
        gain_one.reshape(24),
        *square_grads[:4],
        table.T,
        gain_two.reshape(24),
        *square_grads[4:],
        gain_three.reshape(24),
        ffn_in_grad,
        down_grad,
    )


def solution(mesh):
    whole = (mesh.shape[AXES[0]], mesh.shape[AXES[1]]) == (8, 4)
    placed = (
        P(AXES, None),
        P(AXES, None),
        P(AXES, None),
        P(AXES),
        P(AXES),
        P(AXES),
        P(AXES, None),
        P(AXES, None),
        P(AXES, None),
        P(AXES, None),
        P(),
        P(AXES),
        P(AXES, None),
        P(AXES, None),
        P(AXES, None),
        P(AXES, None),
        P(AXES),
        P(AXES, None),
        P(AXES, None),
    )
    return jax.shard_map(
        body if whole else plain_body,
        mesh=mesh,
        in_specs=placed,
        out_specs=(
            P(AXES, None),
            P(AXES, None),
            P(AXES, None),
            P(AXES),
            P(AXES, None),
            P(AXES, None),
            P(AXES, None),
            P(AXES, None),
            P(),
            P(AXES),
            P(AXES, None),
            P(AXES, None),
            P(AXES, None),
            P(AXES, None),
            P(AXES),
            P(AXES, None),
            P(AXES, None),
        ),
        check_vma=False,
    )
```

```python
import math

import jax
import jax.numpy as jnp
from jax import lax
from jax.experimental import pallas as pl
from jax.experimental.pallas import tpu as pltpu
from jax.sharding import PartitionSpec as P

DH = 64
NB = 32
MAXDIST = 128


AXES = ("wide", "narrow")
EPSILON = 1e-06
NEGATIVE = -1e30


def bucket_index(length):
    offsets = jnp.arange(length, dtype=jnp.int32)
    distance = jnp.maximum(offsets[:, None] - offsets[None, :], 0)
    exact_part = NB // 2
    bucket = jnp.minimum(distance, exact_part)
    for step in range(1, NB - exact_part):
        bound = math.ceil(exact_part * (MAXDIST / exact_part) ** (step / (NB - exact_part)))
        bucket = bucket + (distance >= bound).astype(jnp.int32)
    return bucket


def rms_apply(field, gain):
    inverse = lax.rsqrt(jnp.mean(field * field, axis=-1, keepdims=True) + EPSILON)
    return field * inverse * gain


def gelu_smooth(field):
    return jax.nn.gelu(field, approximate=True)


def product(left, right):
    return jnp.dot(left, right, preferred_element_type=jnp.float32)


def outer_sum(left, right):
    return jnp.einsum("rd,re->de", left, right, preferred_element_type=jnp.float32)


def back_project(left, right):
    return jnp.einsum("re,de->rd", left, right, preferred_element_type=jnp.float32)


def pack_rows(arrays, devices):
    return jnp.concatenate([array.reshape(devices, -1) for array in arrays], axis=1)


def unpack_rows(packed_row, arrays, devices):
    results = []
    offset = 0
    for array in arrays:
        shard_shape = (array.shape[0] // devices,) + array.shape[1:]
        count = array.size // devices
        results.append(packed_row[offset : offset + count].reshape(shard_shape))
        offset = offset + count
    return tuple(results)


def head_blocks(array, index, seq_count):
    block = lax.dynamic_slice_in_dim(array, index * 2 * DH, 2 * DH, 1)
    return block.reshape(seq_count, -1, 2, DH)


def flat_block(block):
    return block.reshape(-1, 2 * DH)


def scored(query_block, keys_block, extra, visible, index):
    scores = jnp.einsum(
        "sqhd,skhd->shqk", query_block, keys_block, preferred_element_type=jnp.float32
    ) * DH ** (-0.5)
    if extra is not None:
        scores = scores + lax.dynamic_slice_in_dim(extra, index * 2, 2, 0)[None]
    return jnp.where(visible[:, None], scores, NEGATIVE)


def attend_forward(query, keys, values, extra, visible, seq_count):
    pairs = query.shape[1] // (2 * DH)
    start_context = jnp.zeros(query.shape, jnp.bfloat16)
    start_totals = jnp.zeros((seq_count, 2 * pairs, query.shape[0] // seq_count), jnp.float32)

    def one_pair(index, carry):
        context, log_total = carry
        query_block = head_blocks(query, index, seq_count)
        scores = scored(query_block, head_blocks(keys, index, seq_count), extra, visible, index)
        peak = jnp.max(scores, axis=-1, keepdims=True)
        raised = jnp.exp(scores - peak)
        total = jnp.sum(raised, axis=-1, keepdims=True)
        attend = (raised / total).astype(jnp.bfloat16)
        mixed = jnp.einsum(
            "shqk,skhd->sqhd",
            attend,
            head_blocks(values, index, seq_count),
            preferred_element_type=jnp.float32,
        )
        context = lax.dynamic_update_slice_in_dim(
            context, flat_block(mixed.astype(jnp.bfloat16)), index * 2 * DH, 1
        )
        log_total = lax.dynamic_update_slice_in_dim(
            log_total, (peak + jnp.log(total))[..., 0], index * 2, 1
        )
        return (context, log_total)

    return lax.fori_loop(0, pairs, one_pair, (start_context, start_totals))


def attend_backward(query, keys, values, extra, visible, seq_count, log_total, grad_context):
    pairs = query.shape[1] // (2 * DH)
    scale = DH ** (-0.5)
    extra_shape = extra.shape if extra is not None else (1,)
    start_grads = (
        jnp.zeros(query.shape, jnp.bfloat16),
        jnp.zeros(keys.shape, jnp.bfloat16),
        jnp.zeros(values.shape, jnp.bfloat16),
        jnp.zeros(extra_shape, jnp.float32),
    )

    def one_pair(index, carry):
        grad_query, grad_keys, grad_values, grad_extra = carry
        query_block = head_blocks(query, index, seq_count)
        keys_block = head_blocks(keys, index, seq_count)
        value_block = head_blocks(values, index, seq_count)
        upstream = head_blocks(grad_context, index, seq_count)
        scores = scored(query_block, keys_block, extra, visible, index)
        attend = jnp.exp(scores - lax.dynamic_slice_in_dim(log_total, index * 2, 2, 1)[..., None])
        grad_attend = jnp.einsum(
            "sqhd,skhd->shqk", upstream, value_block, preferred_element_type=jnp.float32
        )
        value_grad = jnp.einsum(
            "shqk,sqhd->skhd",
            attend.astype(jnp.bfloat16),
            upstream,
            preferred_element_type=jnp.float32,
        ).astype(jnp.bfloat16)
        inner = jnp.sum(attend * grad_attend, axis=-1, keepdims=True)
        grad_score = attend * (grad_attend - inner)
        rounded = grad_score.astype(jnp.bfloat16)
        query_grad = (
            jnp.einsum("shqk,skhd->sqhd", rounded, keys_block, preferred_element_type=jnp.float32)
            * scale
        ).astype(jnp.bfloat16)
        keys_grad = (
            jnp.einsum("shqk,sqhd->skhd", rounded, query_block, preferred_element_type=jnp.float32)
            * scale
        ).astype(jnp.bfloat16)
        offset = index * 2 * DH
        grad_query = lax.dynamic_update_slice_in_dim(grad_query, flat_block(query_grad), offset, 1)
        grad_keys = lax.dynamic_update_slice_in_dim(grad_keys, flat_block(keys_grad), offset, 1)
        grad_values = lax.dynamic_update_slice_in_dim(
            grad_values, flat_block(value_grad), offset, 1
        )
        if extra is not None:
            grad_extra = lax.dynamic_update_slice_in_dim(
                grad_extra, jnp.sum(grad_score, axis=0), index * 2, 0
            )
        return (grad_query, grad_keys, grad_values, grad_extra)

    return lax.fori_loop(0, pairs, one_pair, start_grads)


MESH = pl.DeviceIdType.MESH
HALF = 384
ROWS = 256
LOW, FULL = jnp.bfloat16, jnp.float32
EVERY = slice(None)


def place():
    wide = lax.axis_index(AXES[0])
    narrow = lax.axis_index(AXES[1])
    return wide // 2, lax.rem(wide, 2), narrow // 2, lax.rem(narrow, 2)


def device(z, x, y, c):
    return (z * 2 + x, y * 2 + c)


def partners(z, x, y, c):
    return (
        device(z ^ 1, x, y, c),
        device(z ^ 2, x, y, c),
        device(z ^ 3, x, y, c),
        device(z, 1 - x, y, c),
        device(z, x, 1 - y, c),
        device(z, x, y, 1 - c),
    )


def enter(everyone):
    barrier = pltpu.get_barrier_semaphore()
    for other in everyone:
        pl.semaphore_signal(barrier, inc=1, device_id=other, device_id_type=MESH)
    pl.semaphore_wait(barrier, len(everyone))


class Post:
    def __init__(self, send, recv, near):
        self.send, self.recv, self.near = send, recv, near
        self.used, self.used_near, self.started, self.open = 0, 0, [], []

    def copy(self, source, target, where):
        made = pltpu.make_async_remote_copy(
            src_ref=source,
            dst_ref=target,
            send_sem=self.send.at[self.used],
            recv_sem=self.recv.at[self.used],
            device_id=where,
            device_id_type=MESH,
        )
        self.used += 1
        made.start()
        self.started.append(made)
        return made

    def local(self, source, target, keep=False):
        made = pltpu.make_async_copy(source, target, self.near.at[self.used_near])
        self.used_near += 1
        made.start()
        if not keep:
            self.open.append(made)
        return made

    def finish(self):
        for made in self.started:
            made.wait_send()
        for made in self.open:
            made.wait()


def arrived(copies):
    for made in copies:
        made.wait_recv()


def dot(left, right):
    return jnp.dot(left, right, preferred_element_type=FULL)


def dot_last(left, right):
    return lax.dot_general(left, right, (((1,), (1,)), ((), ())), preferred_element_type=FULL)


def dot_first(left, right):
    return lax.dot_general(left, right, (((0,), (0,)), ((), ())), preferred_element_type=FULL)


def square(ref, index):
    return ref[index].reshape(768, 768)


def bucket_rows():
    distance = lax.broadcasted_iota(jnp.int32, (NB, ROWS), 1)
    row = lax.broadcasted_iota(jnp.int32, (NB, ROWS), 0)
    exact_part = NB // 2
    bucket = jnp.minimum(distance, exact_part)
    for step in range(1, NB - exact_part):
        bound = math.ceil(exact_part * (MAXDIST / exact_part) ** (step / (NB - exact_part)))
        bucket = bucket + (distance >= bound).astype(jnp.int32)
    return (bucket == row).astype(LOW)


def self_mask(length):
    key = lax.broadcasted_iota(jnp.int32, (ROWS, ROWS), 0)
    query = lax.broadcasted_iota(jnp.int32, (ROWS, ROWS), 1)
    return jnp.where((key <= query) & (key < length), 0.0, NEGATIVE)


def memory_mask(length, rows):
    key = lax.broadcasted_iota(jnp.int32, (rows, 1), 0)
    return jnp.where(key < length, 0.0, NEGATIVE)


def slanted(row):
    return pltpu.roll(jnp.broadcast_to(row, (ROWS, ROWS)), 0, 1, stride=1, stride_axis=0)


def one_head(block, head):
    lane = lax.broadcasted_iota(jnp.int32, block.shape, 1)
    return jnp.where((lane < DH) if head == 0 else (lane >= DH), block, jnp.zeros_like(block))


def inverse_rms(field):
    return lax.rsqrt(jnp.mean(field * field, axis=-1, keepdims=True) + EPSILON)


PAIRS = [("gains", 0, 1), (2, 3), (4, 7), (5, 6), (8, 9), (10, 11), ((0, 0), (0, 1))]
LATE = ((1, 0), (1, 1))
ORDERS = {"gains": "zxy", (0, 0): "zxy", (0, 1): "zyx", (1, 0): "xyz", (1, 1): "yxz"}
for _pair in PAIRS[:-1]:
    for _unit, _order in zip(_pair[-2:], ("zxy", "zyx")):
        ORDERS[_unit] = _order


def forward_schedule(ahead=5):
    events = [(unit, 0) for unit in PAIRS[0]] + [(unit, 0) for unit in LATE]
    for pair in PAIRS[1:ahead]:
        events += [(unit, 0) for unit in pair]
    count = len(PAIRS)
    for step in range(count + 4):
        for stage in (1, 0, None, 2, 3, 4):
            if stage is None:
                if step in (0, 2):
                    events += [(unit, 1 + step // 2) for unit in LATE]
                continue
            index = step + ahead if stage == 0 else step - stage + 1
            if (stage > 0 or index >= ahead) and 0 <= index < count:
                events += [(unit, stage) for unit in PAIRS[index]]
    return events + [(unit, stage) for stage in (3, 4) for unit in LATE]


class Gather:
    def __init__(self, post, mats, down, gains, kept, spot, everyone):
        self.post, self.mats, self.down, self.gains, self.kept = post, mats, down, gains, kept
        self.spot, self.everyone = spot, everyone
        self.events = forward_schedule()
        self.waits, self.near, self.ready = {}, {}, set()

    def at(self, unit, *where):
        if unit == "gains":
            return self.gains.at[where]
        if isinstance(unit, tuple):
            return self.down.at[where + (pl.ds(unit[0] * 48, 48), pl.ds(unit[1] * HALF, HALF))]
        return self.mats.at[(unit,) + where]

    def forward(self, unit, where, targets):
        return [self.post.copy(self.at(unit, *where), self.at(unit, *where), target) for target in targets]

    def run(self, unit, stage):
        z, x, y, c = self.spot
        across, along, sibling = self.everyone[3:]
        order = ORDERS[unit]
        if stage == 0:
            targets = {"z": self.everyone[:3], "x": (across,), "y": (along,)}[order[0]]
            self.near[unit] = []
            self.waits[unit] = self.forward(unit, self.spot, targets)
            return
        if stage == 4:
            arrived(self.near[unit])
            self.ready.add(unit)
            if isinstance(unit, int):
                self.post.local(self.mats.at[unit], self.kept[0].at[unit])
            if unit in ((0, 1), (1, 1)):
                rows = (EVERY,) * 4 + (pl.ds(unit[0] * 48, 48),)
                self.post.local(self.down.at[rows], self.kept[1].at[rows])
            return
        arrived(self.waits[unit])
        steps = {
            "zxy": (
                ((EVERY, x, y, c), (across,), (EVERY, x, y, c)),
                ((EVERY, EVERY, y, c), (along,), (EVERY, 1 - x, y, c)),
                (None, (), (EVERY, EVERY, 1 - y, c)),
            ),
            "zyx": (
                ((EVERY, x, y, c), (along,), (EVERY, x, y, c)),
                ((EVERY, x, EVERY, c), (across,), (EVERY, x, 1 - y, c)),
                (None, (), (EVERY, 1 - x, EVERY, c)),
            ),
            "xyz": (
                ((z, EVERY, y, c), (along,), None),
                ((z, EVERY, EVERY, c), self.everyone[:3], (z, EVERY, EVERY, c)),
                (None, (), "others"),
            ),
            "yxz": (
                ((z, x, EVERY, c), (across,), None),
                ((z, EVERY, EVERY, c), self.everyone[:3], (z, EVERY, EVERY, c)),
                (None, (), "others"),
            ),
        }
        where, targets, near = steps[order][stage - 1]
        self.waits[unit] = self.forward(unit, where, targets) if targets else []
        if near == "others":
            for k in range(3):
                self.near[unit] += self.forward(unit, (z ^ (k + 1), EVERY, EVERY, c), (sibling,))
        elif near is not None:
            self.near[unit] += self.forward(unit, near, (sibling,))

    def pump(self, count):
        for _ in range(count):
            if self.events:
                self.run(*self.events.pop(0))

    def require(self, *units):
        for unit in units:
            while unit not in self.ready:
                self.pump(1)


def forward_kernel(*refs):
    shards, (tokens, memory, cotangent, table, lengths, memory_lengths) = refs[:11], refs[11:17]
    kept_mats, kept_down, gain_rows = refs[17:20]
    (turned, memory_turned, small, keys_out, values_out, self_out, cross_out, hidden_out, slope_out, grads_out) = refs[20:30]
    self_log, cross_log = refs[30:32]
    (gains, mats, down, keep, keys, values, stage, memory_stage, hidden, slope) = refs[32:42]
    (hidden_turned, after_self, after_cross, own_cut, other_cut, grads, near, send, recv) = refs[42:]
    spot = place()
    everyone = partners(*spot)
    sibling = everyone[5]
    post = Post(send, recv, near)
    comm = Gather(post, mats, down, gains, (kept_mats, kept_down), spot, everyone)
    for index in range(8):
        mats.at[(index,) + spot][...] = shards[index][...]
    for index in range(4):
        mats.at[(8 + index,) + spot][...] = shards[8][:, index * 768 : (index + 1) * 768]
    down.at[spot][...] = shards[9][...]
    gains.at[spot][...] = shards[10][...]
    enter(everyone)
    comm.pump(9)
    from_sibling = []

    def turn(block, staged, target, lanes=ROWS):
        staged[...] = block.T
        post.local(staged, target.at[:, pl.ds(0, lanes)])
        from_sibling.append(post.copy(staged, target.at[:, pl.ds(lanes, lanes)], sibling))

    for block in range(4):
        turn(memory[block * ROWS : (block + 1) * ROWS], memory_stage.at[block], memory_turned.at[block])
        comm.pump(1)
    live = lax.broadcasted_iota(jnp.int32, (ROWS, 1), 0) < lengths[0]
    grad_low = jnp.where(live, cotangent[...], jnp.zeros_like(cotangent[...]))
    left, right = grad_low[:, :HALF], grad_low[:, HALF:]
    core = spot[3]
    own_cut[0] = jnp.where(core == 0, left, right)
    other_cut[...] = jnp.where(core == 0, right, left)
    from_sibling.append(post.copy(other_cut, own_cut.at[1], sibling))
    source = tokens[...].astype(FULL)
    inverse = inverse_rms(source)
    one_hot = bucket_rows()
    bias = dot(table[...], one_hot)
    visible = self_mask(lengths[0])
    comm.require("gains")
    gain_rows[...] = jnp.sum(gains[...].astype(FULL).reshape(32, 8, 768), axis=0)
    normed = (source * inverse * gain_rows[0:1]).astype(LOW)
    turn(normed, stage.at[0], turned.at[0])

    def project(unit, slot, block):
        comm.require(unit)
        keep[slot] = dot(block, square(mats, unit)).astype(LOW)
        post.local(keep.at[slot], small.at[slot])

    project(0, 0, normed)
    project(1, 1, normed)
    project(2, 2, normed)

    def attend(pair, head, query, key_block, value_block, extra, log_ref):
        scores = dot_last(key_block, one_head(query, head)) + extra
        peak = jnp.max(scores, axis=0, keepdims=True)
        raised = jnp.exp(scores - peak)
        total = jnp.sum(raised, axis=0, keepdims=True)
        mixed = dot_first(value_block, raised.astype(LOW)) / total
        log_ref[pair * 2 + head : pair * 2 + head + 1] = peak + jnp.log(total)
        return mixed[head * DH : head * DH + DH]

    for pair in range(6):
        span = slice(pair * 128, pair * 128 + 128)
        query = keep[0, :, span] * 0.125
        mixed = [
            attend(
                pair,
                head,
                query,
                keep[1, :, span],
                keep[2, :, span],
                slanted(bias[pair * 2 + head : pair * 2 + head + 1]) + visible,
                self_log,
            )
            for head in range(2)
        ]
        keep[3, :, span] = jnp.concatenate(mixed, axis=0).T.astype(LOW)
        comm.pump(1)
    post.local(keep.at[3], small.at[3])
    context = keep[3]
    turn(context, stage.at[1], turned.at[1])
    comm.require(3)
    after_self[...] = source + dot(context, square(mats, 3))
    post.local(after_self, self_out)
    normed = (after_self[...] * inverse_rms(after_self[...]) * gain_rows[1:2]).astype(LOW)
    turn(normed, stage.at[2], turned.at[2])
    project(4, 4, normed)
    for unit, held, out in ((5, keys, keys_out), (6, values, values_out)):
        comm.require(unit)
        for block in range(4):
            held[block] = dot(memory[block * ROWS : (block + 1) * ROWS], square(mats, unit)).astype(LOW)
        post.local(held, out)
    shown = memory_mask(memory_lengths[0], 1024)
    for pair in range(6):
        span = slice(pair * 128, pair * 128 + 128)
        query = keep[4, :, span] * 0.125
        mixed = [
            attend(pair, head, query, keys[:, :, span].reshape(1024, 128), values[:, :, span].reshape(1024, 128), shown, cross_log) for head in range(2)
        ]
        keep[5, :, span] = jnp.concatenate(mixed, axis=0).T.astype(LOW)
        comm.pump(1)
    post.local(keep.at[5], small.at[5])
    context = keep[5]
    turn(context, stage.at[3], turned.at[3])
    comm.require(7)
    after_cross[...] = after_self[...] + dot(context, square(mats, 7))
    post.local(after_cross, cross_out)
    normed = (after_cross[...] * inverse_rms(after_cross[...]) * gain_rows[2:3]).astype(LOW)
    turn(normed, stage.at[4], turned.at[4])
    root = math.sqrt(2.0 / math.pi)
    for block in range(4):
        comm.require(8 + block)
        before = dot(normed, square(mats, 8 + block))
        squared = before * before
        bent = jnp.tanh(root * before * (1.0 + 0.044715 * squared))
        lifted = 0.5 * (1.0 + bent)
        value = (before * lifted).astype(LOW)
        hidden[block] = value
        slope[block] = (
            lifted + 0.5 * root * before * (1.0 - bent * bent) * (1.0 + 3 * 0.044715 * squared)
        ).astype(LOW)
        post.local(hidden.at[block], hidden_out.at[block])
        post.local(slope.at[block], slope_out.at[block])
        hidden_turned[block, :, :ROWS] = value.T
        half = hidden_turned.at[block, :, pl.ds(0, ROWS)]
        from_sibling.append(post.copy(half, hidden_turned.at[block, :, pl.ds(ROWS, ROWS)], sibling))
        comm.pump(1)
    arrived(from_sibling)
    for block in range(4):
        comm.pump(1)
        grads[block] = dot(hidden_turned[block], own_cut[...].reshape(512, HALF)).astype(LOW).reshape(2, 2, 2, 96, HALF)
        post.local(grads.at[block], grads_out.at[block])
    while comm.events:
        comm.pump(1)
    post.finish()


def forward_call(shards, *rest):
    kind = jax.ShapeDtypeStruct
    anywhere, vmem = pl.BlockSpec(memory_space=pl.ANY), pl.BlockSpec(memory_space=pltpu.VMEM)
    smem = pl.BlockSpec(memory_space=pltpu.SMEM)
    outs = (
        (kind((12, 4, 2, 2, 2, 24, 768), LOW), anywhere),
        (kind((4, 2, 2, 2, 96, 768), LOW), anywhere),
        (kind((8, 768), FULL), vmem),
        (kind((5, 768, 512), LOW), anywhere),
        (kind((4, 768, 512), LOW), anywhere),
        (kind((6, 256, 768), LOW), anywhere),
        (kind((4, 256, 768), LOW), anywhere),
        (kind((4, 256, 768), LOW), anywhere),
        (kind((256, 768), FULL), anywhere),
        (kind((256, 768), FULL), anywhere),
        (kind((4, 256, 768), LOW), anywhere),
        (kind((4, 256, 768), LOW), anywhere),
        (kind((4, 2, 2, 2, 96, HALF), LOW), anywhere),
        (kind((16, 256), FULL), vmem),
        (kind((16, 256), FULL), vmem),
    )
    return pl.pallas_call(
        forward_kernel,
        out_shape=tuple(out[0] for out in outs),
        in_specs=[vmem] * 15 + [smem] * 2,
        out_specs=tuple(out[1] for out in outs),
        scratch_shapes=[
            pltpu.VMEM((4, 2, 2, 2, 8, 768), LOW),
            pltpu.VMEM((12, 4, 2, 2, 2, 24, 768), LOW),
            pltpu.VMEM((4, 2, 2, 2, 96, 768), LOW),
            pltpu.VMEM((6, 256, 768), LOW),
            pltpu.VMEM((4, 256, 768), LOW),
            pltpu.VMEM((4, 256, 768), LOW),
            pltpu.VMEM((5, 768, 256), LOW),
            pltpu.VMEM((4, 768, 256), LOW),
            pltpu.VMEM((4, 256, 768), LOW),
            pltpu.VMEM((4, 256, 768), LOW),
            pltpu.VMEM((4, 768, 512), LOW),
            pltpu.VMEM((256, 768), FULL),
            pltpu.VMEM((256, 768), FULL),
            pltpu.VMEM((2, 256, HALF), LOW),
            pltpu.VMEM((256, HALF), LOW),
            pltpu.VMEM((4, 2, 2, 2, 96, HALF), LOW),
            pltpu.SemaphoreType.DMA((80,)),
            pltpu.SemaphoreType.DMA((180,)),
            pltpu.SemaphoreType.DMA((180,)),
        ],
        compiler_params=pltpu.CompilerParams(
            collective_id=0, has_side_effects=True, vmem_limit_bytes=60 * 2**20
        ),
    )(*shards, *rest)


Z_FIRST = (8, 9)


class Scatter:
    def __init__(self, post, grads, inboxes, done, sums, outs, spot, everyone):
        self.post, self.grads, self.inboxes, self.done, self.sums, self.outs = post, grads, inboxes, done, sums, outs
        self.spot, self.everyone = spot, everyone
        self.queue, self.waits, self.flipped, self.count = [], {(0, "sum"): []}, {}, 0

    def at(self, kind, unit, *where):
        mats, down = kind
        if isinstance(unit, int):
            return mats.at[(unit,) + where]
        where += (EVERY,) * (len(down.shape) - 2 - len(where))
        return down.at[where + (pl.ds(0 if unit == "down0" else 48, 48),)]

    def grad(self, unit, *where):
        return self.at(self.grads, unit, *where)

    def box(self, number, unit, *where):
        return self.at(self.inboxes[number], unit, *where)

    def begin(self, unit):
        z, x, y, c = self.spot
        self.flipped[unit] = self.count % 2 == 1
        self.count += 1
        if unit in Z_FIRST:
            first = Z_FIRST.index(unit)
            self.send(
                unit, 0, [(self.grad(unit, z ^ (k + 1)), self.inboxes[3].at[first, k], self.everyone[k]) for k in range(3)]
            )
        elif self.flipped[unit]:
            self.send(unit, 0, [(self.grad(unit, EVERY, 1 - x, EVERY, EVERY), self.box(0, unit), self.everyone[3])])
        else:
            self.send(unit, 0, [(self.grad(unit, EVERY, EVERY, 1 - y, EVERY), self.box(0, unit), self.everyone[4])])

    def send(self, unit, stage, copies):
        self.waits[unit] = [self.post.copy(*copy) for copy in copies]
        self.queue.append((unit, stage + 1))

    def add(self, target, *terms):
        total = target[...].astype(FULL)
        for term in terms:
            total = total + term[...].astype(FULL)
        target[...] = total.astype(LOW)

    def run(self, unit, stage):
        z, x, y, c = self.spot
        across, along, sibling = self.everyone[3:]
        flipped, early = self.flipped[unit], unit in Z_FIRST
        arrived(self.waits[unit])
        if stage == 1 and early:
            box = self.inboxes[3].at[Z_FIRST.index(unit)]
            self.add(self.grad(unit, z), *(box.at[k] for k in range(3)))
            if flipped:
                source, target = (z, 1 - x, EVERY, EVERY), across
            else:
                source, target = (z, EVERY, 1 - y, EVERY), along
            self.send(unit, 1, [(self.grad(unit, *source), self.box(0, unit, 0), target)])
        if stage == 2 and early:
            if flipped:
                self.add(self.grad(unit, z, x), self.box(0, unit, 0))
                source, target = (z, x, 1 - y, EVERY), along
            else:
                self.add(self.grad(unit, z, EVERY, y), self.box(0, unit, 0))
                source, target = (z, 1 - x, y, EVERY), across
            self.send(unit, 2, [(self.grad(unit, *source), self.box(1, unit, 0), target)])
        if stage == 1 and not early:
            if flipped:
                self.add(self.grad(unit, EVERY, x, EVERY, EVERY), self.box(0, unit))
                source, target = (EVERY, x, 1 - y, EVERY), along
            else:
                self.add(self.grad(unit, EVERY, EVERY, y, EVERY), self.box(0, unit))
                source, target = (EVERY, 1 - x, y, EVERY), across
            self.send(unit, 1, [(self.grad(unit, *source), self.box(1, unit), target)])
        if stage == 2 and not early:
            self.add(self.grad(unit, EVERY, x, y, EVERY), self.box(1, unit))
            self.send(
                unit,
                2,
                [(self.grad(unit, z ^ (k + 1), x, y, EVERY), self.box(2, unit, k), self.everyone[k]) for k in range(3)],
            )
        if stage == 3:
            total = []
            for core in (c, 1 - c):
                part = self.grad(unit, z, x, y, core)[...].astype(FULL)
                for k in range(1 if early else 3):
                    part = part + (self.box(1, unit, 0, core) if early else self.box(2, unit, k, core))[...].astype(FULL)
                total.append(part)
            mine = pl.ds(pl.multiple_of(c * HALF, 128), HALF)
            if isinstance(unit, int):
                target = self.outs[0].at[unit, :, mine]
            else:
                target = self.outs[1].at[pl.ds(0 if unit == "down0" else 48, 48), mine]
            target[...] = total[0]
            self.at(self.done, unit)[...] = total[1]
            self.send(unit, 3, [(self.at(self.done, unit), target, sibling)])

    def small_sum(self, hop):
        sums, boxes = self.sums
        hops = ((self.everyone[4],), (self.everyone[3],), self.everyone[:3], (self.everyone[5],))
        arrived(self.waits[0, "sum"])
        if hop in (1, 2, 4):
            sums[hop] = sums[hop - 1] + boxes[(0, 0, 1, 0, 5)[hop]]
        if hop == 3:
            sums[hop] = (sums[hop - 1] + boxes[2]) + (boxes[3] + boxes[4])
        if hop < 4:
            first = (0, 1, 2, 5)[hop]
            self.waits[0, "sum"] = [
                self.post.copy(sums.at[hop], boxes.at[first + k], target) for k, target in enumerate(hops[hop])
            ]
            self.queue.append(("sum", hop + 1))

    def pump(self, count):
        for _ in range(count):
            if self.queue:
                unit, stage = self.queue.pop(0)
                if unit == "sum":
                    self.small_sum(stage)
                else:
                    self.run(unit, stage)


def rms_back(upstream, field, gain):
    inverse = inverse_rms(field)
    scaled = gain * upstream
    shift = inverse * inverse * inverse * jnp.mean(scaled * field, axis=-1, keepdims=True)
    return inverse * scaled - field * shift, jnp.sum(upstream * field * inverse, axis=0, keepdims=True)


def split_dot(dotted, left, right):
    high = left.astype(LOW)
    return dotted(right, high) + dotted(right, (left - high.astype(FULL)).astype(LOW))


def backward_kernel(*refs):
    (mats, down, turned, memory_turned, grads_in) = refs[:5]
    (keys_in, values_in, hidden_in, slope_in, after_self, after_cross) = refs[5:11]
    (small_in, gains, tokens, cotangent, table, self_log, cross_log) = refs[11:18]
    lengths, memory_lengths = refs[18:20]
    (output, input_grad, memory_grad, mats_out, down_out, extra_out) = refs[20:26]
    (pool_a, pool_b, big, turned_box, wide_a, wide_b, rows_out) = refs[26:33]
    (own_cut, other_cut, own_long, other_long, rows_d, rows_bias, rows_distance) = refs[33:40]
    (grads, grads_down, box_one, box_one_down, box_two, box_two_down, box_three, box_three_down, box_early) = refs[40:49]
    (done, done_down, field, extra, extra_box, stage, small, near, send, recv) = refs[49:]
    spot = z, x, y, c = place()
    everyone = partners(*spot)
    sibling = everyone[5]
    post = Post(send, recv, near)
    comm = Scatter(
        post,
        (grads, grads_down),
        ((box_one, box_one_down), (box_two, box_two_down), (box_three, box_three_down), box_early),
        (done, done_down),
        (extra, extra_box),
        (mats_out, down_out),
        spot,
        everyone,
    )

    def fetch(source, target):
        return post.local(source, target, keep=True)

    def weight(ref, index):
        return ref[index * 32 : index * 32 + 32].reshape(768, 768)

    def fetch_weight(index, pool, slot):
        return fetch(mats.at[pl.ds(index * 32, 32)], pool.at[pl.ds(slot * 32, 32)])

    loads = {
        "grads": fetch(grads_in, grads_down),
        "down": fetch(down, pool_a),
        "slope": fetch(slope_in, wide_b),
        "turned4": fetch(turned.at[4], turned_box.at[0]),
    }

    def need(*names):
        for name in names:
            loads.pop(name).wait()

    def halves(value):
        left, right = value[:, :HALF], value[:, HALF:]
        return jnp.where(c == 0, left, right), jnp.where(c == 0, right, left)

    def whole(mine, other):
        return jnp.concatenate([jnp.where(c == 0, mine, other), jnp.where(c == 0, other, mine)], axis=1)

    hand = {}

    def share(slot, value):
        mine, other = halves(value)
        own_cut[slot, 0] = mine
        other_cut[slot] = other
        hand[slot] = post.copy(other_cut.at[slot], own_cut.at[slot, 1], sibling)

    def shared(slot):
        hand.pop(slot).wait_recv()
        return own_cut[slot].reshape(512, HALF)

    def both(slot):
        return whole(own_cut[slot, 0], other_cut[slot])

    def sum_rows(slot, left, right):
        grads[slot] = dot(left, right).astype(LOW).reshape(4, 2, 2, 2, 24, HALF)

    live = lax.broadcasted_iota(jnp.int32, (ROWS, 1), 0) < lengths[0]
    grad_out = jnp.where(live, cotangent[...].astype(FULL), 0.0)
    grad_low = grad_out.astype(LOW)
    enter(everyone)
    need("grads")
    comm.begin("down0")
    comm.begin("down1")
    need("down", "slope")
    loads["in"] = fetch(mats.at[pl.ds(256, 128)], pool_b)
    loads["hidden"] = fetch(hidden_in, wide_a)
    loads["after_cross"] = fetch(after_cross, field)
    for block in range(4):
        grad_hidden = dot_last(grad_low, weight(pool_a, block))
        share(1 + block, (grad_hidden * wide_b[block].astype(FULL)).astype(LOW))
    loads["turned3"] = fetch(turned.at[3], turned_box.at[1])
    loads["values"] = fetch(values_in, wide_b)
    need("turned4")
    for block in range(4):
        sum_rows(8 + block, turned_box[0], shared(1 + block))
        comm.begin(8 + block)
    loads["turned1"] = fetch(turned.at[1], turned_box.at[0])
    need("hidden", "after_cross", "in")
    total = field[...]
    for block in range(4):
        total = total + dot(wide_a[block], weight(pool_a, block))
    output[...] = total.astype(LOW)
    comm.pump(1)
    loads["keys"] = fetch(keys_in, wide_a)
    for slot, index in enumerate((7, 4, 5, 6)):
        loads[index] = fetch_weight(index, pool_a, slot)
    loads["small"] = fetch(small_in, small)
    loads["turned2"] = fetch(turned.at[2], turned_box.at[2])
    loads["memory_turned"] = fetch(memory_turned, big)
    upstream = 0.0
    for block in range(4):
        upstream = upstream + dot_last(both(1 + block), weight(pool_b, block))
    for slot, index in enumerate((3, 0, 1, 2)):
        loads[index] = fetch_weight(index, pool_b, slot)
    step, gain_three = rms_back(upstream, field[...], gains[2:3])
    extra[0] = jnp.zeros((8, 768), FULL)
    extra[0, 2:3] = gain_three
    input_grad[...] = grad_out + step
    grad_low = input_grad[...].astype(LOW)
    share(5, grad_low)
    loads["after_self"] = fetch(after_self, field)
    need(7)
    upstream = dot_last(grad_low, weight(pool_a, 0)).astype(LOW)
    need("turned3")
    sum_rows(7, turned_box[1], shared(5))
    comm.begin(7)
    loads["turned0"] = fetch(turned.at[0], turned_box.at[1])

    heads = (
        lax.broadcasted_iota(jnp.int32, (16, 768), 1) // DH == lax.broadcasted_iota(jnp.int32, (16, 768), 0)
    ).astype(LOW)

    def inner_rows(context):
        rows_d[...] = split_dot(dot_last, upstream_ref[...].astype(FULL) * context.astype(FULL), heads)

    upstream_ref = stage
    upstream_ref[...] = upstream
    need("small")
    inner_rows(small[5])

    def attend_back(pair, query_block, key_block, value_block, log_ref, extra_of, visit):
        span = pl.ds(pl.multiple_of(pair * 128, 128), 128)
        query, handed = query_block(span) * 0.125, upstream_ref[:, span]
        grad_values, grad_keys, grad_query = 0.0, 0.0, []
        key_block, value_block = key_block(span), value_block(span)
        for head in range(2):
            row = pl.ds(pair * 2 + head, 1)
            query_part, handed_part = one_head(query, head), one_head(handed, head)
            attended = jnp.exp(dot_last(key_block, query_part) + extra_of(row) - log_ref[row])
            grad_scores = attended * (dot_last(value_block, handed_part) - rows_d[row])
            visit(row, grad_scores)
            rounded = grad_scores.astype(LOW)
            grad_values = grad_values + dot(attended.astype(LOW), handed_part)
            grad_keys = grad_keys + dot(rounded, query_part)
            grad_query.append(dot_first(key_block, rounded)[head * DH : head * DH + DH])
        grad_query = jnp.concatenate(grad_query, axis=0).T * 0.125
        return grad_query.astype(LOW), grad_keys.astype(LOW), grad_values.astype(LOW)

    need("keys", "values")
    shown = memory_mask(memory_lengths[0], 1024)
    for turn in range(6):
        mine, lane = turn >= 3, slice(turn % 3 * 128, turn % 3 * 128 + 128)
        pair = (c if mine else 1 - c) * 3 + turn % 3
        grad_query, grad_keys, grad_values = attend_back(
            pair,
            lambda span: small[4, :, span],
            lambda span: wide_a[:, :, span].reshape(1024, 128),
            lambda span: wide_b[:, :, span].reshape(1024, 128),
            cross_log,
            lambda row: shown,
            lambda row, value: None,
        )
        grad_keys, grad_values = grad_keys.reshape(4, ROWS, 128), grad_values.reshape(4, ROWS, 128)
        if mine:
            own_cut[6, 0, :, lane] = grad_query
            own_long[0, :, 0, :, lane] = grad_keys
            own_long[1, :, 0, :, lane] = grad_values
        else:
            other_cut[6, :, lane] = grad_query
            other_long[0, :, :, lane] = grad_keys
            other_long[1, :, :, lane] = grad_values
        if turn == 2:
            hand[6] = post.copy(other_cut.at[6], own_cut.at[6, 1], sibling)
            for kind in range(2):
                hand["long", kind] = post.copy(other_long.at[kind], own_long.at[kind, :, 1], sibling)
        comm.pump(1)
    need(4, 5, 6)
    need("turned2", "after_self")
    upstream = dot_last(both(6), weight(pool_a, 1))
    step, gain_two = rms_back(upstream, field[...], gains[1:2])
    extra[0, 1:2] = gain_two
    input_grad[...] = input_grad[...] + step
    grad_low = input_grad[...].astype(LOW)
    share(7, grad_low)
    comm.pump(1)
    need("memory_turned")
    for kind, unit in ((0, 5), (1, 6)):
        hand.pop(("long", kind)).wait_recv()
        total = 0.0
        for block in range(4):
            total = total + dot(big[block], own_long[kind, block].reshape(512, HALF))
        grads[unit] = total.astype(LOW).reshape(4, 2, 2, 2, 24, HALF)
        comm.begin(unit)
        comm.pump(1)
    sum_rows(4, turned_box[2], shared(6))
    comm.begin(4)
    comm.pump(1)
    need(3, "turned1")
    upstream_ref[...] = dot_last(grad_low, weight(pool_b, 0)).astype(LOW)
    inner_rows(small[3])
    sum_rows(3, turned_box[0], shared(7))
    comm.begin(3)
    one_hot = bucket_rows()
    rows_bias[0:12] = dot(table[...], one_hot)
    visible = self_mask(lengths[0])

    def by_distance(row, value):
        eight = value[:8]
        for first in range(8, ROWS, 8):
            eight = eight + pltpu.roll(value[first : first + 8], ROWS - first, 1)
        total = eight[:1]
        for first in range(1, 8):
            total = total + pltpu.roll(eight, ROWS - first, 1)[first : first + 1]
        rows_distance[row] = total

    rows_distance[...] = jnp.zeros((16, ROWS), FULL)
    for turn in range(6):
        mine, lane = turn >= 3, slice(turn % 3 * 128, turn % 3 * 128 + 128)
        pair = (c if mine else 1 - c) * 3 + turn % 3
        parts = attend_back(
            pair,
            lambda span: small[0, :, span],
            lambda span: small[1, :, span],
            lambda span: small[2, :, span],
            self_log,
            lambda row: slanted(rows_bias[row]) + visible,
            by_distance,
        )
        for slot, part in zip((8, 9, 10), parts):
            if mine:
                own_cut[slot, 0, :, lane] = part
            else:
                other_cut[slot, :, lane] = part
        if turn == 2:
            for slot in (8, 9, 10):
                hand[slot] = post.copy(other_cut.at[slot], own_cut.at[slot, 1], sibling)
        comm.pump(1 + turn % 2)
    need("turned0", 0, 1, 2)
    for unit in range(3):
        sum_rows(unit, turned_box[1], shared(8 + unit))
        comm.begin(unit)
        comm.pump(2)
    upstream = 0.0
    for unit in range(3):
        upstream = upstream + dot_last(both(8 + unit), weight(pool_b, 1 + unit))
    step, gain_one = rms_back(upstream, tokens[...].astype(FULL), gains[0:1])
    extra[0, 0:1] = gain_one
    high = rows_distance[...].astype(LOW)
    many = jnp.concatenate([one_hot] * 16, axis=0)
    sums = dot_last(high, many) + dot_last((rows_distance[...] - high.astype(FULL)).astype(LOW), many)
    own_head = lax.broadcasted_iota(jnp.int32, (16, 512), 1) // NB == lax.broadcasted_iota(jnp.int32, (16, 512), 0)
    extra[0, 3:4, :512] = jnp.sum(jnp.where(own_head, sums, 0.0), axis=0, keepdims=True)
    input_grad[...] = input_grad[...] + step
    comm.small_sum(0)
    shown_rows = []
    for block in range(4):
        comm.pump(3)
        if block >= 2:
            shown_rows[block - 2].wait()
        rows_out[block % 2] = dot_last(
            whole(own_long[0, block, 0], other_long[0, block]), weight(pool_a, 2)
        ) + dot_last(whole(own_long[1, block, 0], other_long[1, block]), weight(pool_a, 3))
        shown_rows.append(fetch(rows_out.at[block % 2], memory_grad.at[pl.ds(block * ROWS, ROWS)]))
    while comm.queue:
        comm.pump(1)
    for made in shown_rows[2:]:
        made.wait()
    extra_out[...] = extra[4]
    post.finish()


def backward_call(*args):
    kind = jax.ShapeDtypeStruct
    anywhere, vmem = pl.BlockSpec(memory_space=pl.ANY), pl.BlockSpec(memory_space=pltpu.VMEM)
    smem = pl.BlockSpec(memory_space=pltpu.SMEM)
    vm, dma = pltpu.VMEM, pltpu.SemaphoreType.DMA
    return pl.pallas_call(
        backward_kernel,
        out_shape=(
            kind((256, 768), LOW),
            kind((256, 768), FULL),
            kind((1024, 768), FULL),
            kind((12, 24, 768), FULL),
            kind((96, 768), FULL),
            kind((8, 768), FULL),
        ),
        in_specs=[anywhere] * 12 + [vmem] * 6 + [smem] * 2,
        out_specs=(vmem, vmem, anywhere, vmem, vmem, vmem),
        scratch_shapes=[
            vm((128, 24, 768), LOW),
            vm((128, 24, 768), LOW),
            vm((4, 768, 512), LOW),
            vm((3, 768, 512), LOW),
            vm((4, 256, 768), LOW),
            vm((4, 256, 768), LOW),
            vm((2, 256, 768), FULL),
            vm((11, 2, 256, HALF), LOW),
            vm((11, 256, HALF), LOW),
            vm((2, 4, 2, 256, HALF), LOW),
            vm((2, 4, 256, HALF), LOW),
            vm((16, 256), FULL),
            vm((16, 256), FULL),
            vm((16, 256), FULL),
            vm((12, 4, 2, 2, 2, 24, HALF), LOW),
            vm((4, 2, 2, 2, 96, HALF), LOW),
            vm((12, 4, 2, 2, 24, HALF), LOW),
            vm((4, 2, 2, 96, HALF), LOW),
            vm((12, 4, 2, 24, HALF), LOW),
            vm((4, 2, 96, HALF), LOW),
            vm((12, 3, 2, 24, HALF), LOW),
            vm((3, 2, 96, HALF), LOW),
            vm((len(Z_FIRST), 3, 2, 2, 2, 24, HALF), LOW),
            vm((12, 24, HALF), FULL),
            vm((96, HALF), FULL),
            vm((256, 768), FULL),
            vm((5, 8, 768), FULL),
            vm((6, 8, 768), FULL),
            vm((256, 768), LOW),
            vm((6, 256, 768), LOW),
            dma((60,)),
            dma((150,)),
            dma((150,)),
        ],
        compiler_params=pltpu.CompilerParams(
            collective_id=1, has_side_effects=True, vmem_limit_bytes=60 * 2**20
        ),
    )(*args)


def finish_kernel(*refs):
    (output, input_grad, memory_grad, mats, down, extra), outs = refs[:6], refs[6:]
    for source, target in zip((output, input_grad, memory_grad, down), outs):
        target[...] = source[...]
    for index in range(8):
        outs[4 + index][...] = mats[index]
    for index in range(4):
        outs[12][:, index * 768 : (index + 1) * 768] = mats[8 + index]
    rank = lax.axis_index(AXES[0]) * lax.axis_size(AXES[1]) + lax.axis_index(AXES[1])
    own = pltpu.roll(extra[...], 768 - rank * 24, 1)
    for index in range(3):
        outs[13 + index][...] = own[index : index + 1, :24]
    for head in range(12):
        outs[16][head : head + 1] = extra[3:4, head * NB : head * NB + NB]


def finish(*args):
    kind = jax.ShapeDtypeStruct
    block = lambda *shape: pl.BlockSpec(shape, lambda step: (step, 0))
    whole = lambda *shape: pl.BlockSpec(shape, lambda step: (0,) * len(shape))
    rows = [block(128, 768), block(128, 768), block(512, 768)]
    single = [(96, 768)] + [(24, 768)] * 8 + [(24, 3072)] + [(1, 24)] * 3 + [(12, NB)]
    return pl.pallas_call(
        finish_kernel,
        grid=(2,),
        out_shape=(
            kind((256, 768), LOW),
            kind((256, 768), FULL),
            kind((1024, 768), FULL),
            *[kind(shape, FULL) for shape in single],
        ),
        in_specs=rows + [whole(12, 24, 768), whole(96, 768), whole(8, 768)],
        out_specs=rows + [whole(*shape) for shape in single],
    )(*args)


def plain_body(
    tokens,
    memory,
    cotangent,
    target_lengths,
    memory_lengths,
    self_gain,
    self_query,
    self_key,
    self_value,
    self_out,
    position_table,
    cross_gain,
    cross_query,
    cross_key,
    cross_value,
    cross_out,
    ffn_gain,
    ffn_in,
    ffn_out,
):
    wide_count = lax.axis_size(AXES[0])
    narrow_count = lax.axis_size(AXES[1])
    devices = wide_count * narrow_count
    seq_count = target_lengths.shape[0]
    target_rows = tokens.shape[0] // seq_count
    memory_rows = memory.shape[0] // seq_count
    positions = jnp.arange(target_rows, dtype=jnp.int32)
    live_rows = positions[None, :] < target_lengths[:, None]
    causal = positions[None, :] <= positions[:, None]
    self_visible = causal[None] & live_rows[:, None, :]
    memory_visible = (jnp.arange(memory_rows, dtype=jnp.int32)[None, :] < memory_lengths[:, None])[
        :, None, :
    ]
    grad_out = jnp.where(live_rows.reshape(-1, 1), cotangent.astype(jnp.float32), 0.0)
    bucket = bucket_index(target_rows)
    one_hot = (bucket[:, :, None] == jnp.arange(NB, dtype=jnp.int32)[None, None, :]).astype(
        jnp.float32
    )
    relative = jnp.einsum(
        "ijb,bh->hij", one_hot, position_table.astype(jnp.float32), precision=lax.Precision.HIGHEST
    )
    gain_one, weight_query, weight_key, weight_value, weight_out = (
        lax.all_gather(self_gain, AXES, axis=0, tiled=True),
        lax.all_gather(self_query, AXES, axis=0, tiled=True),
        lax.all_gather(self_key, AXES, axis=0, tiled=True),
        lax.all_gather(self_value, AXES, axis=0, tiled=True),
        lax.all_gather(self_out, AXES, axis=0, tiled=True),
    )
    source = tokens.astype(jnp.float32)
    normed_value, norm_back_one = jax.vjp(rms_apply, source, gain_one.astype(jnp.float32))
    normed_one = normed_value.astype(jnp.bfloat16)
    query_one = product(normed_one, weight_query).astype(jnp.bfloat16)
    keys_one = product(normed_one, weight_key).astype(jnp.bfloat16)
    values_one = product(normed_one, weight_value).astype(jnp.bfloat16)
    context_one, totals_one = attend_forward(
        query_one, keys_one, values_one, relative, self_visible, seq_count
    )
    after_self = source + product(context_one, weight_out)
    gain_two, cross_weight_query, cross_weight_key, cross_weight_value, cross_weight_out = (
        lax.all_gather(cross_gain, AXES, axis=0, tiled=True),
        lax.all_gather(cross_query, AXES, axis=0, tiled=True),
        lax.all_gather(cross_key, AXES, axis=0, tiled=True),
        lax.all_gather(cross_value, AXES, axis=0, tiled=True),
        lax.all_gather(cross_out, AXES, axis=0, tiled=True),
    )
    normed_value, norm_back_two = jax.vjp(rms_apply, after_self, gain_two.astype(jnp.float32))
    normed_two = normed_value.astype(jnp.bfloat16)
    query_two = product(normed_two, cross_weight_query).astype(jnp.bfloat16)
    keys_two = product(memory, cross_weight_key).astype(jnp.bfloat16)
    values_two = product(memory, cross_weight_value).astype(jnp.bfloat16)
    context_two, totals_two = attend_forward(
        query_two, keys_two, values_two, None, memory_visible, seq_count
    )
    after_cross = after_self + product(context_two, cross_weight_out)
    gain_three, weight_in, weight_down = (
        lax.all_gather(ffn_gain, AXES, axis=0, tiled=True),
        lax.all_gather(ffn_in, AXES, axis=0, tiled=True),
        lax.all_gather(ffn_out, AXES, axis=0, tiled=True),
    )
    normed_value, norm_back_three = jax.vjp(rms_apply, after_cross, gain_three.astype(jnp.float32))
    normed_three = normed_value.astype(jnp.bfloat16)
    before = product(normed_three, weight_in)
    gelu_value, gelu_back = jax.vjp(gelu_smooth, before)
    hidden = gelu_value.astype(jnp.bfloat16)
    output = (after_cross + product(hidden, weight_down)).astype(jnp.bfloat16)
    back_in, back_down = (
        lax.all_gather(ffn_in, AXES, axis=0, tiled=True),
        lax.all_gather(ffn_out, AXES, axis=0, tiled=True),
    )
    grad_low = grad_out.astype(jnp.bfloat16)
    grad_down_weight = outer_sum(hidden, grad_low)
    grad_hidden = back_project(grad_low, back_down)
    grad_before = gelu_back(grad_hidden)[0].astype(jnp.bfloat16)
    grad_in_weight = outer_sum(normed_three, grad_before)
    grad_normed_three = back_project(grad_before, back_in)
    grad_cross_part, grad_gain_three = norm_back_three(grad_normed_three)
    grad_cross = grad_out + grad_cross_part
    ffn_terms = (grad_gain_three, grad_in_weight, grad_down_weight)
    summed_ffn = lax.psum_scatter(
        pack_rows(ffn_terms, devices), AXES, scatter_dimension=0, tiled=True
    )
    ffn_gain_grad, ffn_in_grad, ffn_out_grad = unpack_rows(summed_ffn[0], ffn_terms, devices)
    back_cross_query, back_cross_key, back_cross_value, back_cross_out = (
        lax.all_gather(cross_query, AXES, axis=0, tiled=True),
        lax.all_gather(cross_key, AXES, axis=0, tiled=True),
        lax.all_gather(cross_value, AXES, axis=0, tiled=True),
        lax.all_gather(cross_out, AXES, axis=0, tiled=True),
    )
    grad_cross_low = grad_cross.astype(jnp.bfloat16)
    grad_cross_out_weight = outer_sum(context_two, grad_cross_low)
    grad_context_two = back_project(grad_cross_low, back_cross_out).astype(jnp.bfloat16)
    grad_query_two, grad_keys_two, grad_values_two, unused_extra = attend_backward(
        query_two,
        keys_two,
        values_two,
        None,
        memory_visible,
        seq_count,
        totals_two,
        grad_context_two,
    )
    grad_cross_query_weight = outer_sum(normed_two, grad_query_two)
    grad_cross_key_weight = outer_sum(memory, grad_keys_two)
    grad_cross_value_weight = outer_sum(memory, grad_values_two)
    memory_grad = back_project(grad_keys_two, back_cross_key) + back_project(
        grad_values_two, back_cross_value
    )
    grad_self_part, grad_gain_two = norm_back_two(back_project(grad_query_two, back_cross_query))
    grad_self = grad_cross + grad_self_part
    cross_terms = (
        grad_gain_two,
        grad_cross_query_weight,
        grad_cross_key_weight,
        grad_cross_value_weight,
        grad_cross_out_weight,
    )
    summed_cross = lax.psum_scatter(
        pack_rows(cross_terms, devices), AXES, scatter_dimension=0, tiled=True
    )
    cross_gain_grad, cross_query_grad, cross_key_grad, cross_value_grad, cross_out_grad = (
        unpack_rows(summed_cross[0], cross_terms, devices)
    )
    back_query, back_key, back_value, back_out = (
        lax.all_gather(self_query, AXES, axis=0, tiled=True),
        lax.all_gather(self_key, AXES, axis=0, tiled=True),
        lax.all_gather(self_value, AXES, axis=0, tiled=True),
        lax.all_gather(self_out, AXES, axis=0, tiled=True),
    )
    grad_self_low = grad_self.astype(jnp.bfloat16)
    grad_out_weight = outer_sum(context_one, grad_self_low)
    grad_context_one = back_project(grad_self_low, back_out).astype(jnp.bfloat16)
    grad_query_one, grad_keys_one, grad_values_one, grad_relative = attend_backward(
        query_one,
        keys_one,
        values_one,
        relative,
        self_visible,
        seq_count,
        totals_one,
        grad_context_one,
    )
    table_term = jnp.einsum("hij,ijb->bh", grad_relative, one_hot, precision=lax.Precision.HIGHEST)
    position_table_grad = lax.psum(table_term, AXES)
    grad_query_weight = outer_sum(normed_one, grad_query_one)
    grad_key_weight = outer_sum(normed_one, grad_keys_one)
    grad_value_weight = outer_sum(normed_one, grad_values_one)
    grad_normed_one = (
        back_project(grad_query_one, back_query)
        + back_project(grad_keys_one, back_key)
        + back_project(grad_values_one, back_value)
    )
    grad_source_part, grad_gain_one = norm_back_one(grad_normed_one)
    input_grad = grad_self + grad_source_part
    self_terms = (
        grad_gain_one,
        grad_query_weight,
        grad_key_weight,
        grad_value_weight,
        grad_out_weight,
    )
    summed_self = lax.psum_scatter(
        pack_rows(self_terms, devices), AXES, scatter_dimension=0, tiled=True
    )
    self_gain_grad, self_query_grad, self_key_grad, self_value_grad, self_out_grad = unpack_rows(
        summed_self[0], self_terms, devices
    )
    return (
        output,
        input_grad,
        memory_grad,
        self_gain_grad,
        self_query_grad,
        self_key_grad,
        self_value_grad,
        self_out_grad,
        position_table_grad,
        cross_gain_grad,
        cross_query_grad,
        cross_key_grad,
        cross_value_grad,
        cross_out_grad,
        ffn_gain_grad,
        ffn_in_grad,
        ffn_out_grad,
    )


def body(
    tokens,
    memory,
    cotangent,
    target_lengths,
    memory_lengths,
    self_gain,
    self_query,
    self_key,
    self_value,
    self_out,
    position_table,
    cross_gain,
    cross_query,
    cross_key,
    cross_value,
    cross_out,
    ffn_gain,
    ffn_in,
    ffn_out,
):
    rank = lax.axis_index(AXES[0]) * lax.axis_size(AXES[1]) + lax.axis_index(AXES[1])
    own_gains = jnp.stack([self_gain, cross_gain, ffn_gain])
    spread = lax.dynamic_update_slice(jnp.zeros((8, 768), LOW), own_gains, (0, rank * 24))
    shards = (self_query, self_key, self_value, self_out, cross_query, cross_key, cross_value, cross_out, ffn_in, ffn_out)
    (
        mats,
        down,
        gains,
        turned,
        memory_turned,
        small,
        keys,
        values,
        after_self,
        after_cross,
        hidden,
        slope,
        down_grads,
        self_log,
        cross_log,
    ) = forward_call(
        shards + (spread,), tokens, memory, cotangent, position_table.T, target_lengths, memory_lengths
    )
    output, input_grad, memory_grad, mats_grad, down_grad, extra = backward_call(
        mats.reshape(384, 24, 768),
        down.reshape(128, 24, 768),
        turned,
        memory_turned,
        down_grads,
        keys,
        values,
        hidden,
        slope,
        after_self,
        after_cross,
        small,
        gains,
        tokens,
        cotangent,
        position_table.T,
        self_log,
        cross_log,
        target_lengths,
        memory_lengths,
    )
    output, input_grad, memory_grad, down_grad, *square_grads, ffn_in_grad, gain_one, gain_two, gain_three, table = finish(
        output, input_grad, memory_grad, mats_grad, down_grad, extra
    )
    return (
        output,
        input_grad,
        memory_grad,
        gain_one.reshape(24),
        *square_grads[:4],
        table.T,
        gain_two.reshape(24),
        *square_grads[4:],
        gain_three.reshape(24),
        ffn_in_grad,
        down_grad,
    )


def solution(mesh):
    whole = (mesh.shape[AXES[0]], mesh.shape[AXES[1]]) == (8, 4)
    placed = (
        P(AXES, None),
        P(AXES, None),
        P(AXES, None),
        P(AXES),
        P(AXES),
        P(AXES),
        P(AXES, None),
        P(AXES, None),
        P(AXES, None),
        P(AXES, None),
        P(),
        P(AXES),
        P(AXES, None),
        P(AXES, None),
        P(AXES, None),
        P(AXES, None),
        P(AXES),
        P(AXES, None),
        P(AXES, None),
    )
    return jax.shard_map(
        body if whole else plain_body,
        mesh=mesh,
        in_specs=placed,
        out_specs=(
            P(AXES, None),
            P(AXES, None),
            P(AXES, None),
            P(AXES),
            P(AXES, None),
            P(AXES, None),
            P(AXES, None),
            P(AXES, None),
            P(),
            P(AXES),
            P(AXES, None),
            P(AXES, None),
            P(AXES, None),
            P(AXES, None),
            P(AXES),
            P(AXES, None),
            P(AXES, None),
        ),
        check_vma=False,
    )
```

```python
import math

import jax
import jax.numpy as jnp
from jax import lax
from jax.experimental import pallas as pl
from jax.experimental.pallas import tpu as pltpu
from jax.sharding import PartitionSpec as P

DH = 64
NB = 32
MAXDIST = 128


AXES = ("wide", "narrow")
EPSILON = 1e-06
NEGATIVE = -1e30


def bucket_index(length):
    offsets = jnp.arange(length, dtype=jnp.int32)
    distance = jnp.maximum(offsets[:, None] - offsets[None, :], 0)
    exact_part = NB // 2
    bucket = jnp.minimum(distance, exact_part)
    for step in range(1, NB - exact_part):
        bound = math.ceil(exact_part * (MAXDIST / exact_part) ** (step / (NB - exact_part)))
        bucket = bucket + (distance >= bound).astype(jnp.int32)
    return bucket


def rms_apply(field, gain):
    inverse = lax.rsqrt(jnp.mean(field * field, axis=-1, keepdims=True) + EPSILON)
    return field * inverse * gain


def gelu_smooth(field):
    return jax.nn.gelu(field, approximate=True)


def product(left, right):
    return jnp.dot(left, right, preferred_element_type=jnp.float32)


def outer_sum(left, right):
    return jnp.einsum("rd,re->de", left, right, preferred_element_type=jnp.float32)


def back_project(left, right):
    return jnp.einsum("re,de->rd", left, right, preferred_element_type=jnp.float32)


def pack_rows(arrays, devices):
    return jnp.concatenate([array.reshape(devices, -1) for array in arrays], axis=1)


def unpack_rows(packed_row, arrays, devices):
    results = []
    offset = 0
    for array in arrays:
        shard_shape = (array.shape[0] // devices,) + array.shape[1:]
        count = array.size // devices
        results.append(packed_row[offset : offset + count].reshape(shard_shape))
        offset = offset + count
    return tuple(results)


def head_blocks(array, index, seq_count):
    block = lax.dynamic_slice_in_dim(array, index * 2 * DH, 2 * DH, 1)
    return block.reshape(seq_count, -1, 2, DH)


def flat_block(block):
    return block.reshape(-1, 2 * DH)


def scored(query_block, keys_block, extra, visible, index):
    scores = jnp.einsum(
        "sqhd,skhd->shqk", query_block, keys_block, preferred_element_type=jnp.float32
    ) * DH ** (-0.5)
    if extra is not None:
        scores = scores + lax.dynamic_slice_in_dim(extra, index * 2, 2, 0)[None]
    return jnp.where(visible[:, None], scores, NEGATIVE)


def attend_forward(query, keys, values, extra, visible, seq_count):
    pairs = query.shape[1] // (2 * DH)
    start_context = jnp.zeros(query.shape, jnp.bfloat16)
    start_totals = jnp.zeros((seq_count, 2 * pairs, query.shape[0] // seq_count), jnp.float32)

    def one_pair(index, carry):
        context, log_total = carry
        query_block = head_blocks(query, index, seq_count)
        scores = scored(query_block, head_blocks(keys, index, seq_count), extra, visible, index)
        peak = jnp.max(scores, axis=-1, keepdims=True)
        raised = jnp.exp(scores - peak)
        total = jnp.sum(raised, axis=-1, keepdims=True)
        attend = (raised / total).astype(jnp.bfloat16)
        mixed = jnp.einsum(
            "shqk,skhd->sqhd",
            attend,
            head_blocks(values, index, seq_count),
            preferred_element_type=jnp.float32,
        )
        context = lax.dynamic_update_slice_in_dim(
            context, flat_block(mixed.astype(jnp.bfloat16)), index * 2 * DH, 1
        )
        log_total = lax.dynamic_update_slice_in_dim(
            log_total, (peak + jnp.log(total))[..., 0], index * 2, 1
        )
        return (context, log_total)

    return lax.fori_loop(0, pairs, one_pair, (start_context, start_totals))


def attend_backward(query, keys, values, extra, visible, seq_count, log_total, grad_context):
    pairs = query.shape[1] // (2 * DH)
    scale = DH ** (-0.5)
    extra_shape = extra.shape if extra is not None else (1,)
    start_grads = (
        jnp.zeros(query.shape, jnp.bfloat16),
        jnp.zeros(keys.shape, jnp.bfloat16),
        jnp.zeros(values.shape, jnp.bfloat16),
        jnp.zeros(extra_shape, jnp.float32),
    )

    def one_pair(index, carry):
        grad_query, grad_keys, grad_values, grad_extra = carry
        query_block = head_blocks(query, index, seq_count)
        keys_block = head_blocks(keys, index, seq_count)
        value_block = head_blocks(values, index, seq_count)
        upstream = head_blocks(grad_context, index, seq_count)
        scores = scored(query_block, keys_block, extra, visible, index)
        attend = jnp.exp(scores - lax.dynamic_slice_in_dim(log_total, index * 2, 2, 1)[..., None])
        grad_attend = jnp.einsum(
            "sqhd,skhd->shqk", upstream, value_block, preferred_element_type=jnp.float32
        )
        value_grad = jnp.einsum(
            "shqk,sqhd->skhd",
            attend.astype(jnp.bfloat16),
            upstream,
            preferred_element_type=jnp.float32,
        ).astype(jnp.bfloat16)
        inner = jnp.sum(attend * grad_attend, axis=-1, keepdims=True)
        grad_score = attend * (grad_attend - inner)
        rounded = grad_score.astype(jnp.bfloat16)
        query_grad = (
            jnp.einsum("shqk,skhd->sqhd", rounded, keys_block, preferred_element_type=jnp.float32)
            * scale
        ).astype(jnp.bfloat16)
        keys_grad = (
            jnp.einsum("shqk,sqhd->skhd", rounded, query_block, preferred_element_type=jnp.float32)
            * scale
        ).astype(jnp.bfloat16)
        offset = index * 2 * DH
        grad_query = lax.dynamic_update_slice_in_dim(grad_query, flat_block(query_grad), offset, 1)
        grad_keys = lax.dynamic_update_slice_in_dim(grad_keys, flat_block(keys_grad), offset, 1)
        grad_values = lax.dynamic_update_slice_in_dim(
            grad_values, flat_block(value_grad), offset, 1
        )
        if extra is not None:
            grad_extra = lax.dynamic_update_slice_in_dim(
                grad_extra, jnp.sum(grad_score, axis=0), index * 2, 0
            )
        return (grad_query, grad_keys, grad_values, grad_extra)

    return lax.fori_loop(0, pairs, one_pair, start_grads)


MESH = pl.DeviceIdType.MESH
HALF = 384
ROWS = 256
LOW, FULL = jnp.bfloat16, jnp.float32
EVERY = slice(None)


def place():
    wide = lax.axis_index(AXES[0])
    narrow = lax.axis_index(AXES[1])
    return wide // 2, lax.rem(wide, 2), narrow // 2, lax.rem(narrow, 2)


def device(z, x, y, c):
    return (z * 2 + x, y * 2 + c)


def partners(z, x, y, c):
    return (
        device(z ^ 1, x, y, c),
        device(z ^ 2, x, y, c),
        device(z ^ 3, x, y, c),
        device(z, 1 - x, y, c),
        device(z, x, 1 - y, c),
        device(z, x, y, 1 - c),
    )


def enter(everyone):
    barrier = pltpu.get_barrier_semaphore()
    for other in everyone:
        pl.semaphore_signal(barrier, inc=1, device_id=other, device_id_type=MESH)
    pl.semaphore_wait(barrier, len(everyone))


class Post:
    def __init__(self, send, recv, near):
        self.send, self.recv, self.near = send, recv, near
        self.used, self.used_near, self.started, self.open = 0, 0, [], []

    def copy(self, source, target, where):
        made = pltpu.make_async_remote_copy(
            src_ref=source,
            dst_ref=target,
            send_sem=self.send.at[self.used],
            recv_sem=self.recv.at[self.used],
            device_id=where,
            device_id_type=MESH,
        )
        self.used += 1
        made.start()
        self.started.append(made)
        return made

    def local(self, source, target, keep=False):
        made = pltpu.make_async_copy(source, target, self.near.at[self.used_near])
        self.used_near += 1
        made.start()
        if not keep:
            self.open.append(made)
        return made

    def finish(self):
        for made in self.started:
            made.wait_send()
        for made in self.open:
            made.wait()


def arrived(copies):
    for made in copies:
        made.wait_recv()


def dot(left, right):
    return jnp.dot(left, right, preferred_element_type=FULL)


def dot_last(left, right):
    return lax.dot_general(left, right, (((1,), (1,)), ((), ())), preferred_element_type=FULL)


def dot_first(left, right):
    return lax.dot_general(left, right, (((0,), (0,)), ((), ())), preferred_element_type=FULL)


def square(ref, index):
    return ref[index].reshape(768, 768)


def bucket_rows():
    distance = lax.broadcasted_iota(jnp.int32, (NB, ROWS), 1)
    row = lax.broadcasted_iota(jnp.int32, (NB, ROWS), 0)
    exact_part = NB // 2
    bucket = jnp.minimum(distance, exact_part)
    for step in range(1, NB - exact_part):
        bound = math.ceil(exact_part * (MAXDIST / exact_part) ** (step / (NB - exact_part)))
        bucket = bucket + (distance >= bound).astype(jnp.int32)
    return (bucket == row).astype(LOW)


def self_mask(length):
    key = lax.broadcasted_iota(jnp.int32, (ROWS, ROWS), 0)
    query = lax.broadcasted_iota(jnp.int32, (ROWS, ROWS), 1)
    return jnp.where((key <= query) & (key < length), 0.0, NEGATIVE)


def memory_mask(length, rows):
    key = lax.broadcasted_iota(jnp.int32, (rows, 1), 0)
    return jnp.where(key < length, 0.0, NEGATIVE)


def slanted(row):
    return pltpu.roll(jnp.broadcast_to(row, (ROWS, ROWS)), 0, 1, stride=1, stride_axis=0)


def one_head(block, head):
    lane = lax.broadcasted_iota(jnp.int32, block.shape, 1)
    return jnp.where((lane < DH) if head == 0 else (lane >= DH), block, jnp.zeros_like(block))


def inverse_rms(field):
    return lax.rsqrt(jnp.mean(field * field, axis=-1, keepdims=True) + EPSILON)


PAIRS = [("gains", 0, 1), (2, 3), (4, 7), (5, 6), (8, 9), (10, 11), ((0, 0), (0, 1))]
LATE = ((1, 0), (1, 1))
ORDERS = {"gains": "zxy", (0, 0): "zxy", (0, 1): "zyx", (1, 0): "xyz", (1, 1): "yxz"}
for _pair in PAIRS[:-1]:
    for _unit, _order in zip(_pair[-2:], ("zxy", "zyx")):
        ORDERS[_unit] = _order


def forward_schedule(ahead=5):
    events = [(unit, 0) for unit in PAIRS[0]] + [(unit, 0) for unit in LATE]
    for pair in PAIRS[1:ahead]:
        events += [(unit, 0) for unit in pair]
    count = len(PAIRS)
    for step in range(count + 4):
        for stage in (1, 0, None, 2, 3, 4):
            if stage is None:
                if step in (0, 2):
                    events += [(unit, 1 + step // 2) for unit in LATE]
                continue
            index = step + ahead if stage == 0 else step - stage + 1
            if (stage > 0 or index >= ahead) and 0 <= index < count:
                events += [(unit, stage) for unit in PAIRS[index]]
    return events + [(unit, stage) for stage in (3, 4) for unit in LATE]


class Gather:
    def __init__(self, post, mats, down, gains, kept, spot, everyone):
        self.post, self.mats, self.down, self.gains, self.kept = post, mats, down, gains, kept
        self.spot, self.everyone = spot, everyone
        self.events = forward_schedule()
        self.waits, self.near, self.ready = {}, {}, set()

    def at(self, unit, *where):
        if unit == "gains":
            return self.gains.at[where]
        if isinstance(unit, tuple):
            return self.down.at[where + (pl.ds(unit[0] * 48, 48), pl.ds(unit[1] * HALF, HALF))]
        return self.mats.at[(unit,) + where]

    def forward(self, unit, where, targets):
        return [self.post.copy(self.at(unit, *where), self.at(unit, *where), target) for target in targets]

    def run(self, unit, stage):
        z, x, y, c = self.spot
        across, along, sibling = self.everyone[3:]
        order = ORDERS[unit]
        if stage == 0:
            targets = {"z": self.everyone[:3], "x": (across,), "y": (along,)}[order[0]]
            self.near[unit] = []
            self.waits[unit] = self.forward(unit, self.spot, targets)
            return
        if stage == 4:
            arrived(self.near[unit])
            self.ready.add(unit)
            if isinstance(unit, int):
                self.post.local(self.mats.at[unit], self.kept[0].at[unit])
            if unit in ((0, 1), (1, 1)):
                rows = (EVERY,) * 4 + (pl.ds(unit[0] * 48, 48),)
                self.post.local(self.down.at[rows], self.kept[1].at[rows])
            return
        arrived(self.waits[unit])
        steps = {
            "zxy": (
                ((EVERY, x, y, c), (across,), (EVERY, x, y, c)),
                ((EVERY, EVERY, y, c), (along,), (EVERY, 1 - x, y, c)),
                (None, (), (EVERY, EVERY, 1 - y, c)),
            ),
            "zyx": (
                ((EVERY, x, y, c), (along,), (EVERY, x, y, c)),
                ((EVERY, x, EVERY, c), (across,), (EVERY, x, 1 - y, c)),
                (None, (), (EVERY, 1 - x, EVERY, c)),
            ),
            "xyz": (
                ((z, EVERY, y, c), (along,), None),
                ((z, EVERY, EVERY, c), self.everyone[:3], (z, EVERY, EVERY, c)),
                (None, (), "others"),
            ),
            "yxz": (
                ((z, x, EVERY, c), (across,), None),
                ((z, EVERY, EVERY, c), self.everyone[:3], (z, EVERY, EVERY, c)),
                (None, (), "others"),
            ),
        }
        where, targets, near = steps[order][stage - 1]
        self.waits[unit] = self.forward(unit, where, targets) if targets else []
        if near == "others":
            for k in range(3):
                self.near[unit] += self.forward(unit, (z ^ (k + 1), EVERY, EVERY, c), (sibling,))
        elif near is not None:
            self.near[unit] += self.forward(unit, near, (sibling,))

    def pump(self, count):
        for _ in range(count):
            if self.events:
                self.run(*self.events.pop(0))

    def require(self, *units):
        for unit in units:
            while unit not in self.ready:
                self.pump(1)


def forward_kernel(*refs):
    shards, (tokens, memory, cotangent, table, lengths, memory_lengths) = refs[:11], refs[11:17]
    kept_mats, kept_down, gain_rows = refs[17:20]
    (turned, memory_turned, small, keys_out, values_out, self_out, cross_out, hidden_out, slope_out, grads_out) = refs[20:30]
    self_log, cross_log = refs[30:32]
    (gains, mats, down, keep, keys, values, stage, memory_stage, hidden, slope) = refs[32:42]
    (hidden_turned, after_self, after_cross, own_cut, other_cut, grads, near, send, recv) = refs[42:]
    spot = place()
    everyone = partners(*spot)
    sibling = everyone[5]
    post = Post(send, recv, near)
    comm = Gather(post, mats, down, gains, (kept_mats, kept_down), spot, everyone)
    for index in range(8):
        mats.at[(index,) + spot][...] = shards[index][...]
    for index in range(4):
        mats.at[(8 + index,) + spot][...] = shards[8][:, index * 768 : (index + 1) * 768]
    down.at[spot][...] = shards[9][...]
    gains.at[spot][...] = shards[10][...]
    enter(everyone)
    comm.pump(9)
    from_sibling = []

    def turn(block, staged, target, lanes=ROWS):
        staged[...] = block.T
        post.local(staged, target.at[:, pl.ds(0, lanes)])
        from_sibling.append(post.copy(staged, target.at[:, pl.ds(lanes, lanes)], sibling))

    for block in range(4):
        turn(memory[block * ROWS : (block + 1) * ROWS], memory_stage.at[block], memory_turned.at[block])
        comm.pump(1)
    live = lax.broadcasted_iota(jnp.int32, (ROWS, 1), 0) < lengths[0]
    grad_low = jnp.where(live, cotangent[...], jnp.zeros_like(cotangent[...]))
    left, right = grad_low[:, :HALF], grad_low[:, HALF:]
    core = spot[3]
    own_cut[0] = jnp.where(core == 0, left, right)
    other_cut[...] = jnp.where(core == 0, right, left)
    from_sibling.append(post.copy(other_cut, own_cut.at[1], sibling))
    source = tokens[...].astype(FULL)
    inverse = inverse_rms(source)
    one_hot = bucket_rows()
    bias = dot(table[...], one_hot)
    visible = self_mask(lengths[0])
    comm.require("gains")
    gain_rows[...] = jnp.sum(gains[...].astype(FULL).reshape(32, 8, 768), axis=0)
    normed = (source * inverse * gain_rows[0:1]).astype(LOW)
    turn(normed, stage.at[0], turned.at[0])

    def project(unit, slot, block):
        comm.require(unit)
        keep[slot] = dot(block, square(mats, unit)).astype(LOW)
        post.local(keep.at[slot], small.at[slot])

    project(0, 0, normed)
    project(1, 1, normed)
    project(2, 2, normed)

    def attend(pair, head, query, key_block, value_block, extra, log_ref):
        scores = dot_last(key_block, one_head(query, head)) + extra
        peak = jnp.max(scores, axis=0, keepdims=True)
        raised = jnp.exp(scores - peak)
        total = jnp.sum(raised, axis=0, keepdims=True)
        mixed = dot_first(value_block, raised.astype(LOW)) / total
        log_ref[pair * 2 + head : pair * 2 + head + 1] = peak + jnp.log(total)
        return mixed[head * DH : head * DH + DH]

    for pair in range(6):
        span = slice(pair * 128, pair * 128 + 128)
        query = keep[0, :, span] * 0.125
        mixed = [
            attend(
                pair,
                head,
                query,
                keep[1, :, span],
                keep[2, :, span],
                slanted(bias[pair * 2 + head : pair * 2 + head + 1]) + visible,
                self_log,
            )
            for head in range(2)
        ]
        keep[3, :, span] = jnp.concatenate(mixed, axis=0).T.astype(LOW)
        comm.pump(1)
    post.local(keep.at[3], small.at[3])
    context = keep[3]
    turn(context, stage.at[1], turned.at[1])
    comm.require(3)
    after_self[...] = source + dot(context, square(mats, 3))
    post.local(after_self, self_out)
    normed = (after_self[...] * inverse_rms(after_self[...]) * gain_rows[1:2]).astype(LOW)
    turn(normed, stage.at[2], turned.at[2])
    project(4, 4, normed)
    for unit, held, out in ((5, keys, keys_out), (6, values, values_out)):
        comm.require(unit)
        for block in range(4):
            held[block] = dot(memory[block * ROWS : (block + 1) * ROWS], square(mats, unit)).astype(LOW)
        post.local(held, out)
    shown = memory_mask(memory_lengths[0], 1024)
    for pair in range(6):
        span = slice(pair * 128, pair * 128 + 128)
        query = keep[4, :, span] * 0.125
        mixed = [
            attend(pair, head, query, keys[:, :, span].reshape(1024, 128), values[:, :, span].reshape(1024, 128), shown, cross_log) for head in range(2)
        ]
        keep[5, :, span] = jnp.concatenate(mixed, axis=0).T.astype(LOW)
        comm.pump(1)
    post.local(keep.at[5], small.at[5])
    context = keep[5]
    turn(context, stage.at[3], turned.at[3])
    comm.require(7)
    after_cross[...] = after_self[...] + dot(context, square(mats, 7))
    post.local(after_cross, cross_out)
    normed = (after_cross[...] * inverse_rms(after_cross[...]) * gain_rows[2:3]).astype(LOW)
    turn(normed, stage.at[4], turned.at[4])
    root = math.sqrt(2.0 / math.pi)
    for block in range(4):
        comm.require(8 + block)
        before = dot(normed, square(mats, 8 + block))
        squared = before * before
        bent = jnp.tanh(root * before * (1.0 + 0.044715 * squared))
        lifted = 0.5 * (1.0 + bent)
        value = (before * lifted).astype(LOW)
        hidden[block] = value
        slope[block] = (
            lifted + 0.5 * root * before * (1.0 - bent * bent) * (1.0 + 3 * 0.044715 * squared)
        ).astype(LOW)
        post.local(hidden.at[block], hidden_out.at[block])
        post.local(slope.at[block], slope_out.at[block])
        hidden_turned[block, :, :ROWS] = value.T
        half = hidden_turned.at[block, :, pl.ds(0, ROWS)]
        from_sibling.append(post.copy(half, hidden_turned.at[block, :, pl.ds(ROWS, ROWS)], sibling))
        comm.pump(1)
    arrived(from_sibling)
    for block in range(4):
        comm.pump(1)
        grads[block] = dot(hidden_turned[block], own_cut[...].reshape(512, HALF)).astype(LOW).reshape(2, 2, 2, 96, HALF)
        post.local(grads.at[block], grads_out.at[block])
    while comm.events:
        comm.pump(1)
    post.finish()


def forward_call(shards, *rest):
    kind = jax.ShapeDtypeStruct
    anywhere, vmem = pl.BlockSpec(memory_space=pl.ANY), pl.BlockSpec(memory_space=pltpu.VMEM)
    smem = pl.BlockSpec(memory_space=pltpu.SMEM)
    outs = (
        (kind((12, 4, 2, 2, 2, 24, 768), LOW), anywhere),
        (kind((4, 2, 2, 2, 96, 768), LOW), anywhere),
        (kind((8, 768), FULL), vmem),
        (kind((5, 768, 512), LOW), anywhere),
        (kind((4, 768, 512), LOW), anywhere),
        (kind((6, 256, 768), LOW), anywhere),
        (kind((4, 256, 768), LOW), anywhere),
        (kind((4, 256, 768), LOW), anywhere),
        (kind((256, 768), FULL), anywhere),
        (kind((256, 768), FULL), anywhere),
        (kind((4, 256, 768), LOW), anywhere),
        (kind((4, 256, 768), LOW), anywhere),
        (kind((4, 2, 2, 2, 96, HALF), LOW), anywhere),
        (kind((16, 256), FULL), vmem),
        (kind((16, 256), FULL), vmem),
    )
    return pl.pallas_call(
        forward_kernel,
        out_shape=tuple(out[0] for out in outs),
        in_specs=[vmem] * 15 + [smem] * 2,
        out_specs=tuple(out[1] for out in outs),
        scratch_shapes=[
            pltpu.VMEM((4, 2, 2, 2, 8, 768), LOW),
            pltpu.VMEM((12, 4, 2, 2, 2, 24, 768), LOW),
            pltpu.VMEM((4, 2, 2, 2, 96, 768), LOW),
            pltpu.VMEM((6, 256, 768), LOW),
            pltpu.VMEM((4, 256, 768), LOW),
            pltpu.VMEM((4, 256, 768), LOW),
            pltpu.VMEM((5, 768, 256), LOW),
            pltpu.VMEM((4, 768, 256), LOW),
            pltpu.VMEM((4, 256, 768), LOW),
            pltpu.VMEM((4, 256, 768), LOW),
            pltpu.VMEM((4, 768, 512), LOW),
            pltpu.VMEM((256, 768), FULL),
            pltpu.VMEM((256, 768), FULL),
            pltpu.VMEM((2, 256, HALF), LOW),
            pltpu.VMEM((256, HALF), LOW),
            pltpu.VMEM((4, 2, 2, 2, 96, HALF), LOW),
            pltpu.SemaphoreType.DMA((80,)),
            pltpu.SemaphoreType.DMA((180,)),
            pltpu.SemaphoreType.DMA((180,)),
        ],
        compiler_params=pltpu.CompilerParams(
            collective_id=0, has_side_effects=True, vmem_limit_bytes=60 * 2**20
        ),
    )(*shards, *rest)


Z_FIRST = (8, 9)


class Scatter:
    def __init__(self, post, grads, inboxes, done, sums, outs, spot, everyone):
        self.post, self.grads, self.inboxes, self.done, self.sums, self.outs = post, grads, inboxes, done, sums, outs
        self.spot, self.everyone = spot, everyone
        self.queue, self.waits, self.flipped, self.count = [], {(0, "sum"): []}, {}, 0

    def at(self, kind, unit, *where):
        mats, down = kind
        if isinstance(unit, int):
            return mats.at[(unit,) + where]
        where += (EVERY,) * (len(down.shape) - 2 - len(where))
        return down.at[where + (pl.ds(0 if unit == "down0" else 48, 48),)]

    def grad(self, unit, *where):
        return self.at(self.grads, unit, *where)

    def box(self, number, unit, *where):
        return self.at(self.inboxes[number], unit, *where)

    def begin(self, unit):
        z, x, y, c = self.spot
        self.flipped[unit] = self.count % 2 == 1
        self.count += 1
        if unit in Z_FIRST:
            first = Z_FIRST.index(unit)
            self.send(
                unit, 0, [(self.grad(unit, z ^ (k + 1)), self.inboxes[3].at[first, k], self.everyone[k]) for k in range(3)]
            )
        elif self.flipped[unit]:
            self.send(unit, 0, [(self.grad(unit, EVERY, 1 - x, EVERY, EVERY), self.box(0, unit), self.everyone[3])])
        else:
            self.send(unit, 0, [(self.grad(unit, EVERY, EVERY, 1 - y, EVERY), self.box(0, unit), self.everyone[4])])

    def send(self, unit, stage, copies):
        self.waits[unit] = [self.post.copy(*copy) for copy in copies]
        self.queue.append((unit, stage + 1))

    def add(self, target, *terms):
        total = target[...].astype(FULL)
        for term in terms:
            total = total + term[...].astype(FULL)
        target[...] = total.astype(LOW)

    def run(self, unit, stage):
        z, x, y, c = self.spot
        across, along, sibling = self.everyone[3:]
        flipped, early = self.flipped[unit], unit in Z_FIRST
        arrived(self.waits[unit])
        if stage == 1 and early:
            box = self.inboxes[3].at[Z_FIRST.index(unit)]
            self.add(self.grad(unit, z), *(box.at[k] for k in range(3)))
            if flipped:
                source, target = (z, 1 - x, EVERY, EVERY), across
            else:
                source, target = (z, EVERY, 1 - y, EVERY), along
            self.send(unit, 1, [(self.grad(unit, *source), self.box(0, unit, 0), target)])
        if stage == 2 and early:
            if flipped:
                self.add(self.grad(unit, z, x), self.box(0, unit, 0))
                source, target = (z, x, 1 - y, EVERY), along
            else:
                self.add(self.grad(unit, z, EVERY, y), self.box(0, unit, 0))
                source, target = (z, 1 - x, y, EVERY), across
            self.send(unit, 2, [(self.grad(unit, *source), self.box(1, unit, 0), target)])
        if stage == 1 and not early:
            if flipped:
                self.add(self.grad(unit, EVERY, x, EVERY, EVERY), self.box(0, unit))
                source, target = (EVERY, x, 1 - y, EVERY), along
            else:
                self.add(self.grad(unit, EVERY, EVERY, y, EVERY), self.box(0, unit))
                source, target = (EVERY, 1 - x, y, EVERY), across
            self.send(unit, 1, [(self.grad(unit, *source), self.box(1, unit), target)])
        if stage == 2 and not early:
            self.add(self.grad(unit, EVERY, x, y, EVERY), self.box(1, unit))
            self.send(
                unit,
                2,
                [(self.grad(unit, z ^ (k + 1), x, y, EVERY), self.box(2, unit, k), self.everyone[k]) for k in range(3)],
            )
        if stage == 3:
            total = []
            for core in (c, 1 - c):
                part = self.grad(unit, z, x, y, core)[...].astype(FULL)
                for k in range(1 if early else 3):
                    part = part + (self.box(1, unit, 0, core) if early else self.box(2, unit, k, core))[...].astype(FULL)
                total.append(part)
            mine = pl.ds(pl.multiple_of(c * HALF, 128), HALF)
            if isinstance(unit, int):
                target = self.outs[0].at[unit, :, mine]
            else:
                target = self.outs[1].at[pl.ds(0 if unit == "down0" else 48, 48), mine]
            target[...] = total[0]
            self.at(self.done, unit)[...] = total[1]
            self.send(unit, 3, [(self.at(self.done, unit), target, sibling)])

    def small_sum(self, hop):
        sums, boxes = self.sums
        hops = ((self.everyone[4],), (self.everyone[3],), self.everyone[:3], (self.everyone[5],))
        arrived(self.waits[0, "sum"])
        if hop in (1, 2, 4):
            sums[hop] = sums[hop - 1] + boxes[(0, 0, 1, 0, 5)[hop]]
        if hop == 3:
            sums[hop] = (sums[hop - 1] + boxes[2]) + (boxes[3] + boxes[4])
        if hop < 4:
            first = (0, 1, 2, 5)[hop]
            self.waits[0, "sum"] = [
                self.post.copy(sums.at[hop], boxes.at[first + k], target) for k, target in enumerate(hops[hop])
            ]
            self.queue.append(("sum", hop + 1))

    def pump(self, count):
        for _ in range(count):
            if self.queue:
                unit, stage = self.queue.pop(0)
                if unit == "sum":
                    self.small_sum(stage)
                else:
                    self.run(unit, stage)


def rms_back(upstream, field, gain):
    inverse = inverse_rms(field)
    scaled = gain * upstream
    shift = inverse * inverse * inverse * jnp.mean(scaled * field, axis=-1, keepdims=True)
    return inverse * scaled - field * shift, jnp.sum(upstream * field * inverse, axis=0, keepdims=True)


def split_dot(dotted, left, right):
    high = left.astype(LOW)
    return dotted(right, high) + dotted(right, (left - high.astype(FULL)).astype(LOW))


def backward_kernel(*refs):
    (mats, down, turned, memory_turned, grads_in) = refs[:5]
    (keys_in, values_in, hidden_in, slope_in, after_self, after_cross) = refs[5:11]
    (small_in, gains, tokens, cotangent, table, self_log, cross_log) = refs[11:18]
    lengths, memory_lengths = refs[18:20]
    (output, input_grad, memory_grad, mats_out, down_out, extra_out) = refs[20:26]
    (pool_a, pool_b, big, turned_box, wide_a, wide_b, rows_out) = refs[26:33]
    (own_cut, other_cut, own_long, other_long, rows_d, rows_bias, rows_distance) = refs[33:40]
    (grads, grads_down, box_one, box_one_down, box_two, box_two_down, box_three, box_three_down, box_early) = refs[40:49]
    (done, done_down, field, extra, extra_box, stage, small, near, send, recv) = refs[49:]
    spot = z, x, y, c = place()
    everyone = partners(*spot)
    sibling = everyone[5]
    post = Post(send, recv, near)
    comm = Scatter(
        post,
        (grads, grads_down),
        ((box_one, box_one_down), (box_two, box_two_down), (box_three, box_three_down), box_early),
        (done, done_down),
        (extra, extra_box),
        (mats_out, down_out),
        spot,
        everyone,
    )

    def fetch(source, target):
        return post.local(source, target, keep=True)

    def weight(ref, index):
        return ref[index * 32 : index * 32 + 32].reshape(768, 768)

    def fetch_weight(index, pool, slot):
        return fetch(mats.at[pl.ds(index * 32, 32)], pool.at[pl.ds(slot * 32, 32)])

    loads = {
        "grads": fetch(grads_in, grads_down),
        "down": fetch(down, pool_a),
        "slope": fetch(slope_in, wide_b),
        "turned4": fetch(turned.at[4], turned_box.at[0]),
    }

    def need(*names):
        for name in names:
            loads.pop(name).wait()

    def halves(value):
        left, right = value[:, :HALF], value[:, HALF:]
        return jnp.where(c == 0, left, right), jnp.where(c == 0, right, left)

    def whole(mine, other):
        return jnp.concatenate([jnp.where(c == 0, mine, other), jnp.where(c == 0, other, mine)], axis=1)

    hand = {}

    def share(slot, value):
        mine, other = halves(value)
        own_cut[slot, 0] = mine
        other_cut[slot] = other
        hand[slot] = post.copy(other_cut.at[slot], own_cut.at[slot, 1], sibling)

    def shared(slot):
        hand.pop(slot).wait_recv()
        return own_cut[slot].reshape(512, HALF)

    def both(slot):
        return whole(own_cut[slot, 0], other_cut[slot])

    def sum_rows(slot, left, right):
        grads[slot] = dot(left, right).astype(LOW).reshape(4, 2, 2, 2, 24, HALF)

    live = lax.broadcasted_iota(jnp.int32, (ROWS, 1), 0) < lengths[0]
    grad_out = jnp.where(live, cotangent[...].astype(FULL), 0.0)
    grad_low = grad_out.astype(LOW)
    enter(everyone)
    need("grads")
    comm.begin("down0")
    comm.begin("down1")
    need("down", "slope")
    loads["in"] = fetch(mats.at[pl.ds(256, 128)], pool_b)
    loads["hidden"] = fetch(hidden_in, wide_a)
    loads["after_cross"] = fetch(after_cross, field)
    for block in range(4):
        grad_hidden = dot_last(grad_low, weight(pool_a, block))
        share(1 + block, (grad_hidden * wide_b[block].astype(FULL)).astype(LOW))
    loads["turned3"] = fetch(turned.at[3], turned_box.at[1])
    loads["values"] = fetch(values_in, wide_b)
    need("turned4")
    for block in range(4):
        sum_rows(8 + block, turned_box[0], shared(1 + block))
        comm.begin(8 + block)
    loads["turned1"] = fetch(turned.at[1], turned_box.at[0])
    need("hidden", "after_cross", "in")
    total = field[...]
    for block in range(4):
        total = total + dot(wide_a[block], weight(pool_a, block))
    output[...] = total.astype(LOW)
    comm.pump(1)
    loads["keys"] = fetch(keys_in, wide_a)
    for slot, index in enumerate((7, 4, 5, 6)):
        loads[index] = fetch_weight(index, pool_a, slot)
    loads["small"] = fetch(small_in, small)
    loads["turned2"] = fetch(turned.at[2], turned_box.at[2])
    loads["memory_turned"] = fetch(memory_turned, big)
    upstream = 0.0
    for block in range(4):
        upstream = upstream + dot_last(both(1 + block), weight(pool_b, block))
    for slot, index in enumerate((3, 0, 1, 2)):
        loads[index] = fetch_weight(index, pool_b, slot)
    step, gain_three = rms_back(upstream, field[...], gains[2:3])
    extra[0] = jnp.zeros((8, 768), FULL)
    extra[0, 2:3] = gain_three
    input_grad[...] = grad_out + step
    grad_low = input_grad[...].astype(LOW)
    share(5, grad_low)
    loads["after_self"] = fetch(after_self, field)
    need(7)
    upstream = dot_last(grad_low, weight(pool_a, 0)).astype(LOW)
    need("turned3")
    sum_rows(7, turned_box[1], shared(5))
    comm.begin(7)
    loads["turned0"] = fetch(turned.at[0], turned_box.at[1])

    heads = (
        lax.broadcasted_iota(jnp.int32, (16, 768), 1) // DH == lax.broadcasted_iota(jnp.int32, (16, 768), 0)
    ).astype(LOW)

    def inner_rows(context):
        rows_d[...] = split_dot(dot_last, upstream_ref[...].astype(FULL) * context.astype(FULL), heads)

    upstream_ref = stage
    upstream_ref[...] = upstream
    need("small")
    inner_rows(small[5])

    def attend_back(pair, query_block, key_block, value_block, log_ref, extra_of, visit):
        span = pl.ds(pl.multiple_of(pair * 128, 128), 128)
        query, handed = query_block(span) * 0.125, upstream_ref[:, span]
        grad_values, grad_keys, grad_query = 0.0, 0.0, []
        key_block, value_block = key_block(span), value_block(span)
        for head in range(2):
            row = pl.ds(pair * 2 + head, 1)
            query_part, handed_part = one_head(query, head), one_head(handed, head)
            attended = jnp.exp(dot_last(key_block, query_part) + extra_of(row) - log_ref[row])
            grad_scores = attended * (dot_last(value_block, handed_part) - rows_d[row])
            visit(row, grad_scores)
            rounded = grad_scores.astype(LOW)
            grad_values = grad_values + dot(attended.astype(LOW), handed_part)
            grad_keys = grad_keys + dot(rounded, query_part)
            grad_query.append(dot_first(key_block, rounded)[head * DH : head * DH + DH])
        grad_query = jnp.concatenate(grad_query, axis=0).T * 0.125
        return grad_query.astype(LOW), grad_keys.astype(LOW), grad_values.astype(LOW)

    need("keys", "values")
    shown = memory_mask(memory_lengths[0], 1024)
    for turn in range(6):
        mine, lane = turn >= 3, slice(turn % 3 * 128, turn % 3 * 128 + 128)
        pair = (c if mine else 1 - c) * 3 + turn % 3
        grad_query, grad_keys, grad_values = attend_back(
            pair,
            lambda span: small[4, :, span],
            lambda span: wide_a[:, :, span].reshape(1024, 128),
            lambda span: wide_b[:, :, span].reshape(1024, 128),
            cross_log,
            lambda row: shown,
            lambda row, value: None,
        )
        grad_keys, grad_values = grad_keys.reshape(4, ROWS, 128), grad_values.reshape(4, ROWS, 128)
        if mine:
            own_cut[6, 0, :, lane] = grad_query
            own_long[0, :, 0, :, lane] = grad_keys
            own_long[1, :, 0, :, lane] = grad_values
        else:
            other_cut[6, :, lane] = grad_query
            other_long[0, :, :, lane] = grad_keys
            other_long[1, :, :, lane] = grad_values
        if turn == 2:
            hand[6] = post.copy(other_cut.at[6], own_cut.at[6, 1], sibling)
            for kind in range(2):
                hand["long", kind] = post.copy(other_long.at[kind], own_long.at[kind, :, 1], sibling)
        comm.pump(1)
    need(4, 5, 6)
    need("turned2", "after_self")
    upstream = dot_last(both(6), weight(pool_a, 1))
    step, gain_two = rms_back(upstream, field[...], gains[1:2])
    extra[0, 1:2] = gain_two
    input_grad[...] = input_grad[...] + step
    grad_low = input_grad[...].astype(LOW)
    share(7, grad_low)
    comm.pump(1)
    need("memory_turned")
    for kind, unit in ((0, 5), (1, 6)):
        hand.pop(("long", kind)).wait_recv()
        total = 0.0
        for block in range(4):
            total = total + dot(big[block], own_long[kind, block].reshape(512, HALF))
        grads[unit] = total.astype(LOW).reshape(4, 2, 2, 2, 24, HALF)
        comm.begin(unit)
        comm.pump(1)
    sum_rows(4, turned_box[2], shared(6))
    comm.begin(4)
    comm.pump(1)
    need(3, "turned1")
    upstream_ref[...] = dot_last(grad_low, weight(pool_b, 0)).astype(LOW)
    inner_rows(small[3])
    sum_rows(3, turned_box[0], shared(7))
    comm.begin(3)
    one_hot = bucket_rows()
    rows_bias[0:12] = dot(table[...], one_hot)
    visible = self_mask(lengths[0])

    def by_distance(row, value):
        eight = value[:8]
        for first in range(8, ROWS, 8):
            eight = eight + pltpu.roll(value[first : first + 8], ROWS - first, 1)
        total = eight[:1]
        for first in range(1, 8):
            total = total + pltpu.roll(eight, ROWS - first, 1)[first : first + 1]
        rows_distance[row] = total

    rows_distance[...] = jnp.zeros((16, ROWS), FULL)
    for turn in range(6):
        mine, lane = turn >= 3, slice(turn % 3 * 128, turn % 3 * 128 + 128)
        pair = (c if mine else 1 - c) * 3 + turn % 3
        parts = attend_back(
            pair,
            lambda span: small[0, :, span],
            lambda span: small[1, :, span],
            lambda span: small[2, :, span],
            self_log,
            lambda row: slanted(rows_bias[row]) + visible,
            by_distance,
        )
        for slot, part in zip((8, 9, 10), parts):
            if mine:
                own_cut[slot, 0, :, lane] = part
            else:
                other_cut[slot, :, lane] = part
        if turn == 2:
            for slot in (8, 9, 10):
                hand[slot] = post.copy(other_cut.at[slot], own_cut.at[slot, 1], sibling)
        comm.pump(2)
    need("turned0", 0, 1, 2)
    for unit in range(3):
        sum_rows(unit, turned_box[1], shared(8 + unit))
        comm.begin(unit)
        comm.pump(2)
    upstream = 0.0
    for unit in range(3):
        upstream = upstream + dot_last(both(8 + unit), weight(pool_b, 1 + unit))
    step, gain_one = rms_back(upstream, tokens[...].astype(FULL), gains[0:1])
    extra[0, 0:1] = gain_one
    high = rows_distance[...].astype(LOW)
    many = jnp.concatenate([one_hot] * 16, axis=0)
    sums = dot_last(high, many) + dot_last((rows_distance[...] - high.astype(FULL)).astype(LOW), many)
    own_head = lax.broadcasted_iota(jnp.int32, (16, 512), 1) // NB == lax.broadcasted_iota(jnp.int32, (16, 512), 0)
    extra[0, 3:4, :512] = jnp.sum(jnp.where(own_head, sums, 0.0), axis=0, keepdims=True)
    input_grad[...] = input_grad[...] + step
    comm.small_sum(0)
    shown_rows = []
    for block in range(4):
        comm.pump(3)
        if block >= 2:
            shown_rows[block - 2].wait()
        rows_out[block % 2] = dot_last(
            whole(own_long[0, block, 0], other_long[0, block]), weight(pool_a, 2)
        ) + dot_last(whole(own_long[1, block, 0], other_long[1, block]), weight(pool_a, 3))
        shown_rows.append(fetch(rows_out.at[block % 2], memory_grad.at[pl.ds(block * ROWS, ROWS)]))
    while comm.queue:
        comm.pump(1)
    for made in shown_rows[2:]:
        made.wait()
    extra_out[...] = extra[4]
    post.finish()


def backward_call(*args):
    kind = jax.ShapeDtypeStruct
    anywhere, vmem = pl.BlockSpec(memory_space=pl.ANY), pl.BlockSpec(memory_space=pltpu.VMEM)
    smem = pl.BlockSpec(memory_space=pltpu.SMEM)
    vm, dma = pltpu.VMEM, pltpu.SemaphoreType.DMA
    return pl.pallas_call(
        backward_kernel,
        out_shape=(
            kind((256, 768), LOW),
            kind((256, 768), FULL),
            kind((1024, 768), FULL),
            kind((12, 24, 768), FULL),
            kind((96, 768), FULL),
            kind((8, 768), FULL),
        ),
        in_specs=[anywhere] * 12 + [vmem] * 6 + [smem] * 2,
        out_specs=(vmem, vmem, anywhere, vmem, vmem, vmem),
        scratch_shapes=[
            vm((128, 24, 768), LOW),
            vm((128, 24, 768), LOW),
            vm((4, 768, 512), LOW),
            vm((3, 768, 512), LOW),
            vm((4, 256, 768), LOW),
            vm((4, 256, 768), LOW),
            vm((2, 256, 768), FULL),
            vm((11, 2, 256, HALF), LOW),
            vm((11, 256, HALF), LOW),
            vm((2, 4, 2, 256, HALF), LOW),
            vm((2, 4, 256, HALF), LOW),
            vm((16, 256), FULL),
            vm((16, 256), FULL),
            vm((16, 256), FULL),
            vm((12, 4, 2, 2, 2, 24, HALF), LOW),
            vm((4, 2, 2, 2, 96, HALF), LOW),
            vm((12, 4, 2, 2, 24, HALF), LOW),
            vm((4, 2, 2, 96, HALF), LOW),
            vm((12, 4, 2, 24, HALF), LOW),
            vm((4, 2, 96, HALF), LOW),
            vm((12, 3, 2, 24, HALF), LOW),
            vm((3, 2, 96, HALF), LOW),
            vm((len(Z_FIRST), 3, 2, 2, 2, 24, HALF), LOW),
            vm((12, 24, HALF), FULL),
            vm((96, HALF), FULL),
            vm((256, 768), FULL),
            vm((5, 8, 768), FULL),
            vm((6, 8, 768), FULL),
            vm((256, 768), LOW),
            vm((6, 256, 768), LOW),
            dma((60,)),
            dma((150,)),
            dma((150,)),
        ],
        compiler_params=pltpu.CompilerParams(
            collective_id=1, has_side_effects=True, vmem_limit_bytes=60 * 2**20
        ),
    )(*args)


def finish_kernel(*refs):
    (output, input_grad, memory_grad, mats, down, extra), outs = refs[:6], refs[6:]
    for source, target in zip((output, input_grad, memory_grad, down), outs):
        target[...] = source[...]
    for index in range(8):
        outs[4 + index][...] = mats[index]
    for index in range(4):
        outs[12][:, index * 768 : (index + 1) * 768] = mats[8 + index]
    rank = lax.axis_index(AXES[0]) * lax.axis_size(AXES[1]) + lax.axis_index(AXES[1])
    own = pltpu.roll(extra[...], 768 - rank * 24, 1)
    for index in range(3):
        outs[13 + index][...] = own[index : index + 1, :24]
    for head in range(12):
        outs[16][head : head + 1] = extra[3:4, head * NB : head * NB + NB]


def finish(*args):
    kind = jax.ShapeDtypeStruct
    block = lambda *shape: pl.BlockSpec(shape, lambda step: (step, 0))
    whole = lambda *shape: pl.BlockSpec(shape, lambda step: (0,) * len(shape))
    rows = [block(128, 768), block(128, 768), block(512, 768)]
    single = [(96, 768)] + [(24, 768)] * 8 + [(24, 3072)] + [(1, 24)] * 3 + [(12, NB)]
    return pl.pallas_call(
        finish_kernel,
        grid=(2,),
        out_shape=(
            kind((256, 768), LOW),
            kind((256, 768), FULL),
            kind((1024, 768), FULL),
            *[kind(shape, FULL) for shape in single],
        ),
        in_specs=rows + [whole(12, 24, 768), whole(96, 768), whole(8, 768)],
        out_specs=rows + [whole(*shape) for shape in single],
    )(*args)


def plain_body(
    tokens,
    memory,
    cotangent,
    target_lengths,
    memory_lengths,
    self_gain,
    self_query,
    self_key,
    self_value,
    self_out,
    position_table,
    cross_gain,
    cross_query,
    cross_key,
    cross_value,
    cross_out,
    ffn_gain,
    ffn_in,
    ffn_out,
):
    wide_count = lax.axis_size(AXES[0])
    narrow_count = lax.axis_size(AXES[1])
    devices = wide_count * narrow_count
    seq_count = target_lengths.shape[0]
    target_rows = tokens.shape[0] // seq_count
    memory_rows = memory.shape[0] // seq_count
    positions = jnp.arange(target_rows, dtype=jnp.int32)
    live_rows = positions[None, :] < target_lengths[:, None]
    causal = positions[None, :] <= positions[:, None]
    self_visible = causal[None] & live_rows[:, None, :]
    memory_visible = (jnp.arange(memory_rows, dtype=jnp.int32)[None, :] < memory_lengths[:, None])[
        :, None, :
    ]
    grad_out = jnp.where(live_rows.reshape(-1, 1), cotangent.astype(jnp.float32), 0.0)
    bucket = bucket_index(target_rows)
    one_hot = (bucket[:, :, None] == jnp.arange(NB, dtype=jnp.int32)[None, None, :]).astype(
        jnp.float32
    )
    relative = jnp.einsum(
        "ijb,bh->hij", one_hot, position_table.astype(jnp.float32), precision=lax.Precision.HIGHEST
    )
    gain_one, weight_query, weight_key, weight_value, weight_out = (
        lax.all_gather(self_gain, AXES, axis=0, tiled=True),
        lax.all_gather(self_query, AXES, axis=0, tiled=True),
        lax.all_gather(self_key, AXES, axis=0, tiled=True),
        lax.all_gather(self_value, AXES, axis=0, tiled=True),
        lax.all_gather(self_out, AXES, axis=0, tiled=True),
    )
    source = tokens.astype(jnp.float32)
    normed_value, norm_back_one = jax.vjp(rms_apply, source, gain_one.astype(jnp.float32))
    normed_one = normed_value.astype(jnp.bfloat16)
    query_one = product(normed_one, weight_query).astype(jnp.bfloat16)
    keys_one = product(normed_one, weight_key).astype(jnp.bfloat16)
    values_one = product(normed_one, weight_value).astype(jnp.bfloat16)
    context_one, totals_one = attend_forward(
        query_one, keys_one, values_one, relative, self_visible, seq_count
    )
    after_self = source + product(context_one, weight_out)
    gain_two, cross_weight_query, cross_weight_key, cross_weight_value, cross_weight_out = (
        lax.all_gather(cross_gain, AXES, axis=0, tiled=True),
        lax.all_gather(cross_query, AXES, axis=0, tiled=True),
        lax.all_gather(cross_key, AXES, axis=0, tiled=True),
        lax.all_gather(cross_value, AXES, axis=0, tiled=True),
        lax.all_gather(cross_out, AXES, axis=0, tiled=True),
    )
    normed_value, norm_back_two = jax.vjp(rms_apply, after_self, gain_two.astype(jnp.float32))
    normed_two = normed_value.astype(jnp.bfloat16)
    query_two = product(normed_two, cross_weight_query).astype(jnp.bfloat16)
    keys_two = product(memory, cross_weight_key).astype(jnp.bfloat16)
    values_two = product(memory, cross_weight_value).astype(jnp.bfloat16)
    context_two, totals_two = attend_forward(
        query_two, keys_two, values_two, None, memory_visible, seq_count
    )
    after_cross = after_self + product(context_two, cross_weight_out)
    gain_three, weight_in, weight_down = (
        lax.all_gather(ffn_gain, AXES, axis=0, tiled=True),
        lax.all_gather(ffn_in, AXES, axis=0, tiled=True),
        lax.all_gather(ffn_out, AXES, axis=0, tiled=True),
    )
    normed_value, norm_back_three = jax.vjp(rms_apply, after_cross, gain_three.astype(jnp.float32))
    normed_three = normed_value.astype(jnp.bfloat16)
    before = product(normed_three, weight_in)
    gelu_value, gelu_back = jax.vjp(gelu_smooth, before)
    hidden = gelu_value.astype(jnp.bfloat16)
    output = (after_cross + product(hidden, weight_down)).astype(jnp.bfloat16)
    back_in, back_down = (
        lax.all_gather(ffn_in, AXES, axis=0, tiled=True),
        lax.all_gather(ffn_out, AXES, axis=0, tiled=True),
    )
    grad_low = grad_out.astype(jnp.bfloat16)
    grad_down_weight = outer_sum(hidden, grad_low)
    grad_hidden = back_project(grad_low, back_down)
    grad_before = gelu_back(grad_hidden)[0].astype(jnp.bfloat16)
    grad_in_weight = outer_sum(normed_three, grad_before)
    grad_normed_three = back_project(grad_before, back_in)
    grad_cross_part, grad_gain_three = norm_back_three(grad_normed_three)
    grad_cross = grad_out + grad_cross_part
    ffn_terms = (grad_gain_three, grad_in_weight, grad_down_weight)
    summed_ffn = lax.psum_scatter(
        pack_rows(ffn_terms, devices), AXES, scatter_dimension=0, tiled=True
    )
    ffn_gain_grad, ffn_in_grad, ffn_out_grad = unpack_rows(summed_ffn[0], ffn_terms, devices)
    back_cross_query, back_cross_key, back_cross_value, back_cross_out = (
        lax.all_gather(cross_query, AXES, axis=0, tiled=True),
        lax.all_gather(cross_key, AXES, axis=0, tiled=True),
        lax.all_gather(cross_value, AXES, axis=0, tiled=True),
        lax.all_gather(cross_out, AXES, axis=0, tiled=True),
    )
    grad_cross_low = grad_cross.astype(jnp.bfloat16)
    grad_cross_out_weight = outer_sum(context_two, grad_cross_low)
    grad_context_two = back_project(grad_cross_low, back_cross_out).astype(jnp.bfloat16)
    grad_query_two, grad_keys_two, grad_values_two, unused_extra = attend_backward(
        query_two,
        keys_two,
        values_two,
        None,
        memory_visible,
        seq_count,
        totals_two,
        grad_context_two,
    )
    grad_cross_query_weight = outer_sum(normed_two, grad_query_two)
    grad_cross_key_weight = outer_sum(memory, grad_keys_two)
    grad_cross_value_weight = outer_sum(memory, grad_values_two)
    memory_grad = back_project(grad_keys_two, back_cross_key) + back_project(
        grad_values_two, back_cross_value
    )
    grad_self_part, grad_gain_two = norm_back_two(back_project(grad_query_two, back_cross_query))
    grad_self = grad_cross + grad_self_part
    cross_terms = (
        grad_gain_two,
        grad_cross_query_weight,
        grad_cross_key_weight,
        grad_cross_value_weight,
        grad_cross_out_weight,
    )
    summed_cross = lax.psum_scatter(
        pack_rows(cross_terms, devices), AXES, scatter_dimension=0, tiled=True
    )
    cross_gain_grad, cross_query_grad, cross_key_grad, cross_value_grad, cross_out_grad = (
        unpack_rows(summed_cross[0], cross_terms, devices)
    )
    back_query, back_key, back_value, back_out = (
        lax.all_gather(self_query, AXES, axis=0, tiled=True),
        lax.all_gather(self_key, AXES, axis=0, tiled=True),
        lax.all_gather(self_value, AXES, axis=0, tiled=True),
        lax.all_gather(self_out, AXES, axis=0, tiled=True),
    )
    grad_self_low = grad_self.astype(jnp.bfloat16)
    grad_out_weight = outer_sum(context_one, grad_self_low)
    grad_context_one = back_project(grad_self_low, back_out).astype(jnp.bfloat16)
    grad_query_one, grad_keys_one, grad_values_one, grad_relative = attend_backward(
        query_one,
        keys_one,
        values_one,
        relative,
        self_visible,
        seq_count,
        totals_one,
        grad_context_one,
    )
    table_term = jnp.einsum("hij,ijb->bh", grad_relative, one_hot, precision=lax.Precision.HIGHEST)
    position_table_grad = lax.psum(table_term, AXES)
    grad_query_weight = outer_sum(normed_one, grad_query_one)
    grad_key_weight = outer_sum(normed_one, grad_keys_one)
    grad_value_weight = outer_sum(normed_one, grad_values_one)
    grad_normed_one = (
        back_project(grad_query_one, back_query)
        + back_project(grad_keys_one, back_key)
        + back_project(grad_values_one, back_value)
    )
    grad_source_part, grad_gain_one = norm_back_one(grad_normed_one)
    input_grad = grad_self + grad_source_part
    self_terms = (
        grad_gain_one,
        grad_query_weight,
        grad_key_weight,
        grad_value_weight,
        grad_out_weight,
    )
    summed_self = lax.psum_scatter(
        pack_rows(self_terms, devices), AXES, scatter_dimension=0, tiled=True
    )
    self_gain_grad, self_query_grad, self_key_grad, self_value_grad, self_out_grad = unpack_rows(
        summed_self[0], self_terms, devices
    )
    return (
        output,
        input_grad,
        memory_grad,
        self_gain_grad,
        self_query_grad,
        self_key_grad,
        self_value_grad,
        self_out_grad,
        position_table_grad,
        cross_gain_grad,
        cross_query_grad,
        cross_key_grad,
        cross_value_grad,
        cross_out_grad,
        ffn_gain_grad,
        ffn_in_grad,
        ffn_out_grad,
    )


def body(
    tokens,
    memory,
    cotangent,
    target_lengths,
    memory_lengths,
    self_gain,
    self_query,
    self_key,
    self_value,
    self_out,
    position_table,
    cross_gain,
    cross_query,
    cross_key,
    cross_value,
    cross_out,
    ffn_gain,
    ffn_in,
    ffn_out,
):
    rank = lax.axis_index(AXES[0]) * lax.axis_size(AXES[1]) + lax.axis_index(AXES[1])
    own_gains = jnp.stack([self_gain, cross_gain, ffn_gain])
    spread = lax.dynamic_update_slice(jnp.zeros((8, 768), LOW), own_gains, (0, rank * 24))
    shards = (self_query, self_key, self_value, self_out, cross_query, cross_key, cross_value, cross_out, ffn_in, ffn_out)
    (
        mats,
        down,
        gains,
        turned,
        memory_turned,
        small,
        keys,
        values,
        after_self,
        after_cross,
        hidden,
        slope,
        down_grads,
        self_log,
        cross_log,
    ) = forward_call(
        shards + (spread,), tokens, memory, cotangent, position_table.T, target_lengths, memory_lengths
    )
    output, input_grad, memory_grad, mats_grad, down_grad, extra = backward_call(
        mats.reshape(384, 24, 768),
        down.reshape(128, 24, 768),
        turned,
        memory_turned,
        down_grads,
        keys,
        values,
        hidden,
        slope,
        after_self,
        after_cross,
        small,
        gains,
        tokens,
        cotangent,
        position_table.T,
        self_log,
        cross_log,
        target_lengths,
        memory_lengths,
    )
    output, input_grad, memory_grad, down_grad, *square_grads, ffn_in_grad, gain_one, gain_two, gain_three, table = finish(
        output, input_grad, memory_grad, mats_grad, down_grad, extra
    )
    return (
        output,
        input_grad,
        memory_grad,
        gain_one.reshape(24),
        *square_grads[:4],
        table.T,
        gain_two.reshape(24),
        *square_grads[4:],
        gain_three.reshape(24),
        ffn_in_grad,
        down_grad,
    )


def solution(mesh):
    whole = (mesh.shape[AXES[0]], mesh.shape[AXES[1]]) == (8, 4)
    placed = (
        P(AXES, None),
        P(AXES, None),
        P(AXES, None),
        P(AXES),
        P(AXES),
        P(AXES),
        P(AXES, None),
        P(AXES, None),
        P(AXES, None),
        P(AXES, None),
        P(),
        P(AXES),
        P(AXES, None),
        P(AXES, None),
        P(AXES, None),
        P(AXES, None),
        P(AXES),
        P(AXES, None),
        P(AXES, None),
    )
    return jax.shard_map(
        body if whole else plain_body,
        mesh=mesh,
        in_specs=placed,
        out_specs=(
            P(AXES, None),
            P(AXES, None),
            P(AXES, None),
            P(AXES),
            P(AXES, None),
            P(AXES, None),
            P(AXES, None),
            P(AXES, None),
            P(),
            P(AXES),
            P(AXES, None),
            P(AXES, None),
            P(AXES, None),
            P(AXES, None),
            P(AXES),
            P(AXES, None),
            P(AXES, None),
        ),
        check_vma=False,
    )
```
